128 devices in a mesh: dp: 2 (over y_lo), ctx: 8 (over y_hi, z), tp: 8 (over x, core).
Axes of the slice: x: 4, y: 4 (y_hi: 2, y_lo: 2; y = y_hi * 2 + y_lo), z: 4, core: 2. Of those that a mesh axis runs over, the one named last changes fastest.
Arguments:
- hidden: bfloat16 [16384, 8192], P(('dp', 'ctx', 'tp')), parts along dimension 0, may hold values from -6 to 6
- gain: bfloat16 [8192], replicated, may hold values from 0.099609375 to 1.8984375
- basis: bfloat16 [8192, 4096], P(None, 'tp'), may hold values from -0.0625 to 0.0625
- w_query: bfloat16 [4096, 4096], P(None, 'tp'), may hold values from -64 to 64
- key_matrix: bfloat16 [4096, 512], replicated, may hold values from -0.09375 to 0.09375
- value_matrix: bfloat16 [4096, 512], replicated, may hold values from -0.09375 to 0.09375
- doc_ids: int32 [16384], P(('dp', 'ctx', 'tp')), parts along dimension 0, may hold values from 0 to 7, never falling along the last dimension, each value on 1 to 4096 neighbouring positions
Outputs:
- attended: bfloat16 [16384, 4096], P(('dp', 'ctx', 'tp')), parts along dimension 0
The draws below stay inside these ranges and needn't reach their ends.
There are 2 independent parts, one for each index of `dp`. The reference program is written for one: setup_inputs(seed, part) draws one part's arguments, and reference() takes and returns one part's arrays. A program takes and returns all parts, laid end to end along the dimension named above; an argument that names none is the same for every part. Nothing has to cross between parts.
Inputs may be any that keep to these rules, and one draw needn't show every extreme that they name: `doc_ids`: document ids never fall along the sequence; each of the 8 documents has 1 to 4096 tokens, one exactly 4096.
All inputs are finite; a program needn't handle non-finite values.
Results may differ from the reference program's by a relative error of at most 0.02.
The reference program's roundings to bfloat16 on the way count: a program that leaves them out, or rounds other values in their place, can miss the bound.
Values may be sent and summed in bfloat16 or wider, within the bound.
No kernel may reach another device: no remote copies, remote signals or barrier semaphores. Data moves between devices by JAX's collectives and lax.ppermute only.
A program may use at most 192 MiB of HBM per device.

```python
import math
import jax
import jax.numpy as jnp
import numpy as np
from jax import lax

D = 8192
HEAD_WIDTH = 128
PROJECTED_WIDTH = 4096
QUERY_HEADS = 32
KEY_VALUE_HEADS = 4
DOCS = 8
SEQUENCE_TOKENS = 8192


def head_ladder(key, top_scale):
    order = jax.random.permutation(key, QUERY_HEADS).astype(jnp.float32)
    return top_scale ** (order / max(QUERY_HEADS - 1, 1))


def draw_w_query(key, part):
    key = jax.random.fold_in(key, 11)
    scale_key = jax.random.fold_in(key, 1)
    entry_key = jax.random.fold_in(key, 2)
    entries = jnp.clip(jax.random.normal(entry_key, (PROJECTED_WIDTH, QUERY_HEADS, HEAD_WIDTH), jnp.float32), -5.0, 5.0)
    ladder = head_ladder(scale_key, 48.0)
    scaled = entries * ladder[None, :, None] * float(PROJECTED_WIDTH) ** (-0.5)
    return scaled.reshape(PROJECTED_WIDTH, QUERY_HEADS * HEAD_WIDTH).astype(jnp.bfloat16)


def block_levels(key, dims, pieces, smallest, top_value):
    level = 1.0
    for dim, parts in pieces:
        steps = jax.random.uniform(jax.random.fold_in(jax.random.fold_in(key, 6), dim), (parts,), jnp.float32, smallest / len(pieces), top_value / len(pieces))
        level = level * jnp.repeat(jnp.exp(steps), dims[dim] // parts).reshape((-1,) + (1,) * (len(dims) - 1 - dim))
    return level


def split_up(number_of, total, bound, skew):
    weights = [(1 << 20) // math.isqrt(standing ** skew) + 1 for standing in range(2, number_of + 1)]
    surplus, holding = total - bound - (number_of - 1), [1] * (number_of - 1)
    while surplus > 0:
        candidates = [i for i in range(number_of - 1) if holding[i] < bound]
        pool, left = sum([weights[i] for i in candidates]), surplus
        for i in candidates:
            more = min(bound - holding[i], max(1, left * weights[i] // pool), surplus)
            holding[i] = holding[i] + more
            surplus = surplus - more
    return np.array([bound] + holding)


def ragged(rng, amount, total, limit, skew):
    if amount == 2:
        one = jax.random.randint(rng, (), max(1, total - limit), min(limit, total - 1) + 1)
        return jnp.stack([one, total - one])
    sizes = jnp.asarray(split_up(amount, total, limit, skew), jnp.int32)
    twos = (amount - 1) // 2
    giver, taker = sizes[1:1 + 2 * twos:2], sizes[2:2 + 2 * twos:2]
    margin = jnp.minimum(giver - 1, limit - taker)
    shifted = jax.random.randint(jax.random.fold_in(rng, 1), (twos,), 0, 1 << 20) % (margin + 1)
    sizes = sizes.at[1:1 + 2 * twos:2].set(giver - shifted).at[2:2 + 2 * twos:2].set(taker + shifted)
    return sizes[jax.random.permutation(jax.random.fold_in(rng, 2), amount)]


def scatter_about(stream_key, dims, scale, limit, pieces=(), kind=jnp.bfloat16):
    drawn = jax.random.normal(stream_key, dims, jnp.float32) * scale
    if len(pieces) > 0:
        drawn = block_levels(stream_key, dims, pieces, -0.22, 0.18) * drawn
    return jnp.clip(drawn, min=-limit, max=limit).astype(kind)


def setup_inputs(seed: int = 0, part: int = 0) -> dict:
    seeds = jax.random.split(jax.random.key(seed), 8)
    part_keys = jax.random.split(jax.random.fold_in(seeds[7], part), 8)
    hidden = scatter_about(part_keys[0], (SEQUENCE_TOKENS, D), 1.0, 6.0, ((0, 64),))
    gain = jnp.clip(1.0 + 0.18 * jax.random.normal(seeds[1], (D,), jnp.float32), 0.099609375, 1.8984375).astype(jnp.bfloat16)
    basis = scatter_about(seeds[2], (D, PROJECTED_WIDTH), D ** -0.5, 0.0625, ((1, 8),))
    w_query = draw_w_query(jax.random.fold_in(seeds[7], 71), part)
    key_matrix = scatter_about(seeds[4], (PROJECTED_WIDTH, KEY_VALUE_HEADS * HEAD_WIDTH), PROJECTED_WIDTH ** -0.5, 0.09375)
    value_matrix = scatter_about(seeds[5], (PROJECTED_WIDTH, KEY_VALUE_HEADS * HEAD_WIDTH), PROJECTED_WIDTH ** -0.5, 0.09375)
    doc_ids = jnp.searchsorted(jnp.cumsum(ragged(part_keys[6], DOCS, SEQUENCE_TOKENS, SEQUENCE_TOKENS // 2, 2)), jnp.arange(SEQUENCE_TOKENS), side="right").astype(jnp.int32)
    return dict(hidden=hidden, gain=gain, basis=basis, w_query=w_query, key_matrix=key_matrix, value_matrix=value_matrix, doc_ids=doc_ids)


def apply_rotary(values, positions):
    half_width = values.shape[-1] // 2
    frequency = 500000.0 ** (-jnp.arange(half_width, dtype=jnp.float32) * 2.0 / values.shape[-1])
    angles = positions[:, None, None] * frequency
    cosine = jnp.cos(angles)
    sine_part = jnp.sin(angles)
    first_half = values[..., :half_width]
    second_half = values[..., half_width:]
    return jnp.concatenate([first_half * cosine - second_half * sine_part, second_half * cosine + first_half * sine_part], axis=-1)

def reference(hidden, gain, basis, w_query, key_matrix, value_matrix, doc_ids):
    values = hidden.astype(jnp.float32)
    meansq = lax.optimization_barrier(jnp.mean(values * values, axis=-1, keepdims=True))
    normed = (values * lax.rsqrt(meansq + 1e-05) * gain.astype(jnp.float32)).astype(jnp.bfloat16)
    espace_input = jnp.dot(normed, basis, preferred_element_type=jnp.float32).astype(jnp.bfloat16)
    positions = jnp.arange(SEQUENCE_TOKENS, dtype=jnp.int32)
    position_real = positions.astype(jnp.float32)
    queries = apply_rotary(jnp.dot(espace_input, w_query, preferred_element_type=jnp.float32).reshape(SEQUENCE_TOKENS, QUERY_HEADS, HEAD_WIDTH), position_real).astype(jnp.bfloat16)
    shared_key_rows = apply_rotary(jnp.dot(espace_input, key_matrix, preferred_element_type=jnp.float32).reshape(SEQUENCE_TOKENS, KEY_VALUE_HEADS, HEAD_WIDTH), position_real).astype(jnp.bfloat16)
    shared_value_rows = jnp.dot(espace_input, value_matrix, preferred_element_type=jnp.float32).reshape(SEQUENCE_TOKENS, KEY_VALUE_HEADS, HEAD_WIDTH).astype(jnp.bfloat16)
    query_group_count = QUERY_HEADS // KEY_VALUE_HEADS
    keys_wide = jnp.repeat(shared_key_rows, query_group_count, axis=1).astype(jnp.float32)
    values_wide = jnp.repeat(shared_value_rows, query_group_count, axis=1).astype(jnp.float32)
    block_rows = math.gcd(SEQUENCE_TOKENS, 128)
    block_count = SEQUENCE_TOKENS // block_rows

    def one_block(block_items):
        query_block, pos_block, id_block = block_items
        scores = jnp.einsum('bhd,shd->hbs', query_block.astype(jnp.float32), keys_wide) * HEAD_WIDTH ** (-0.5)
        visible = (positions[None, :] <= pos_block[:, None]) & (doc_ids[None, :] == id_block[:, None])
        scores = jnp.where(visible[None], scores, -1e+30)
        row_max = lax.optimization_barrier(jnp.max(scores, axis=-1, keepdims=True))
        weights = jnp.where(visible[None], jnp.exp(scores - row_max), 0.0)
        norm_sum = lax.optimization_barrier(jnp.sum(weights, axis=-1))
        mixed = jnp.einsum('hbs,shd->hbd', weights.astype(jnp.bfloat16).astype(jnp.float32), values_wide) / norm_sum[..., None]
        return mixed.transpose(1, 0, 2).reshape(block_rows, QUERY_HEADS * HEAD_WIDTH).astype(jnp.bfloat16)
    blocks_out = lax.map(one_block, (queries.reshape(block_count, block_rows, QUERY_HEADS, HEAD_WIDTH), positions.reshape(block_count, block_rows), doc_ids.reshape(block_count, block_rows)))
    return blocks_out.reshape(SEQUENCE_TOKENS, QUERY_HEADS * HEAD_WIDTH)
```

```python
import functools
import math

import jax
import jax.numpy as jnp
from jax import lax
from jax.experimental import pallas as pl
from jax.experimental.pallas import tpu as pltpu
from jax.sharding import PartitionSpec as P

HEAD_WIDTH = 128
QUERY_HEADS = 32
KEY_VALUE_HEADS = 4
DOCS = 8
LONGEST_DOC = 4096
QUERY_TILE = 256
KEY_TILE = 512
HIDDEN_SCORE = -1e30
LOWEST_MAX = -0.5e30


def rotary_tables(positions):
    half_width = HEAD_WIDTH // 2
    frequency = 500000.0 ** (-jnp.arange(half_width, dtype=jnp.float32) * 2.0 / HEAD_WIDTH)
    angles = positions[:, None] * frequency
    cosine = jnp.cos(angles)
    sine = jnp.sin(angles)
    return (
        jnp.concatenate([cosine, cosine], axis=-1),
        jnp.concatenate([-sine, sine], axis=-1),
    )


def qkv_kernel(x_ref, w_ref, cos_ref, sin_ref, q_ref, kv_ref):
    cosine, sine = cos_ref[...], sin_ref[...]

    def rotated(u):
        return (u * cosine + pltpu.roll(u, HEAD_WIDTH // 2, 1) * sine).astype(jnp.bfloat16)

    parts, _, depth = x_ref.shape
    pair = 2 * HEAD_WIDTH
    for n in range(w_ref.shape[1] // pair):
        total = None
        for part in range(parts):
            term = jnp.dot(
                x_ref[part],
                w_ref[part * depth : (part + 1) * depth, n * pair : (n + 1) * pair],
                preferred_element_type=jnp.float32,
            )
            total = term if total is None else total + term
        left, right = total[:, :HEAD_WIDTH], total[:, HEAD_WIDTH:]
        if n * pair < q_ref.shape[1]:
            q_ref[:, n * pair : n * pair + HEAD_WIDTH] = rotated(left)
            q_ref[:, n * pair + HEAD_WIDTH : (n + 1) * pair] = rotated(right)
        else:
            kv_ref[:, :HEAD_WIDTH] = rotated(left)
            kv_ref[:, HEAD_WIDTH:] = right.astype(jnp.bfloat16)


def project_heads(x, weights, cosine, sine, query_columns):
    parts, rows, depth = x.shape
    tile = math.gcd(rows, 256)
    wide = weights.shape[1]
    return pl.pallas_call(
        qkv_kernel,
        grid=(rows // tile,),
        in_specs=[
            pl.BlockSpec((parts, tile, depth), lambda i: (0, i, 0)),
            pl.BlockSpec((parts * depth, wide), lambda i: (0, 0)),
            pl.BlockSpec((tile, HEAD_WIDTH), lambda i: (i, 0)),
            pl.BlockSpec((tile, HEAD_WIDTH), lambda i: (i, 0)),
        ],
        out_specs=[
            pl.BlockSpec((tile, query_columns), lambda i: (i, 0)),
            pl.BlockSpec((tile, 2 * HEAD_WIDTH), lambda i: (i, 0)),
        ],
        out_shape=[
            jax.ShapeDtypeStruct((rows, query_columns), jnp.bfloat16),
            jax.ShapeDtypeStruct((rows, 2 * HEAD_WIDTH), jnp.bfloat16),
        ],
        compiler_params=pltpu.CompilerParams(vmem_limit_bytes=48 * 1024 * 1024),
        cost_estimate=pl.CostEstimate(
            flops=2 * rows * parts * depth * wide,
            bytes_accessed=2 * (rows * parts * depth + parts * depth * wide + rows * wide),
            transcendentals=0,
        ),
    )(x, weights, cosine, sine)


def attention_kernel(bounds_ref, q_ref, kv_ref, first_ref, o_ref, max_ref, sum_ref, acc_ref):
    tile = pl.program_id(0)
    rows, columns = q_ref.shape
    heads = columns // HEAD_WIDTH
    row_start = kv_ref.shape[0] - pl.num_programs(0) * rows + tile * rows
    scale = HEAD_WIDTH**-0.5 * math.log2(math.e)
    max_ref[...] = jnp.full(max_ref.shape, LOWEST_MAX, jnp.float32)
    sum_ref[...] = jnp.zeros(sum_ref.shape, jnp.float32)
    acc_ref[...] = jnp.zeros(acc_ref.shape, jnp.float32)

    def visit(key_tile, masked):
        start = pl.multiple_of(key_tile * KEY_TILE, KEY_TILE)
        keys = kv_ref[pl.ds(start, KEY_TILE), :HEAD_WIDTH]
        values = kv_ref[pl.ds(start, KEY_TILE), HEAD_WIDTH:]
        if masked:
            key_pos = start + lax.broadcasted_iota(jnp.int32, (rows, KEY_TILE), 1)
            query_pos = row_start + lax.broadcasted_iota(jnp.int32, (rows, KEY_TILE), 0)
            visible = (key_pos >= first_ref[...]) & (key_pos <= query_pos)
        for h in range(heads):
            scores = lax.dot_general(
                q_ref[:, h * HEAD_WIDTH : (h + 1) * HEAD_WIDTH],
                keys,
                (((1,), (1,)), ((), ())),
                preferred_element_type=jnp.float32,
            )
            if masked:
                scores = jnp.where(visible, scores, HIDDEN_SCORE)
            old_max = max_ref[h]
            new_max = jnp.maximum(old_max, jnp.max(scores, axis=1, keepdims=True))
            rescale = jnp.exp2((old_max - new_max) * scale)
            weights = jnp.exp2(scores * scale - new_max[:, :1] * scale)
            partial = weights[:, :HEAD_WIDTH]
            for g in range(1, KEY_TILE // HEAD_WIDTH):
                partial = partial + weights[:, g * HEAD_WIDTH : (g + 1) * HEAD_WIDTH]
            max_ref[h] = new_max
            sum_ref[h] = sum_ref[h] * rescale + partial
            acc_ref[h] = acc_ref[h] * rescale + jnp.dot(
                weights.astype(jnp.bfloat16), values, preferred_element_type=jnp.float32
            )

    low, full_low, full_high, high = (bounds_ref[4 * tile + i] for i in range(4))
    pl.loop(low, full_low)(lambda k: visit(k, True))
    pl.loop(full_low, full_high)(lambda k: visit(k, False))
    pl.loop(full_high, high)(lambda k: visit(k, True))
    for h in range(heads):
        total = jnp.sum(sum_ref[h], axis=1, keepdims=True)
        o_ref[:, h * HEAD_WIDTH : (h + 1) * HEAD_WIDTH] = (acc_ref[h] / total).astype(jnp.bfloat16)


def attend(queries, window, first_key):
    rows, columns = queries.shape
    tile = math.gcd(rows, QUERY_TILE)
    tiles = rows // tile
    before = window.shape[0] - rows
    heads = columns // HEAD_WIDTH
    at = before + tile * jnp.arange(tiles, dtype=jnp.int32)
    first = first_key.reshape(tiles, tile)
    low = first[:, 0] // KEY_TILE
    high = (at + tile - 1) // KEY_TILE + 1
    full_low = jnp.clip((first[:, -1] + KEY_TILE - 1) // KEY_TILE, low, high)
    full_high = jnp.maximum(full_low, jnp.minimum((at + 1) // KEY_TILE, high))
    bounds = jnp.stack([low, full_low, full_high, high], axis=1).reshape(-1)
    return pl.pallas_call(
        attention_kernel,
        grid_spec=pltpu.PrefetchScalarGridSpec(
            num_scalar_prefetch=1,
            grid=(tiles,),
            in_specs=[
                pl.BlockSpec((tile, columns), lambda i, b: (i, 0)),
                pl.BlockSpec(window.shape, lambda i, b: (0, 0)),
                pl.BlockSpec((tile, 1), lambda i, b: (i, 0)),
            ],
            out_specs=pl.BlockSpec((tile, columns), lambda i, b: (i, 0)),
            scratch_shapes=[
                pltpu.VMEM((heads, tile, HEAD_WIDTH), jnp.float32),
                pltpu.VMEM((heads, tile, HEAD_WIDTH), jnp.float32),
                pltpu.VMEM((heads, tile, HEAD_WIDTH), jnp.float32),
            ],
        ),
        out_shape=jax.ShapeDtypeStruct((rows, columns), jnp.bfloat16),
        compiler_params=pltpu.CompilerParams(vmem_limit_bytes=48 * 1024 * 1024),
        cost_estimate=pl.CostEstimate(
            flops=4 * rows * columns * window.shape[0] // 2,
            bytes_accessed=4 * rows * columns + 2 * window.size,
            transcendentals=rows * heads * window.shape[0] // 2,
        ),
    )(bounds, queries, window, first_key[:, None])


def local(hidden, gain, basis, w_query, key_matrix, value_matrix, doc_ids):
    ctx_count, tp_count = lax.axis_size("ctx"), lax.axis_size("tp")
    ctx_rank, tp_rank = lax.axis_index("ctx"), lax.axis_index("tp")
    values = hidden.astype(jnp.float32)
    meansq = jnp.mean(values * values, axis=-1, keepdims=True)
    normed = (values * lax.rsqrt(meansq + 1e-05) * gain.astype(jnp.float32)).astype(jnp.bfloat16)

    token_rows = lax.all_gather(normed, "tp", axis=0, tiled=True)
    block_len = token_rows.shape[0]
    head_count = w_query.shape[1] // HEAD_WIDTH
    kv_head = tp_rank * head_count // (QUERY_HEADS // KEY_VALUE_HEADS)
    key_columns = lax.dynamic_slice_in_dim(key_matrix, kv_head * HEAD_WIDTH, HEAD_WIDTH, 1)
    value_columns = lax.dynamic_slice_in_dim(value_matrix, kv_head * HEAD_WIDTH, HEAD_WIDTH, 1)
    weights = jnp.concatenate([w_query, key_columns, value_columns], axis=1)
    first_token = ctx_rank * block_len
    row_index = jnp.arange(block_len, dtype=jnp.int32)
    cosine, sine = rotary_tables((first_token + row_index).astype(jnp.float32))

    ids = lax.all_gather(doc_ids, ("ctx", "tp"), axis=0, tiled=True)
    block_ids = lax.dynamic_slice_in_dim(ids, first_token, block_len, 0)
    doc_first = jnp.zeros_like(block_ids)
    for d in range(1, DOCS):
        doc_first = jnp.where(block_ids == d, jnp.sum((ids < d).astype(jnp.int32)), doc_first)
    blocks_before = min(-(-(LONGEST_DOC - 1) // block_len), ctx_count - 1)
    first_key = doc_first - first_token + blocks_before * block_len

    column_part = jnp.dot(token_rows, basis, preferred_element_type=jnp.float32).astype(jnp.bfloat16)
    projected = lax.all_gather(column_part, "tp", axis=0, tiled=False)
    queries, key_values = project_heads(projected, weights, cosine, sine, w_query.shape[1])

    half = block_len // 2
    core = tp_rank % 2
    swap = [(t, t ^ 1) for t in range(tp_count)]
    mine = lax.dynamic_slice_in_dim(key_values, core * half, half, 0)
    fetched = jnp.stack(
        [
            lax.ppermute(mine, "ctx", [(i, i + s) for i in range(ctx_count - s)])
            for s in range(blocks_before, 0, -1)
        ]
    )
    other = lax.ppermute(fetched, "tp", swap)
    first_half = jnp.where(core == 0, fetched, other)
    second_half = jnp.where(core == 0, other, fetched)
    earlier = jnp.concatenate([first_half, second_half], axis=1).reshape(-1, 2 * HEAD_WIDTH)
    window = jnp.concatenate([earlier, key_values], axis=0)
    attended = attend(queries, window, first_key)
    return lax.all_to_all(attended, "tp", split_axis=0, concat_axis=1, tiled=True)


def solution(mesh):
    in_specs = (
        P(("dp", "ctx", "tp"), None),
        P(),
        P(None, "tp"),
        P(None, "tp"),
        P(),
        P(),
        P(("dp", "ctx", "tp")),
    )
    out_specs = P(("dp", "ctx", "tp"), None)
    return jax.shard_map(local, mesh=mesh, in_specs=in_specs, out_specs=out_specs, check_vma=False)
```

```python
import math

import jax
import jax.numpy as jnp
from jax import lax
from jax.experimental import pallas as pl
from jax.experimental.pallas import tpu as pltpu
from jax.sharding import PartitionSpec as P

HEAD_WIDTH = 128
DOCS = 8
LONGEST_DOC = 4096
CORES = 2
CHUNKS = (32, 32, 32, 32)
HIDDEN_SCORE = -1e30
LOWEST_MAX = -0.5e30
VMEM_BYTES = 48 * 1024 * 1024


def rotary_tables(positions):
    half_width = HEAD_WIDTH // 2
    frequency = 500000.0 ** (-jnp.arange(half_width, dtype=jnp.float32) * 2.0 / HEAD_WIDTH)
    angles = positions[:, None] * frequency
    cosine = jnp.cos(angles)
    sine = jnp.sin(angles)
    return (
        jnp.concatenate([cosine, cosine], axis=-1),
        jnp.concatenate([-sine, sine], axis=-1),
    )


def project_kernel(
    place_ref, own_ref, right_ref, left_ref, far_a_ref, far_b_ref, mine_ref, other_ref, o_ref, acc_ref
):
    step = pl.program_id(0)
    chips, count, _ = o_ref.shape
    chip = place_ref[0]
    rows = jnp.concatenate(
        [own_ref[...], right_ref[...], left_ref[...], far_a_ref[...], far_b_ref[...]], axis=0
    )
    wide = mine_ref.shape[1]

    @pl.when(step == 0)
    def _():
        acc_ref[...] = jnp.zeros_like(acc_ref)

    acc_ref[:, :wide] += jnp.dot(rows, mine_ref[...], preferred_element_type=jnp.float32)
    acc_ref[:, wide:] += jnp.dot(rows, other_ref[...], preferred_element_type=jnp.float32)

    @pl.when(step == pl.num_programs(0) - 1)
    def _():
        for slot, away in enumerate((0, chips - 1, 1, 2)):
            o_ref[lax.rem(chip + away, chips)] = acc_ref[slot * count : (slot + 1) * count, :].astype(
                jnp.bfloat16
            )


def project(place, own, right, left, far_a, far_b, mine, other, chips):
    count, depth = own.shape
    wide = mine.shape[1]
    block = math.gcd(depth, 1024)
    pieces = [own, right, left, far_a, far_b]
    return pl.pallas_call(
        project_kernel,
        grid_spec=pltpu.PrefetchScalarGridSpec(
            num_scalar_prefetch=1,
            grid=(depth // block,),
            in_specs=[pl.BlockSpec((piece.shape[0], block), lambda i, p: (0, i)) for piece in pieces]
            + [pl.BlockSpec((block, wide), lambda i, p: (i, 0))] * 2,
            out_specs=pl.BlockSpec((chips, count, 2 * wide), lambda i, p: (0, 0, 0)),
            scratch_shapes=[pltpu.VMEM((chips * count, 2 * wide), jnp.float32)],
        ),
        out_shape=jax.ShapeDtypeStruct((chips, count, 2 * wide), jnp.bfloat16),
        compiler_params=pltpu.CompilerParams(vmem_limit_bytes=VMEM_BYTES),
        cost_estimate=pl.CostEstimate(
            flops=4 * chips * count * depth * wide,
            bytes_accessed=2 * depth * (chips * count + 2 * wide),
            transcendentals=0,
        ),
    )(place, *pieces, mine, other)


def heads_kernel(
    place_ref,
    own_ref,
    right_ref,
    left_ref,
    far_a_ref,
    far_b_ref,
    mine_ref,
    other_ref,
    key_ref,
    value_ref,
    cos_ref,
    sin_ref,
    q_ref,
    kv_ref,
    x_ref,
    acc_ref,
):
    step = pl.program_id(0)
    parts, rows, depth = x_ref.shape
    chips = parts // CORES
    chip, core = place_ref[0], place_ref[1]
    wide = mine_ref.shape[1]

    @pl.when(step == 0)
    def _():
        acc_ref[...] = jnp.zeros_like(acc_ref)
        for away, piece in ((0, own_ref), (chips - 1, right_ref), (1, left_ref)):
            at = CORES * lax.rem(chip + away, chips)
            x_ref[at + core] = piece[:, :depth]
            x_ref[at + 1 - core] = piece[:, depth:]
        at = CORES * lax.rem(chip + 2, chips)
        half = rows // 2
        for start, piece in ((0, far_a_ref), (half, far_b_ref)):
            x_ref[at + core, start : start + half, :] = piece[:, :depth]
            x_ref[at + 1 - core, start : start + half, :] = piece[:, depth:]

    x = x_ref[step]
    acc_ref[:, :wide] += jnp.dot(x, mine_ref[...], preferred_element_type=jnp.float32)
    acc_ref[:, wide : 2 * wide] += jnp.dot(x, other_ref[...], preferred_element_type=jnp.float32)
    both = jnp.concatenate([key_ref[...], value_ref[...]], axis=1)
    acc_ref[:, 2 * wide :] += jnp.dot(x, both, preferred_element_type=jnp.float32)

    @pl.when(step == parts - 1)
    def _():
        cosine, sine = cos_ref[...], sin_ref[...]

        def rotated(start):
            u = acc_ref[:, start : start + HEAD_WIDTH]
            return (u * cosine + pltpu.roll(u, HEAD_WIDTH // 2, 1) * sine).astype(jnp.bfloat16)

        for side, at in ((0, core), (1, 1 - core)):
            for h in range(wide // HEAD_WIDTH):
                q_ref[at, :, h * HEAD_WIDTH : (h + 1) * HEAD_WIDTH] = rotated(
                    side * wide + h * HEAD_WIDTH
                )
        kv_ref[:, :HEAD_WIDTH] = rotated(2 * wide)
        kv_ref[:, HEAD_WIDTH:] = acc_ref[:, 2 * wide + HEAD_WIDTH :].astype(jnp.bfloat16)


def project_heads(place, pieces, mine, other, key_matrix, value_matrix, cosine, sine):
    rows, wide_in = pieces[0].shape
    depth = wide_in // CORES
    parts = mine.shape[0] // depth
    wide = mine.shape[1]
    total = 2 * wide + 2 * HEAD_WIDTH
    whole = lambda i, p: (0, 0)
    return pl.pallas_call(
        heads_kernel,
        grid_spec=pltpu.PrefetchScalarGridSpec(
            num_scalar_prefetch=1,
            grid=(parts,),
            in_specs=[pl.BlockSpec(piece.shape, whole) for piece in pieces]
            + [pl.BlockSpec((depth, wide), lambda i, p: (i, 0))] * 2
            + [pl.BlockSpec((depth, HEAD_WIDTH), lambda i, p: (i, p[0]))] * 2
            + [pl.BlockSpec((rows, HEAD_WIDTH), whole)] * 2,
            out_specs=[
                pl.BlockSpec((CORES, rows, wide), lambda i, p: (0, 0, 0)),
                pl.BlockSpec((rows, 2 * HEAD_WIDTH), whole),
            ],
            scratch_shapes=[
                pltpu.VMEM((parts, rows, depth), jnp.bfloat16),
                pltpu.VMEM((rows, total), jnp.float32),
            ],
        ),
        out_shape=[
            jax.ShapeDtypeStruct((CORES, rows, wide), jnp.bfloat16),
            jax.ShapeDtypeStruct((rows, 2 * HEAD_WIDTH), jnp.bfloat16),
        ],
        compiler_params=pltpu.CompilerParams(vmem_limit_bytes=VMEM_BYTES),
        cost_estimate=pl.CostEstimate(
            flops=2 * rows * parts * depth * total,
            bytes_accessed=2 * (rows * parts * depth + parts * depth * total + rows * total),
            transcendentals=0,
        ),
    )(place, *pieces, mine, other, key_matrix, value_matrix, cosine, sine)


def attention_kernel(
    place_ref, bounds_ref, q_ref, mine_ref, other_ref, first_ref, o_ref, q_all, max_ref, sum_ref, acc_ref
):
    tile = pl.program_id(0)
    core = place_ref[1]
    count = first_ref.shape[0]
    pairs, rows, _ = q_all.shape
    together = rows // count
    half_tile = 2 * count
    key_tile = CORES * half_tile
    window = CORES * mine_ref.shape[0]
    block = CORES * count * pl.num_programs(0)
    row_start = window - block + CORES * count * tile + count * core
    scale = HEAD_WIDTH**-0.5 * math.log2(math.e)
    per_half = q_ref.shape[3] // HEAD_WIDTH

    for pair in range(pairs):
        for inside in range(together):
            h = pair * together + inside
            start = (h % per_half) * HEAD_WIDTH
            q_all[pair, inside * count : (inside + 1) * count, :] = q_ref[
                h // per_half, 0, :, start : start + HEAD_WIDTH
            ]
    max_ref[...] = jnp.full(max_ref.shape, LOWEST_MAX, jnp.float32)
    sum_ref[...] = jnp.zeros(sum_ref.shape, jnp.float32)
    acc_ref[...] = jnp.zeros(acc_ref.shape, jnp.float32)

    def visit(key_at, masked):
        start = pl.multiple_of(key_at * half_tile, half_tile)
        at = pl.ds(start, half_tile)
        keys = jnp.concatenate([mine_ref[at, :HEAD_WIDTH], other_ref[at, :HEAD_WIDTH]], axis=0)
        values = jnp.concatenate([mine_ref[at, HEAD_WIDTH:], other_ref[at, HEAD_WIDTH:]], axis=0)
        if masked:
            column = lax.broadcasted_iota(jnp.int32, (count, key_tile), 1)
            side = column >= half_tile
            row = jnp.where(side, column - half_tile, column)
            of_core = jnp.where(side, 1 - core, core)
            key_pos = key_at * key_tile + row + jnp.where(row >= count, count, 0) + count * of_core
            query_pos = row_start + lax.broadcasted_iota(jnp.int32, (count, key_tile), 0)
            seen = (key_pos >= first_ref[...]) & (key_pos <= query_pos)
            hide = jnp.where(seen, 0.0, HIDDEN_SCORE)
            hide = jnp.concatenate([hide] * together, axis=0)
        for pair in range(pairs):
            scores = lax.dot_general(
                q_all[pair], keys, (((1,), (1,)), ((), ())), preferred_element_type=jnp.float32
            )
            if masked:
                scores = jnp.where(hide < 0.0, hide, scores)
            old_max = max_ref[pair]
            new_max = jnp.maximum(old_max, jnp.max(scores, axis=1, keepdims=True))
            rescale = jnp.exp2((old_max - new_max) * scale)
            weights = jnp.exp2(scores * scale - new_max[:, :1] * scale)
            partial = weights[:, :HEAD_WIDTH]
            for g in range(1, key_tile // HEAD_WIDTH):
                partial = partial + weights[:, g * HEAD_WIDTH : (g + 1) * HEAD_WIDTH]
            max_ref[pair] = new_max
            sum_ref[pair] = sum_ref[pair] * rescale + partial
            acc_ref[pair] = acc_ref[pair] * rescale + jnp.dot(
                weights.astype(jnp.bfloat16), values, preferred_element_type=jnp.float32
            )

    low, full_low, full_high, high = (bounds_ref[4 * tile + i] for i in range(4))
    pl.loop(low, full_low)(lambda k: visit(k, True))
    pl.loop(full_low, full_high)(lambda k: visit(k, False))
    pl.loop(full_high, high)(lambda k: visit(k, True))
    for pair in range(pairs):
        result = (acc_ref[pair] / jnp.sum(sum_ref[pair], axis=1, keepdims=True)).astype(jnp.bfloat16)
        for inside in range(together):
            h = pair * together + inside
            o_ref[0, :, h * HEAD_WIDTH : (h + 1) * HEAD_WIDTH] = result[
                inside * count : (inside + 1) * count, :
            ]


def attend(place, queries, mine, other, first_key):
    _, chips, count, wide = queries.shape
    core = place[1]
    window = CORES * mine.shape[0]
    key_tile = 2 * CORES * count
    heads = CORES * wide // HEAD_WIDTH
    together = 2
    at = window - CORES * chips * count + CORES * count * jnp.arange(chips, dtype=jnp.int32) + core * count
    low = first_key[:, 0] // key_tile
    high = (at + count - 1) // key_tile + 1
    full_low = jnp.clip((first_key[:, -1] + key_tile - 1) // key_tile, low, high)
    full_high = jnp.maximum(full_low, jnp.minimum((at + 1) // key_tile, high))
    bounds = jnp.stack([low, full_low, full_high, high], axis=1).reshape(-1)
    state = pltpu.VMEM((heads // together, together * count, HEAD_WIDTH), jnp.float32)
    return pl.pallas_call(
        attention_kernel,
        grid_spec=pltpu.PrefetchScalarGridSpec(
            num_scalar_prefetch=2,
            grid=(chips,),
            in_specs=[
                pl.BlockSpec((CORES, 1, count, wide), lambda i, p, b: (0, i, 0, 0)),
                pl.BlockSpec(mine.shape, lambda i, p, b: (0, 0)),
                pl.BlockSpec(other.shape, lambda i, p, b: (0, 0)),
                pl.BlockSpec((count, 1), lambda i, p, b: (i, 0)),
            ],
            out_specs=pl.BlockSpec((1, count, CORES * wide), lambda i, p, b: (i, 0, 0)),
            scratch_shapes=[
                pltpu.VMEM((heads // together, together * count, HEAD_WIDTH), jnp.bfloat16),
                state,
                state,
                state,
            ],
        ),
        out_shape=jax.ShapeDtypeStruct((chips, count, CORES * wide), jnp.bfloat16),
        compiler_params=pltpu.CompilerParams(vmem_limit_bytes=VMEM_BYTES),
        cost_estimate=pl.CostEstimate(
            flops=2 * queries.size * window,
            bytes_accessed=4 * queries.size + 4 * mine.size,
            transcendentals=chips * count * heads * window // 2,
        ),
    )(place, bounds, queries, mine, other, first_key.reshape(-1, 1))


def local(hidden, gain, basis, w_query, key_matrix, value_matrix, doc_ids):
    ctx_count, tp_count = lax.axis_size("ctx"), lax.axis_size("tp")
    ctx_rank, tp_rank = lax.axis_index("ctx"), lax.axis_index("tp")
    chips = tp_count // CORES
    chip, core = tp_rank // CORES, tp_rank % CORES
    place = jnp.stack([chip, core]).astype(jnp.int32)
    count = hidden.shape[0]
    block_len = count * tp_count

    def along(value, step):
        moves = [(t, ((t // CORES + step) % chips) * CORES + t % CORES) for t in range(tp_count)]
        return lax.ppermute(value, "tp", moves)

    def swapped(value):
        return lax.ppermute(value, "tp", [(t, t ^ 1) for t in range(tp_count)])

    def spread(value):
        half = value.shape[0] // 2
        right, left = along(value, 1), along(value, -1)
        return value, right, left, along(right[:half], 1), along(left[half:], -1)

    basis_other = swapped(basis)
    query_other = swapped(w_query)

    smaller = jnp.sum(
        (doc_ids[None, :] < jnp.arange(DOCS, dtype=jnp.int32)[:, None]).astype(jnp.int32), axis=1
    )
    doc_starts = lax.psum(smaller, ("ctx", "tp"))

    first_token = ctx_rank * block_len
    row_pos = (
        first_token
        + CORES * count * jnp.arange(chips, dtype=jnp.int32)[:, None]
        + count * core
        + jnp.arange(count, dtype=jnp.int32)[None, :]
    )
    cosine, sine = rotary_tables(row_pos.reshape(-1).astype(jnp.float32))
    cosine = cosine.reshape(chips, count, HEAD_WIDTH)
    sine = sine.reshape(chips, count, HEAD_WIDTH)
    doc_first = jnp.max(
        jnp.where(doc_starts[:, None, None] <= row_pos[None], doc_starts[:, None, None], 0), axis=0
    )
    blocks_before = min(-(-(LONGEST_DOC - 1) // block_len), ctx_count - 1)
    first_key = doc_first - first_token + blocks_before * block_len

    queries, key_values = [], []
    begin = 0
    for size in CHUNKS:
        values = hidden[begin : begin + size].astype(jnp.float32)
        meansq = jnp.mean(values * values, axis=-1, keepdims=True)
        normed = (values * lax.rsqrt(meansq + 1e-05) * gain.astype(jnp.float32)).astype(jnp.bfloat16)
        columns = project(place, *spread(normed), basis, basis_other, chips)
        pieces = spread(columns.reshape(chips * size, -1))
        chunk_q, chunk_kv = project_heads(
            place,
            pieces,
            w_query,
            query_other,
            key_matrix,
            value_matrix,
            cosine[:, begin : begin + size].reshape(chips * size, HEAD_WIDTH),
            sine[:, begin : begin + size].reshape(chips * size, HEAD_WIDTH),
        )
        queries.append(chunk_q.reshape(CORES, chips, size, -1))
        key_values.append(chunk_kv.reshape(chips, size, -1))
        begin += size

    queries = jnp.concatenate(queries, axis=2)
    own = jnp.concatenate(key_values, axis=1).reshape(chips * count, -1)
    fetched = [
        lax.ppermute(own, "ctx", [(i, i + s) for i in range(ctx_count - s)])
        for s in range(blocks_before, 0, -1)
    ]
    mine = jnp.concatenate(fetched + [own], axis=0)
    other = swapped(mine)
    attended = attend(place, queries, mine, other, first_key)

    def rows_for(away):
        return lax.dynamic_index_in_dim(attended, (chip + away) % chips, 0, keepdims=False)

    received = jnp.stack([rows_for(0)] + [along(rows_for(away), away) for away in range(1, chips)])
    return jnp.concatenate(
        [
            lax.dynamic_index_in_dim(received, (chip - g) % chips, 0, keepdims=False)
            for g in range(chips)
        ],
        axis=1,
    )


def solution(mesh):
    in_specs = (
        P(("dp", "ctx", "tp"), None),
        P(),
        P(None, "tp"),
        P(None, "tp"),
        P(),
        P(),
        P(("dp", "ctx", "tp")),
    )
    out_specs = P(("dp", "ctx", "tp"), None)
    return jax.shard_map(local, mesh=mesh, in_specs=in_specs, out_specs=out_specs, check_vma=False)
```

```python
import math

import jax
import jax.numpy as jnp
from jax import lax
from jax.experimental import pallas as pl
from jax.experimental.pallas import tpu as pltpu
from jax.sharding import PartitionSpec as P

HEAD_WIDTH = 128
DOCS = 8
LONGEST_DOC = 4096
CORES = 2
CHUNKS = (64, 64)
HIDDEN_SCORE = -1e30
LOWEST_MAX = -0.5e30
VMEM_BYTES = 24 * 1024 * 1024


def rotary_tables(positions):
    half_width = HEAD_WIDTH // 2
    frequency = 500000.0 ** (-jnp.arange(half_width, dtype=jnp.float32) * 2.0 / HEAD_WIDTH)
    angles = positions[:, None] * frequency
    cosine = jnp.cos(angles)
    sine = jnp.sin(angles)
    return (
        jnp.concatenate([cosine, cosine], axis=-1),
        jnp.concatenate([-sine, sine], axis=-1),
    )


def project_kernel(
    place_ref, own_ref, right_ref, left_ref, far_a_ref, far_b_ref, mine_ref, other_ref, o_ref, acc_ref
):
    step = pl.program_id(0)
    chips, count, _ = o_ref.shape
    chip = place_ref[0]
    rows = jnp.concatenate(
        [own_ref[...], right_ref[...], left_ref[...], far_a_ref[...], far_b_ref[...]], axis=0
    )
    wide = mine_ref.shape[1]

    @pl.when(step == 0)
    def _():
        acc_ref[...] = jnp.zeros_like(acc_ref)

    acc_ref[:, :wide] += jnp.dot(rows, mine_ref[...], preferred_element_type=jnp.float32)
    acc_ref[:, wide:] += jnp.dot(rows, other_ref[...], preferred_element_type=jnp.float32)

    @pl.when(step == pl.num_programs(0) - 1)
    def _():
        for slot, away in enumerate((0, chips - 1, 1, 2)):
            o_ref[lax.rem(chip + away, chips)] = acc_ref[slot * count : (slot + 1) * count, :].astype(
                jnp.bfloat16
            )


def project(place, own, right, left, far_a, far_b, mine, other, chips):
    count, depth = own.shape
    wide = mine.shape[1]
    block = math.gcd(depth, 2048)
    pieces = [own, right, left, far_a, far_b]
    return pl.pallas_call(
        project_kernel,
        grid_spec=pltpu.PrefetchScalarGridSpec(
            num_scalar_prefetch=1,
            grid=(depth // block,),
            in_specs=[pl.BlockSpec((piece.shape[0], block), lambda i, p: (0, i)) for piece in pieces]
            + [pl.BlockSpec((block, wide), lambda i, p: (i, 0))] * 2,
            out_specs=pl.BlockSpec((chips, count, 2 * wide), lambda i, p: (0, 0, 0)),
            scratch_shapes=[pltpu.VMEM((chips * count, 2 * wide), jnp.float32)],
        ),
        out_shape=jax.ShapeDtypeStruct((chips, count, 2 * wide), jnp.bfloat16),
        compiler_params=pltpu.CompilerParams(vmem_limit_bytes=VMEM_BYTES),
        cost_estimate=pl.CostEstimate(
            flops=4 * chips * count * depth * wide,
            bytes_accessed=2 * depth * (chips * count + 2 * wide),
            transcendentals=0,
        ),
    )(place, *pieces, mine, other)


def heads_kernel(
    place_ref,
    own_ref,
    right_ref,
    left_ref,
    far_a_ref,
    far_b_ref,
    mine_ref,
    other_ref,
    key_ref,
    value_ref,
    cos_ref,
    sin_ref,
    q_ref,
    kv_ref,
    x_ref,
    acc_ref,
):
    step = pl.program_id(0)
    parts, rows, depth = x_ref.shape
    chips = parts // CORES
    chip, core = place_ref[0], place_ref[1]
    wide = mine_ref.shape[1]

    @pl.when(step == 0)
    def _():
        acc_ref[...] = jnp.zeros_like(acc_ref)
        for away, piece in ((0, own_ref), (chips - 1, right_ref), (1, left_ref)):
            at = CORES * lax.rem(chip + away, chips)
            x_ref[at + core] = piece[:, :depth]
            x_ref[at + 1 - core] = piece[:, depth:]
        at = CORES * lax.rem(chip + 2, chips)
        half = rows // 2
        for start, piece in ((0, far_a_ref), (half, far_b_ref)):
            x_ref[at + core, start : start + half, :] = piece[:, :depth]
            x_ref[at + 1 - core, start : start + half, :] = piece[:, depth:]

    x = x_ref[step]
    acc_ref[:, :wide] += jnp.dot(x, mine_ref[...], preferred_element_type=jnp.float32)
    acc_ref[:, wide : 2 * wide] += jnp.dot(x, other_ref[...], preferred_element_type=jnp.float32)
    both = jnp.concatenate([key_ref[...], value_ref[...]], axis=1)
    acc_ref[:, 2 * wide :] += jnp.dot(x, both, preferred_element_type=jnp.float32)

    @pl.when(step == parts - 1)
    def _():
        cosine, sine = cos_ref[...], sin_ref[...]

        def rotated(start):
            u = acc_ref[:, start : start + HEAD_WIDTH]
            return (u * cosine + pltpu.roll(u, HEAD_WIDTH // 2, 1) * sine).astype(jnp.bfloat16)

        for side, at in ((0, core), (1, 1 - core)):
            for h in range(wide // HEAD_WIDTH):
                q_ref[at, :, h * HEAD_WIDTH : (h + 1) * HEAD_WIDTH] = rotated(
                    side * wide + h * HEAD_WIDTH
                )
        kv_ref[:, :HEAD_WIDTH] = rotated(2 * wide)
        kv_ref[:, HEAD_WIDTH:] = acc_ref[:, 2 * wide + HEAD_WIDTH :].astype(jnp.bfloat16)


def project_heads(place, pieces, mine, other, key_matrix, value_matrix, cosine, sine):
    rows, wide_in = pieces[0].shape
    depth = wide_in // CORES
    parts = mine.shape[0] // depth
    wide = mine.shape[1]
    total = 2 * wide + 2 * HEAD_WIDTH
    whole = lambda i, p: (0, 0)
    return pl.pallas_call(
        heads_kernel,
        grid_spec=pltpu.PrefetchScalarGridSpec(
            num_scalar_prefetch=1,
            grid=(parts,),
            in_specs=[pl.BlockSpec(piece.shape, whole) for piece in pieces]
            + [pl.BlockSpec((depth, wide), lambda i, p: (i, 0))] * 2
            + [pl.BlockSpec((depth, HEAD_WIDTH), lambda i, p: (i, p[0]))] * 2
            + [pl.BlockSpec((rows, HEAD_WIDTH), whole)] * 2,
            out_specs=[
                pl.BlockSpec((CORES, rows, wide), lambda i, p: (0, 0, 0)),
                pl.BlockSpec((rows, 2 * HEAD_WIDTH), whole),
            ],
            scratch_shapes=[
                pltpu.VMEM((parts, rows, depth), jnp.bfloat16),
                pltpu.VMEM((rows, total), jnp.float32),
            ],
        ),
        out_shape=[
            jax.ShapeDtypeStruct((CORES, rows, wide), jnp.bfloat16),
            jax.ShapeDtypeStruct((rows, 2 * HEAD_WIDTH), jnp.bfloat16),
        ],
        compiler_params=pltpu.CompilerParams(vmem_limit_bytes=VMEM_BYTES),
        cost_estimate=pl.CostEstimate(
            flops=2 * rows * parts * depth * total,
            bytes_accessed=2 * (rows * parts * depth + parts * depth * total + rows * total),
            transcendentals=0,
        ),
    )(place, *pieces, mine, other, key_matrix, value_matrix, cosine, sine)


def attention_kernel(
    place_ref, bounds_ref, q_ref, mine_ref, other_ref, first_ref, o_ref, q_all, max_ref, sum_ref, acc_ref
):
    tile = pl.program_id(0)
    core = place_ref[1]
    count = first_ref.shape[0]
    pairs, rows, _ = q_all.shape
    together = rows // count
    half_tile = 2 * count
    key_tile = CORES * half_tile
    window = CORES * mine_ref.shape[0]
    block = CORES * count * pl.num_programs(0)
    row_start = window - block + CORES * count * tile + count * core
    scale = HEAD_WIDTH**-0.5 * math.log2(math.e)
    per_half = q_ref.shape[3] // HEAD_WIDTH

    for pair in range(pairs):
        for inside in range(together):
            h = pair * together + inside
            start = (h % per_half) * HEAD_WIDTH
            q_all[pair, inside * count : (inside + 1) * count, :] = q_ref[
                h // per_half, 0, :, start : start + HEAD_WIDTH
            ]
    max_ref[...] = jnp.full(max_ref.shape, LOWEST_MAX, jnp.float32)
    sum_ref[...] = jnp.zeros(sum_ref.shape, jnp.float32)
    acc_ref[...] = jnp.zeros(acc_ref.shape, jnp.float32)

    def visit(key_at, masked):
        start = pl.multiple_of(key_at * half_tile, half_tile)
        at = pl.ds(start, half_tile)
        keys = jnp.concatenate([mine_ref[at, :HEAD_WIDTH], other_ref[at, :HEAD_WIDTH]], axis=0)
        values = jnp.concatenate([mine_ref[at, HEAD_WIDTH:], other_ref[at, HEAD_WIDTH:]], axis=0)
        if masked:
            column = lax.broadcasted_iota(jnp.int32, (count, key_tile), 1)
            side = column >= half_tile
            row = jnp.where(side, column - half_tile, column)
            of_core = jnp.where(side, 1 - core, core)
            key_pos = key_at * key_tile + row + jnp.where(row >= count, count, 0) + count * of_core
            query_pos = row_start + lax.broadcasted_iota(jnp.int32, (count, key_tile), 0)
            seen = (key_pos >= first_ref[...]) & (key_pos <= query_pos)
            hide = jnp.where(seen, 0.0, HIDDEN_SCORE)
            hide = jnp.concatenate([hide] * together, axis=0)
        for pair in range(pairs):
            scores = lax.dot_general(
                q_all[pair], keys, (((1,), (1,)), ((), ())), preferred_element_type=jnp.float32
            )
            if masked:
                scores = jnp.where(hide < 0.0, hide, scores)
            old_max = max_ref[pair]
            new_max = jnp.maximum(old_max, jnp.max(scores, axis=1, keepdims=True))
            rescale = jnp.exp2((old_max - new_max) * scale)
            weights = jnp.exp2(scores * scale - new_max[:, :1] * scale)
            partial = weights[:, :HEAD_WIDTH]
            for g in range(1, key_tile // HEAD_WIDTH):
                partial = partial + weights[:, g * HEAD_WIDTH : (g + 1) * HEAD_WIDTH]
            max_ref[pair] = new_max
            sum_ref[pair] = sum_ref[pair] * rescale + partial
            acc_ref[pair] = acc_ref[pair] * rescale + jnp.dot(
                weights.astype(jnp.bfloat16), values, preferred_element_type=jnp.float32
            )

    low, full_low, full_high, high = (bounds_ref[4 * tile + i] for i in range(4))
    pl.loop(low, full_low)(lambda k: visit(k, True))
    pl.loop(full_low, full_high)(lambda k: visit(k, False))
    pl.loop(full_high, high)(lambda k: visit(k, True))
    for pair in range(pairs):
        result = (acc_ref[pair] / jnp.sum(sum_ref[pair], axis=1, keepdims=True)).astype(jnp.bfloat16)
        for inside in range(together):
            h = pair * together + inside
            o_ref[0, :, h * HEAD_WIDTH : (h + 1) * HEAD_WIDTH] = result[
                inside * count : (inside + 1) * count, :
            ]


def attend(place, queries, mine, other, first_key):
    _, chips, count, wide = queries.shape
    core = place[1]
    window = CORES * mine.shape[0]
    key_tile = 2 * CORES * count
    heads = CORES * wide // HEAD_WIDTH
    together = 2
    at = window - CORES * chips * count + CORES * count * jnp.arange(chips, dtype=jnp.int32) + core * count
    low = first_key[:, 0] // key_tile
    high = (at + count - 1) // key_tile + 1
    full_low = jnp.clip((first_key[:, -1] + key_tile - 1) // key_tile, low, high)
    full_high = jnp.maximum(full_low, jnp.minimum((at + 1) // key_tile, high))
    bounds = jnp.stack([low, full_low, full_high, high], axis=1).reshape(-1)
    state = pltpu.VMEM((heads // together, together * count, HEAD_WIDTH), jnp.float32)
    return pl.pallas_call(
        attention_kernel,
        grid_spec=pltpu.PrefetchScalarGridSpec(
            num_scalar_prefetch=2,
            grid=(chips,),
            in_specs=[
                pl.BlockSpec((CORES, 1, count, wide), lambda i, p, b: (0, i, 0, 0)),
                pl.BlockSpec(mine.shape, lambda i, p, b: (0, 0)),
                pl.BlockSpec(other.shape, lambda i, p, b: (0, 0)),
                pl.BlockSpec((count, 1), lambda i, p, b: (i, 0)),
            ],
            out_specs=pl.BlockSpec((1, count, CORES * wide), lambda i, p, b: (i, 0, 0)),
            scratch_shapes=[
                pltpu.VMEM((heads // together, together * count, HEAD_WIDTH), jnp.bfloat16),
                state,
                state,
                state,
            ],
        ),
        out_shape=jax.ShapeDtypeStruct((chips, count, CORES * wide), jnp.bfloat16),
        compiler_params=pltpu.CompilerParams(vmem_limit_bytes=VMEM_BYTES),
        cost_estimate=pl.CostEstimate(
            flops=2 * queries.size * window,
            bytes_accessed=4 * queries.size + 4 * mine.size,
            transcendentals=chips * count * heads * window // 2,
        ),
    )(place, bounds, queries, mine, other, first_key.reshape(-1, 1))


def local(hidden, gain, basis, w_query, key_matrix, value_matrix, doc_ids):
    ctx_count, tp_count = lax.axis_size("ctx"), lax.axis_size("tp")
    ctx_rank, tp_rank = lax.axis_index("ctx"), lax.axis_index("tp")
    chips = tp_count // CORES
    chip, core = tp_rank // CORES, tp_rank % CORES
    place = jnp.stack([chip, core]).astype(jnp.int32)
    count = hidden.shape[0]
    block_len = count * tp_count

    def along(value, step):
        moves = [(t, ((t // CORES + step) % chips) * CORES + t % CORES) for t in range(tp_count)]
        return lax.ppermute(value, "tp", moves)

    def swapped(value):
        return lax.ppermute(value, "tp", [(t, t ^ 1) for t in range(tp_count)])

    def after(value, *others):
        return lax.optimization_barrier((value, *others))[0]

    def spread(value, gate):
        half = value.shape[0] // 2
        right, left = along(value, 1), along(value, -1)
        if gate is None:
            return value, right, left, along(right[:half], 1), along(left[half:], -1)
        onward_right, onward_left = after(right, gate)[:half], after(left, gate)[half:]
        return value, right, left, along(onward_right, 1), along(onward_left, -1)

    basis_other = swapped(basis)
    query_other = swapped(w_query)

    first_token = ctx_rank * block_len
    row_pos = (
        first_token
        + CORES * count * jnp.arange(chips, dtype=jnp.int32)[:, None]
        + count * core
        + jnp.arange(count, dtype=jnp.int32)[None, :]
    )
    cosine, sine = rotary_tables(row_pos.reshape(-1).astype(jnp.float32))
    cosine = cosine.reshape(chips, count, HEAD_WIDTH)
    sine = sine.reshape(chips, count, HEAD_WIDTH)
    blocks_before = min(-(-(LONGEST_DOC - 1) // block_len), ctx_count - 1)
    def normed_rows(start, size):
        values = hidden[start : start + size].astype(jnp.float32)
        meansq = jnp.mean(values * values, axis=-1, keepdims=True)
        return (values * lax.rsqrt(meansq + 1e-05) * gain.astype(jnp.float32)).astype(jnp.bfloat16)

    begins = [sum(CHUNKS[:k]) for k in range(len(CHUNKS))]
    normed = [normed_rows(begin, size) for begin, size in zip(begins, CHUNKS)]

    smaller = jnp.sum(
        (after(doc_ids, normed[0])[None, :] < jnp.arange(DOCS, dtype=jnp.int32)[:, None]).astype(
            jnp.int32
        ),
        axis=1,
    )
    doc_starts = lax.psum(smaller, ("ctx", "tp"))
    doc_first = jnp.max(
        jnp.where(doc_starts[:, None, None] <= row_pos[None], doc_starts[:, None, None], 0), axis=0
    )
    first_key = doc_first - first_token + blocks_before * block_len

    columns, pieces = [], []
    for k, rows in enumerate(normed):
        if k == 1:
            rows = after(rows, doc_starts)
        gathered = spread(rows, columns[-1] if columns else None)
        columns.append(project(place, *gathered, basis, basis_other, chips))
        pieces.append(spread(columns[-1].reshape(chips * CHUNKS[k], -1), None))
    queries, mine, other = [], [], []
    for k, size in enumerate(CHUNKS):
        begin = begins[k]
        chunk = pieces[k]
        if k + 1 < len(CHUNKS):
            chunk = (after(chunk[0], columns[k + 1]),) + chunk[1:]
        chunk_q, chunk_kv = project_heads(
            place,
            chunk,
            w_query,
            query_other,
            key_matrix,
            value_matrix,
            cosine[:, begin : begin + size].reshape(chips * size, HEAD_WIDTH),
            sine[:, begin : begin + size].reshape(chips * size, HEAD_WIDTH),
        )
        queries.append(chunk_q.reshape(CORES, chips, size, -1))
        blocks = [
            lax.ppermute(chunk_kv, "ctx", [(i, i + s) for i in range(ctx_count - s)])
            for s in range(blocks_before, 0, -1)
        ] + [chunk_kv]
        fetched = jnp.stack(blocks)
        mine.append(fetched.reshape(-1, size, 2 * HEAD_WIDTH))
        other.append(swapped(fetched).reshape(-1, size, 2 * HEAD_WIDTH))

    queries = jnp.concatenate(queries, axis=2)
    mine = jnp.concatenate(mine, axis=1).reshape(-1, 2 * HEAD_WIDTH)
    other = jnp.concatenate(other, axis=1).reshape(-1, 2 * HEAD_WIDTH)
    attended = attend(place, queries, mine, other, first_key)

    def rows_for(away):
        return lax.dynamic_index_in_dim(attended, (chip + away) % chips, 0, keepdims=False)

    received = jnp.stack([rows_for(0)] + [along(rows_for(away), away) for away in range(1, chips)])
    return jnp.concatenate(
        [
            lax.dynamic_index_in_dim(received, (chip - g) % chips, 0, keepdims=False)
            for g in range(chips)
        ],
        axis=1,
    )


def solution(mesh):
    in_specs = (
        P(("dp", "ctx", "tp"), None),
        P(),
        P(None, "tp"),
        P(None, "tp"),
        P(),
        P(),
        P(("dp", "ctx", "tp")),
    )
    out_specs = P(("dp", "ctx", "tp"), None)
    return jax.shard_map(local, mesh=mesh, in_specs=in_specs, out_specs=out_specs, check_vma=False)
```

```python
import functools
import math

import jax
import jax.numpy as jnp
from jax import lax
from jax.experimental import pallas as pl
from jax.experimental.pallas import tpu as pltpu
from jax.sharding import PartitionSpec as P

HEAD_WIDTH = 128
DOCS = 8
LONGEST_DOC = 4096
CORES = 2
CHUNKS = (64, 64)
HIDDEN_SCORE = -1e30
LOWEST_MAX = -0.5e30
VMEM_BYTES = 28 * 1024 * 1024
COLUMN_TILE = 256
PER_DEVICE = sum(CHUNKS)
SMALL_COST = pl.CostEstimate(flops=1, bytes_accessed=1, transcendentals=0)


def rotary_tables(positions):
    half_width = HEAD_WIDTH // 2
    frequency = 500000.0 ** (-jnp.arange(half_width, dtype=jnp.float32) * 2.0 / HEAD_WIDTH)
    angles = positions[:, None] * frequency
    cosine = jnp.cos(angles)
    sine = jnp.sin(angles)
    return (
        jnp.concatenate([cosine, cosine], axis=-1),
        jnp.concatenate([-sine, sine], axis=-1),
    )


def ring_order(place_ref, chips):
    chip = place_ref[0]
    return [lax.rem(chip + away, chips) for away in (0, chips - 1, 1, 2)]


def project_kernel(
    place_ref, own_ref, right_ref, left_ref, far_ref, mine_ref, other_ref, o_ref
):
    chips, count, columns = o_ref.shape
    rows = jnp.concatenate([own_ref[...], right_ref[...], left_ref[...], far_ref[...]], axis=0)
    order = ring_order(place_ref, chips)
    wide = columns // CORES
    for side, w_ref in enumerate((mine_ref, other_ref)):
        for n in range(0, wide, COLUMN_TILE):
            result = jnp.dot(
                rows, w_ref[:, n : n + COLUMN_TILE], preferred_element_type=jnp.float32
            ).astype(jnp.bfloat16)
            at = side * wide + n
            for slot, chip in enumerate(order):
                o_ref[chip, :, at : at + COLUMN_TILE] = result[slot * count : (slot + 1) * count, :]


def project(place, pieces, mine, other, chips):
    count, depth = pieces[0].shape
    wide = mine.shape[1]
    vmem = pl.BlockSpec(memory_space=pltpu.VMEM)
    return pl.pallas_call(
        project_kernel,
        in_specs=[pl.BlockSpec(memory_space=pltpu.SMEM)] + [vmem] * 6,
        out_specs=vmem,
        out_shape=jax.ShapeDtypeStruct((chips, count, CORES * wide), jnp.bfloat16),
        compiler_params=pltpu.CompilerParams(vmem_limit_bytes=VMEM_BYTES),
        cost_estimate=SMALL_COST,
    )(place, *pieces, mine, other)


def heads_kernel(
    place_ref,
    own_ref,
    right_ref,
    left_ref,
    far_ref,
    mine_ref,
    other_ref,
    kv_weights_ref,
    cos_ref,
    sin_ref,
    q_ref,
    kv_ref,
):
    parts, depth, wide = mine_ref.shape
    core = place_ref[1]
    order = ring_order(place_ref, parts // CORES)
    pieces = [own_ref[...], right_ref[...], left_ref[...], far_ref[...]]
    cosine, sine = cos_ref[...], sin_ref[...]

    def rotated(u):
        return (u * cosine + pltpu.roll(u, HEAD_WIDTH // 2, 1) * sine).astype(jnp.bfloat16)

    def product(w_ref, n):
        total = None
        for chip, piece in zip(order, pieces):
            for side, which in ((0, core), (1, 1 - core)):
                term = jnp.dot(
                    piece[:, side * depth : (side + 1) * depth],
                    w_ref[CORES * chip + which, :, n : n + 2 * HEAD_WIDTH],
                    preferred_element_type=jnp.float32,
                )
                total = term if total is None else total + term
        return total

    both = product(kv_weights_ref, 0)
    kv_ref[:, :HEAD_WIDTH] = rotated(both[:, :HEAD_WIDTH])
    kv_ref[:, HEAD_WIDTH:] = both[:, HEAD_WIDTH:].astype(jnp.bfloat16)
    for w_ref, at in ((mine_ref, core), (other_ref, 1 - core)):
        for n in range(0, wide, 2 * HEAD_WIDTH):
            both = product(w_ref, n)
            q_ref[at, :, n : n + HEAD_WIDTH] = rotated(both[:, :HEAD_WIDTH])
            q_ref[at, :, n + HEAD_WIDTH : n + 2 * HEAD_WIDTH] = rotated(both[:, HEAD_WIDTH:])


def project_heads(place, pieces, mine, other, kv_weights, cosine, sine):
    rows, wide_in = pieces[0].shape
    depth = wide_in // CORES
    wide = mine.shape[1]
    vmem = pl.BlockSpec(memory_space=pltpu.VMEM)
    by_part = [w.reshape(-1, depth, w.shape[1]) for w in (mine, other, kv_weights)]
    return pl.pallas_call(
        heads_kernel,
        in_specs=[pl.BlockSpec(memory_space=pltpu.SMEM)] + [vmem] * 9,
        out_specs=[vmem, vmem],
        out_shape=[
            jax.ShapeDtypeStruct((CORES, rows, wide), jnp.bfloat16),
            jax.ShapeDtypeStruct((rows, 2 * HEAD_WIDTH), jnp.bfloat16),
        ],
        compiler_params=pltpu.CompilerParams(vmem_limit_bytes=VMEM_BYTES),
        cost_estimate=SMALL_COST,
    )(place, *pieces, *by_part, cosine, sine)


def attention_kernel(settings, place_ref, order_ref, bounds_ref, *refs):
    query_sizes, offset, key_size, key_begin, chips, states, finish = settings
    refs = list(refs)
    take = lambda number: [refs.pop(0) for _ in range(number)]
    q_refs = take(len(query_sizes))
    mine_ref, other_ref, first_ref = take(3)
    state_refs = [take(2) for _ in query_sizes] if states else []
    out_refs = take(1 if finish else 2)
    q_all, max_ref, sum_ref, acc_ref = refs

    chip = order_ref[pl.program_id(0)]
    core = place_ref[1]
    groups, rows, _ = q_all.shape
    count = sum(query_sizes)
    together = rows // count
    per_device = PER_DEVICE
    half_tile = chips * key_size
    key_tile = CORES * half_tile
    block = CORES * chips * per_device
    last_block = mine_ref.shape[0] // half_tile - 1
    row_start = last_block * block + CORES * per_device * chip + per_device * core + offset
    scale = HEAD_WIDTH**-0.5 * math.log2(math.e)
    per_half = q_refs[0].shape[3] // HEAD_WIDTH
    lane = lax.broadcasted_iota(jnp.int32, (1, HEAD_WIDTH), 1)

    if not states:
        max_ref[...] = jnp.full(max_ref.shape, LOWEST_MAX, jnp.float32)
        sum_ref[...] = jnp.zeros(sum_ref.shape, jnp.float32)
        acc_ref[...] = jnp.zeros(acc_ref.shape, jnp.float32)
    for h in range(groups * together):
        group, inside = h // together, h % together
        start = (h % per_half) * HEAD_WIDTH
        at = inside * count
        for j, size in enumerate(query_sizes):
            to = slice(at, at + size)
            q_all[group, to, :] = q_refs[j][h // per_half, 0, :, start : start + HEAD_WIDTH]
            if states:
                packed = state_refs[j][1][0, h]
                acc_ref[group, to, :] = state_refs[j][0][0, h]
                max_ref[group, to, :] = jnp.broadcast_to(packed[:, :1], packed.shape)
                sum_ref[group, to, :] = jnp.where(lane == HEAD_WIDTH - 1, packed, 0.0)
            at += size

    def visit(key_block, masked):
        at = pl.ds(pl.multiple_of(key_block * half_tile, half_tile), half_tile)
        keys = jnp.concatenate([mine_ref[at, :HEAD_WIDTH], other_ref[at, :HEAD_WIDTH]], axis=0)
        values = jnp.concatenate([mine_ref[at, HEAD_WIDTH:], other_ref[at, HEAD_WIDTH:]], axis=0)
        if masked:
            column = lax.broadcasted_iota(jnp.int32, (1, key_tile), 1)
            side = column >= half_tile
            row = jnp.where(side, column - half_tile, column)
            key_pos = key_block * block + key_begin + row
            for k in range(1, chips):
                key_pos = key_pos + jnp.where(row >= k * key_size, CORES * per_device - key_size, 0)
            key_pos = key_pos + per_device * jnp.where(side, 1 - core, core)
            query_pos = row_start + lax.broadcasted_iota(jnp.int32, (count, key_tile), 0)
            seen = (key_pos >= first_ref[...]) & (key_pos <= query_pos)
            hide = jnp.where(seen, 0.0, HIDDEN_SCORE)
            hide = jnp.concatenate([hide] * together, axis=0)
        for group in range(groups):
            scores = lax.dot_general(
                q_all[group], keys, (((1,), (1,)), ((), ())), preferred_element_type=jnp.float32
            )
            if masked:
                scores = jnp.where(hide < 0.0, hide, scores)
            old_max = max_ref[group]
            new_max = jnp.maximum(old_max, jnp.max(scores, axis=1, keepdims=True))
            rescale = jnp.exp2((old_max - new_max) * scale)
            weights = jnp.exp2(scores * scale - new_max[:, :1] * scale)
            partial = weights[:, :HEAD_WIDTH]
            for g in range(1, key_tile // HEAD_WIDTH):
                partial = partial + weights[:, g * HEAD_WIDTH : (g + 1) * HEAD_WIDTH]
            max_ref[group] = new_max
            sum_ref[group] = sum_ref[group] * rescale + partial
            acc_ref[group] = acc_ref[group] * rescale + jnp.dot(
                weights.astype(jnp.bfloat16), values, preferred_element_type=jnp.float32
            )

    low, full_low, full_high, high = (bounds_ref[4 * chip + i] for i in range(4))
    pl.loop(low, full_low)(lambda k: visit(k, True))
    pl.loop(full_low, full_high)(lambda k: visit(k, False))
    pl.loop(full_high, high)(lambda k: visit(k, True))
    for group in range(groups):
        total = jnp.sum(sum_ref[group], axis=1, keepdims=True)
        if finish:
            result = (acc_ref[group] / total).astype(jnp.bfloat16)
        else:
            packed = jnp.where(lane == HEAD_WIDTH - 1, total, max_ref[group])
        for inside in range(together):
            h = group * together + inside
            of = slice(inside * count, (inside + 1) * count)
            if finish:
                out_refs[0][0, :, h * HEAD_WIDTH : (h + 1) * HEAD_WIDTH] = result[of, :]
            else:
                out_refs[0][0, h] = acc_ref[group, of, :]
                out_refs[1][0, h] = packed[of, :]


def attend(place, order, queries, window, first_key, offset, key_begin, states=None, finish=False):
    _, chips, _, wide = queries[0].shape
    sizes = [q.shape[2] for q in queries]
    count = sum(sizes)
    blocks, _, key_size, _ = window[0].shape
    heads = CORES * wide // HEAD_WIDTH
    together = max(t for t in (1, 2, 4, 8) if t * count <= 256 and heads % t == 0)
    block = CORES * chips * PER_DEVICE
    first_key = first_key[:, offset : offset + count]
    high = jnp.full((chips,), blocks, jnp.int32)
    low = jnp.minimum(first_key[:, 0] // block, high)
    full_low = jnp.clip((first_key[:, -1] + block - 1) // block, low, high)
    full_high = jnp.maximum(full_low, jnp.full((chips,), blocks - 1, jnp.int32))
    bounds = jnp.stack([low, full_low, full_high, high], axis=1).reshape(-1)
    flat = [w.reshape(-1, w.shape[3]) for w in window]
    state = pltpu.VMEM((heads // together, together * count, HEAD_WIDTH), jnp.float32)
    by_chip = lambda i, p, o, b: (o[i], 0, 0, 0)
    in_specs = [pl.BlockSpec((CORES, 1, size, wide), lambda i, p, o, b: (0, o[i], 0, 0)) for size in sizes]
    in_specs += [pl.BlockSpec(f.shape, lambda i, p, o, b: (0, 0)) for f in flat]
    in_specs += [pl.BlockSpec((count, 1), lambda i, p, o, b: (o[i], 0))]
    operands = [*queries, *flat, first_key.reshape(-1, 1)]
    if states is not None:
        for size, pair in zip(sizes, states):
            in_specs += [pl.BlockSpec((1, heads, size, HEAD_WIDTH), by_chip)] * 2
            operands += pair
    steps = order.shape[0]
    if finish:
        out_specs = [pl.BlockSpec((1, count, CORES * wide), lambda i, p, o, b: (i, 0, 0))]
        out_shape = [jax.ShapeDtypeStruct((steps, count, CORES * wide), jnp.bfloat16)]
    else:
        out_specs = [pl.BlockSpec((1, heads, count, HEAD_WIDTH), by_chip)] * 2
        out_shape = [jax.ShapeDtypeStruct((chips, heads, count, HEAD_WIDTH), jnp.float32)] * 2
    settings = (sizes, offset, key_size, key_begin, chips, states is not None, finish)
    return pl.pallas_call(
        functools.partial(attention_kernel, settings),
        grid_spec=pltpu.PrefetchScalarGridSpec(
            num_scalar_prefetch=3,
            grid=(steps,),
            in_specs=in_specs,
            out_specs=out_specs,
            scratch_shapes=[
                pltpu.VMEM((heads // together, together * count, HEAD_WIDTH), jnp.bfloat16),
                state,
                state,
                state,
            ],
        ),
        out_shape=out_shape,
        compiler_params=pltpu.CompilerParams(vmem_limit_bytes=VMEM_BYTES),
        cost_estimate=SMALL_COST,
    )(place, order, bounds, *operands)


def local(hidden, gain, basis, w_query, key_matrix, value_matrix, doc_ids):
    ctx_count, tp_count = lax.axis_size("ctx"), lax.axis_size("tp")
    ctx_rank, tp_rank = lax.axis_index("ctx"), lax.axis_index("tp")
    chips = tp_count // CORES
    chip, core = tp_rank // CORES, tp_rank % CORES
    place = jnp.stack([chip, core]).astype(jnp.int32)
    count = hidden.shape[0]
    block_len = count * tp_count

    def along(value, step):
        moves = [(t, ((t // CORES + step) % chips) * CORES + t % CORES) for t in range(tp_count)]
        return lax.ppermute(value, "tp", moves)

    def swapped(value):
        return lax.ppermute(value, "tp", [(t, t ^ 1) for t in range(tp_count)])

    def after(value, *others):
        return lax.optimization_barrier((value, *others))[0]

    basis_other = swapped(basis)
    kv_weights = jnp.concatenate(
        [
            lax.dynamic_slice_in_dim(matrix, chip * HEAD_WIDTH, HEAD_WIDTH, 1)
            for matrix in (key_matrix, value_matrix)
        ],
        axis=1,
    )

    first_token = ctx_rank * block_len
    row_pos = (
        first_token
        + CORES * count * jnp.arange(chips, dtype=jnp.int32)[:, None]
        + count * core
        + jnp.arange(count, dtype=jnp.int32)[None, :]
    )
    cosine, sine = rotary_tables(row_pos.reshape(-1).astype(jnp.float32))
    cosine = cosine.reshape(chips, count, HEAD_WIDTH)
    sine = sine.reshape(chips, count, HEAD_WIDTH)
    blocks_before = min(-(-(LONGEST_DOC - 1) // block_len), ctx_count - 1)

    def normed_rows(start, size):
        values = hidden[start : start + size].astype(jnp.float32)
        meansq = jnp.mean(values * values, axis=-1, keepdims=True)
        return (values * lax.rsqrt(meansq + 1e-05) * gain.astype(jnp.float32)).astype(jnp.bfloat16)

    begins = [sum(CHUNKS[:k]) for k in range(len(CHUNKS))]
    normed = [normed_rows(begin, size) for begin, size in zip(begins, CHUNKS)]

    def gather(first, second):
        first_right, second_left = along(first, 1), along(second, -1)
        second_right, first_left = along(second, 1), along(first, -1)
        first_far, second_far = along(first_right, 1), along(second_left, -1)
        return [
            (first, first_right, first_left, first_far),
            (second, second_right, second_left, second_far),
        ]

    gathered = gather(*normed)

    ids, cosine, sine, kv_weights = lax.optimization_barrier(
        (doc_ids, cosine, sine, kv_weights, gathered[0][1], gathered[1][2], basis_other)
    )[:4]
    smaller = jnp.sum(
        (ids[None, :] < jnp.arange(DOCS, dtype=jnp.int32)[:, None]).astype(jnp.int32), axis=1
    )
    doc_starts = lax.psum(smaller, ("ctx", "tp"))
    gathered[0] = (after(gathered[0][0], doc_starts, *gathered[1]),) + gathered[0][1:]
    columns = [project(place, group, basis, basis_other, chips) for group in gathered]
    pieces = gather(*[c.reshape(-1, c.shape[2]) for c in columns])

    doc_first = jnp.max(
        jnp.where(doc_starts[:, None, None] <= row_pos[None], doc_starts[:, None, None], 0), axis=0
    )
    first_key = doc_first - first_token + blocks_before * block_len

    query_other = swapped(after(w_query, columns[0]))
    queries, windows, states = [], [], []
    everyone = jnp.arange(chips, dtype=jnp.int32)
    for k, size in enumerate(CHUNKS):
        begin = begins[k]
        chunk = pieces[k]
        if k + 1 < len(CHUNKS):
            chunk = (after(chunk[0], columns[k + 1]),) + chunk[1:]
        else:
            chunk = (after(chunk[0], *states[0]),) + chunk[1:]
        chunk_q, chunk_kv = project_heads(
            place,
            chunk,
            w_query,
            query_other,
            kv_weights,
            cosine[:, begin : begin + size].reshape(chips * size, HEAD_WIDTH),
            sine[:, begin : begin + size].reshape(chips * size, HEAD_WIDTH),
        )
        queries.append(chunk_q.reshape(CORES, chips, size, -1))
        blocks = [
            lax.ppermute(chunk_kv, "ctx", [(i, i + s) for i in range(ctx_count - s)])
            for s in range(blocks_before, 0, -1)
        ] + [chunk_kv]
        if k > 0:
            states.append(attend(place, everyone, [queries[k]], windows[0], first_key, begin, begins[0]))
            blocks = [after(received, *states[k]) for received in blocks[:-1]] + blocks[-1:]
        mine = jnp.stack(blocks)
        other = swapped(mine)
        windows.append([w.reshape(-1, chips, size, 2 * HEAD_WIDTH) for w in (mine, other)])
        if k == 0:
            q = after(queries[0], pieces[1][1], pieces[1][2])
            states.append(attend(place, everyone, [q], windows[0], first_key, begin, begins[0]))

    def finished(aways):
        order = (chip + jnp.array(aways, jnp.int32)) % chips
        return attend(place, order, queries, windows[1], first_key, 0, begins[1], states, True)[0]

    first_two, last_two = finished((2, 1)), finished((3, 0))
    received = jnp.stack(
        [last_two[1], along(first_two[1], 1), along(first_two[0], 2), along(last_two[0], 3)]
    )
    return jnp.concatenate(
        [
            lax.dynamic_index_in_dim(received, (chip - g) % chips, 0, keepdims=False)
            for g in range(chips)
        ],
        axis=1,
    )


def solution(mesh):
    in_specs = (
        P(("dp", "ctx", "tp"), None),
        P(),
        P(None, "tp"),
        P(None, "tp"),
        P(),
        P(),
        P(("dp", "ctx", "tp")),
    )
    out_specs = P(("dp", "ctx", "tp"), None)
    return jax.shard_map(local, mesh=mesh, in_specs=in_specs, out_specs=out_specs, check_vma=False)
```

```python
import functools
import math

import jax
import jax.numpy as jnp
from jax import lax
from jax.experimental import pallas as pl
from jax.experimental.pallas import tpu as pltpu
from jax.sharding import PartitionSpec as P

HEAD_WIDTH = 128
DOCS = 8
LONGEST_DOC = 4096
CORES = 2
CHUNKS = (64, 64)
HIDDEN_SCORE = -1e30
LOWEST_MAX = -0.5e30
VMEM_BYTES = 16 * 1024 * 1024
ATTENTION_VMEM_BYTES = 28 * 1024 * 1024
COLUMN_TILE = 256
PER_DEVICE = sum(CHUNKS)
SMALL_COST = pl.CostEstimate(flops=1, bytes_accessed=1, transcendentals=0)


def rotary_tables(positions):
    half_width = HEAD_WIDTH // 2
    frequency = 500000.0 ** (-jnp.arange(half_width, dtype=jnp.float32) * 2.0 / HEAD_WIDTH)
    angles = positions[:, None] * frequency
    cosine = jnp.cos(angles)
    sine = jnp.sin(angles)
    return (
        jnp.concatenate([cosine, cosine], axis=-1),
        jnp.concatenate([-sine, sine], axis=-1),
    )


def ring_order(place_ref, chips):
    chip = place_ref[0]
    return [lax.rem(chip + away, chips) for away in (0, chips - 1, 1, 2)]


def project_kernel(
    place_ref, own_ref, right_ref, left_ref, far_ref, mine_ref, other_ref, o_ref
):
    chips, count, columns = o_ref.shape
    rows = jnp.concatenate([own_ref[...], right_ref[...], left_ref[...], far_ref[...]], axis=0)
    order = ring_order(place_ref, chips)
    wide = columns // CORES
    for side, w_ref in enumerate((mine_ref, other_ref)):
        for n in range(0, wide, COLUMN_TILE):
            result = jnp.dot(
                rows, w_ref[:, n : n + COLUMN_TILE], preferred_element_type=jnp.float32
            ).astype(jnp.bfloat16)
            at = side * wide + n
            for slot, chip in enumerate(order):
                o_ref[chip, :, at : at + COLUMN_TILE] = result[slot * count : (slot + 1) * count, :]


def project(place, pieces, mine, other, chips):
    count, depth = pieces[0].shape
    wide = mine.shape[1]
    vmem = pl.BlockSpec(memory_space=pltpu.VMEM)
    return pl.pallas_call(
        project_kernel,
        in_specs=[pl.BlockSpec(memory_space=pltpu.SMEM)] + [vmem] * 6,
        out_specs=vmem,
        out_shape=jax.ShapeDtypeStruct((chips, count, CORES * wide), jnp.bfloat16),
        compiler_params=pltpu.CompilerParams(vmem_limit_bytes=VMEM_BYTES),
        cost_estimate=SMALL_COST,
    )(place, *pieces, mine, other)


def heads_kernel(
    place_ref,
    own_ref,
    right_ref,
    left_ref,
    far_ref,
    mine_ref,
    other_ref,
    kv_weights_ref,
    cos_ref,
    sin_ref,
    q_ref,
    kv_ref,
):
    parts, depth, wide = mine_ref.shape
    core = place_ref[1]
    order = ring_order(place_ref, parts // CORES)
    pieces = [own_ref[...], right_ref[...], left_ref[...], far_ref[...]]
    cosine, sine = cos_ref[...], sin_ref[...]

    def rotated(u):
        return (u * cosine + pltpu.roll(u, HEAD_WIDTH // 2, 1) * sine).astype(jnp.bfloat16)

    def product(w_ref, n):
        total = None
        for chip, piece in zip(order, pieces):
            for side, which in ((0, core), (1, 1 - core)):
                term = jnp.dot(
                    piece[:, side * depth : (side + 1) * depth],
                    w_ref[CORES * chip + which, :, n : n + 2 * HEAD_WIDTH],
                    preferred_element_type=jnp.float32,
                )
                total = term if total is None else total + term
        return total

    both = product(kv_weights_ref, 0)
    kv_ref[:, :HEAD_WIDTH] = rotated(both[:, :HEAD_WIDTH])
    kv_ref[:, HEAD_WIDTH:] = both[:, HEAD_WIDTH:].astype(jnp.bfloat16)
    for w_ref, at in ((mine_ref, core), (other_ref, 1 - core)):
        for n in range(0, wide, 2 * HEAD_WIDTH):
            both = product(w_ref, n)
            q_ref[at, :, n : n + HEAD_WIDTH] = rotated(both[:, :HEAD_WIDTH])
            q_ref[at, :, n + HEAD_WIDTH : n + 2 * HEAD_WIDTH] = rotated(both[:, HEAD_WIDTH:])


def project_heads(place, pieces, mine, other, kv_weights, cosine, sine):
    rows, wide_in = pieces[0].shape
    depth = wide_in // CORES
    wide = mine.shape[1]
    vmem = pl.BlockSpec(memory_space=pltpu.VMEM)
    by_part = [w.reshape(-1, depth, w.shape[1]) for w in (mine, other, kv_weights)]
    return pl.pallas_call(
        heads_kernel,
        in_specs=[pl.BlockSpec(memory_space=pltpu.SMEM)] + [vmem] * 9,
        out_specs=[vmem, vmem],
        out_shape=[
            jax.ShapeDtypeStruct((CORES, rows, wide), jnp.bfloat16),
            jax.ShapeDtypeStruct((rows, 2 * HEAD_WIDTH), jnp.bfloat16),
        ],
        compiler_params=pltpu.CompilerParams(vmem_limit_bytes=VMEM_BYTES),
        cost_estimate=SMALL_COST,
    )(place, *pieces, *by_part, cosine, sine)


def attention_kernel(settings, place_ref, bounds_ref, *refs):
    key_begin, states, finish = settings
    refs = list(refs)
    take = lambda number: [refs.pop(0) for _ in range(number)]
    q_refs = take(len(CHUNKS))
    mine_ref, other_ref, first_ref = take(3)
    state_refs = take(3) if states else []
    out_refs = take(1 if finish else 3)
    q_all = refs.pop(0)
    max_ref, sum_ref, acc_ref = take(3) if finish else out_refs

    core = place_ref[1]
    groups, rows, _ = q_all.shape
    _, chips, key_size, wide = q_refs[0].shape
    per_chip = groups // chips
    together = rows // PER_DEVICE
    block_rows = chips * key_size
    block = CORES * chips * PER_DEVICE
    before = mine_ref.shape[0] // block_rows - 1
    scale = HEAD_WIDTH**-0.5 * math.log2(math.e)

    if states:
        for ref, state_ref in zip((max_ref, sum_ref, acc_ref), state_refs):
            ref[...] = state_ref[...]
    else:
        max_ref[...] = jnp.full(max_ref.shape, LOWEST_MAX, jnp.float32)
        sum_ref[...] = jnp.zeros(sum_ref.shape, jnp.float32)
        acc_ref[...] = jnp.zeros(acc_ref.shape, jnp.float32)
    for chip in range(chips):
        for h in range(per_chip * together):
            at = (h % together) * PER_DEVICE
            side, start = divmod(h * HEAD_WIDTH, wide)
            for q_ref in q_refs:
                size = q_ref.shape[2]
                q_all[chip * per_chip + h // together, at : at + size, :] = q_ref[
                    side, chip, :, start : start + HEAD_WIDTH
                ]
                at += size

    def rows_of(start, number):
        at = pl.ds(start, number)
        keys = jnp.concatenate([mine_ref[at, :HEAD_WIDTH], other_ref[at, :HEAD_WIDTH]], axis=0)
        values = jnp.concatenate([mine_ref[at, HEAD_WIDTH:], other_ref[at, HEAD_WIDTH:]], axis=0)
        return keys, values

    def hidden_scores(chip, start, number, diagonal):
        column = lax.broadcasted_iota(jnp.int32, (1, CORES * number), 1)
        side = column >= number
        row = jnp.where(side, column - number, column)
        inside = lax.rem(row, key_size)
        stretch = CORES * PER_DEVICE // key_size
        key_pos = stretch * (start + row - inside) + inside + key_begin
        key_pos = key_pos + PER_DEVICE * jnp.where(side, 1 - core, core)
        seen = key_pos >= first_ref[chip * PER_DEVICE : (chip + 1) * PER_DEVICE, :]
        if diagonal:
            query_pos = before * block + CORES * PER_DEVICE * chip + PER_DEVICE * core
            query_pos = query_pos + lax.broadcasted_iota(jnp.int32, (PER_DEVICE, 1), 0)
            seen = seen & (key_pos <= query_pos)
        hide = jnp.where(seen, 0.0, HIDDEN_SCORE)
        return jnp.concatenate([hide] * together, axis=0)

    def scores_of(job):
        group, keys, _, hide = job
        scores = lax.dot_general(
            q_all[group], keys, (((1,), (1,)), ((), ())), preferred_element_type=jnp.float32
        )
        return scores if hide is None else scores + hide

    def weigh(job, scores):
        group = job[0]
        old_max = max_ref[group]
        new_max = jnp.maximum(old_max, jnp.max(scores, axis=1, keepdims=True))
        rescale = jnp.exp2((old_max - new_max) * scale)
        weights = jnp.exp2(scores * scale - new_max[:, :1] * scale)
        partial = weights[:, :HEAD_WIDTH]
        for g in range(1, weights.shape[1] // HEAD_WIDTH):
            partial = partial + weights[:, g * HEAD_WIDTH : (g + 1) * HEAD_WIDTH]
        max_ref[group] = new_max
        sum_ref[group] = sum_ref[group] * rescale + partial
        return weights.astype(jnp.bfloat16), rescale

    def collect(job, weights, rescale):
        group, _, values, _ = job
        acc_ref[group] = acc_ref[group] * rescale + jnp.dot(
            weights, values, preferred_element_type=jnp.float32
        )

    def run(jobs):
        scores, last = scores_of(jobs[0]), None
        for i, job in enumerate(jobs):
            following = scores_of(jobs[i + 1]) if i + 1 < len(jobs) else None
            weighed = weigh(job, scores)
            if last is not None:
                collect(*last)
            last, scores = (job, *weighed), following
        collect(*last)

    def visit(pair, masked):
        start = pl.multiple_of(pair * 2 * block_rows, 2 * block_rows)
        keys, values = rows_of(start, 2 * block_rows)
        jobs = []
        for chip in range(chips):
            hide = hidden_scores(chip, start, 2 * block_rows, False) if masked else None
            jobs += [(chip * per_chip + g, keys, values, hide) for g in range(per_chip)]
        run(jobs)

    low, full, pairs = bounds_ref[0], bounds_ref[1], before // 2
    pl.loop(low, full)(lambda pair: visit(pair, True))
    pl.loop(full, pairs)(lambda pair: visit(pair, False))
    jobs = []
    for chip in range(chips):
        start = 2 * pairs * block_rows
        number = (before - 2 * pairs) * block_rows + (chip + 1) * key_size
        keys, values = rows_of(start, number)
        hide = hidden_scores(chip, start, number, True)
        jobs += [(chip * per_chip + g, keys, values, hide) for g in range(per_chip)]
    run(jobs)

    if finish:
        for chip in range(chips):
            for h in range(per_chip * together):
                group, at = chip * per_chip + h // together, (h % together) * PER_DEVICE
                of = slice(at, at + PER_DEVICE)
                total = jnp.sum(sum_ref[group, of, :], axis=1, keepdims=True)
                out_refs[0][chip, :, h * HEAD_WIDTH : (h + 1) * HEAD_WIDTH] = (
                    acc_ref[group, of, :] / total
                ).astype(jnp.bfloat16)


def attend(place, queries, mine, other, first_key, key_begin, states, finish):
    _, chips, key_size, wide = queries[0].shape
    heads = CORES * wide // HEAD_WIDTH
    together = max(t for t in (1, 2, 4, 8) if t * PER_DEVICE <= 256 and heads % t == 0)
    block = CORES * chips * PER_DEVICE
    pairs = (mine.shape[0] // (chips * key_size) - 1) // 2
    low = jnp.minimum(first_key[0, 0] // (2 * block), pairs)
    full = jnp.clip((first_key[-1, -1] + 2 * block - 1) // (2 * block), low, pairs)
    bounds = jnp.stack([low, full]).astype(jnp.int32)
    state = (chips * heads // together, together * PER_DEVICE, HEAD_WIDTH)
    vmem, smem = pl.BlockSpec(memory_space=pltpu.VMEM), pl.BlockSpec(memory_space=pltpu.SMEM)
    operands = [*queries, mine, other, first_key.reshape(-1, 1), *states]
    if finish:
        out_shape = [jax.ShapeDtypeStruct((chips, PER_DEVICE, CORES * wide), jnp.bfloat16)]
    else:
        out_shape = [jax.ShapeDtypeStruct(state, jnp.float32)] * 3
    return pl.pallas_call(
        functools.partial(attention_kernel, (key_begin, len(states) > 0, finish)),
        in_specs=[smem, smem] + [vmem] * len(operands),
        out_specs=[vmem] * len(out_shape),
        scratch_shapes=[pltpu.VMEM(state, jnp.bfloat16)]
        + ([pltpu.VMEM(state, jnp.float32)] * 3 if finish else []),
        out_shape=out_shape,
        compiler_params=pltpu.CompilerParams(vmem_limit_bytes=ATTENTION_VMEM_BYTES),
        cost_estimate=SMALL_COST,
    )(place, bounds, *operands)


def local(hidden, gain, basis, w_query, key_matrix, value_matrix, doc_ids):
    ctx_count, tp_count = lax.axis_size("ctx"), lax.axis_size("tp")
    ctx_rank, tp_rank = lax.axis_index("ctx"), lax.axis_index("tp")
    chips = tp_count // CORES
    chip, core = tp_rank // CORES, tp_rank % CORES
    place = jnp.stack([chip, core]).astype(jnp.int32)
    count = hidden.shape[0]
    block_len = count * tp_count

    def along(value, step):
        moves = [(t, ((t // CORES + step) % chips) * CORES + t % CORES) for t in range(tp_count)]
        return lax.ppermute(value, "tp", moves)

    def swapped(value):
        return lax.ppermute(value, "tp", [(t, t ^ 1) for t in range(tp_count)])

    def after(value, *others):
        return lax.optimization_barrier((value, *others))[0]

    basis_other = swapped(basis)
    kv_weights = jnp.concatenate(
        [
            lax.dynamic_slice_in_dim(matrix, chip * HEAD_WIDTH, HEAD_WIDTH, 1)
            for matrix in (key_matrix, value_matrix)
        ],
        axis=1,
    )

    first_token = ctx_rank * block_len
    row_pos = (
        first_token
        + CORES * count * jnp.arange(chips, dtype=jnp.int32)[:, None]
        + count * core
        + jnp.arange(count, dtype=jnp.int32)[None, :]
    )
    cosine, sine = rotary_tables(row_pos.reshape(-1).astype(jnp.float32))
    cosine = cosine.reshape(chips, count, HEAD_WIDTH)
    sine = sine.reshape(chips, count, HEAD_WIDTH)
    blocks_before = min(-(-(LONGEST_DOC - 1) // block_len), ctx_count - 1)

    def normed_rows(start, size):
        values = hidden[start : start + size].astype(jnp.float32)
        meansq = jnp.mean(values * values, axis=-1, keepdims=True)
        return (values * lax.rsqrt(meansq + 1e-05) * gain.astype(jnp.float32)).astype(jnp.bfloat16)

    begins = [sum(CHUNKS[:k]) for k in range(len(CHUNKS))]
    normed = [normed_rows(begin, size) for begin, size in zip(begins, CHUNKS)]

    def gather(first, second):
        first_right, second_left = along(first, 1), along(second, -1)
        second_right, first_left = along(second, 1), along(first, -1)
        first_far, second_far = along(first_right, 1), along(second_left, -1)
        return [
            (first, first_right, first_left, first_far),
            (second, second_right, second_left, second_far),
        ]

    gathered = gather(*normed)

    ids, cosine, sine, kv_weights = lax.optimization_barrier(
        (doc_ids, cosine, sine, kv_weights, gathered[0][1], gathered[1][2], basis_other)
    )[:4]
    smaller = (ids[None, :] < jnp.arange(DOCS, dtype=jnp.int32)[:, None]).astype(jnp.int32)
    doc_starts = jnp.sum(smaller, axis=1)
    for axis, length in (("ctx", ctx_count), ("tp", tp_count)):
        step = 1
        while step < length:
            doc_starts += lax.ppermute(doc_starts, axis, [(i, i ^ step) for i in range(length)])
            step *= 2
    gathered[0] = (after(gathered[0][0], doc_starts, *gathered[1]),) + gathered[0][1:]
    columns = [project(place, group, basis, basis_other, chips) for group in gathered]
    pieces = gather(*[c.reshape(-1, c.shape[2]) for c in columns])

    doc_first = jnp.max(
        jnp.where(doc_starts[:, None, None] <= row_pos[None], doc_starts[:, None, None], 0), axis=0
    )
    first_key = doc_first - first_token + blocks_before * block_len

    query_other = swapped(after(w_query, columns[0]))
    queries, windows, states = [], [], []
    for k, size in enumerate(CHUNKS):
        begin = begins[k]
        chunk = pieces[k]
        if k + 1 < len(CHUNKS):
            chunk = (after(chunk[0], columns[k + 1]),) + chunk[1:]
        chunk_q, chunk_kv = project_heads(
            place,
            chunk,
            w_query,
            query_other,
            kv_weights,
            cosine[:, begin : begin + size].reshape(chips * size, HEAD_WIDTH),
            sine[:, begin : begin + size].reshape(chips * size, HEAD_WIDTH),
        )
        queries.append(chunk_q.reshape(CORES, chips, size, -1))
        blocks = [
            lax.ppermute(chunk_kv, "ctx", [(i, i + s) for i in range(ctx_count - s)])
            for s in range(blocks_before, 0, -1)
        ] + [chunk_kv]
        if k > 0:
            states = attend(place, queries, *windows[0], first_key, begins[0], [], False)
            blocks = [after(received, *states) for received in blocks[:-1]] + blocks[-1:]
        mine = jnp.concatenate(blocks, axis=0)
        windows.append((mine, swapped(mine)))

    attended = attend(place, queries, *windows[1], first_key, begins[1], states, True)[0]

    def rows_for(away):
        return lax.dynamic_index_in_dim(attended, (chip + away) % chips, 0, keepdims=False)

    received = jnp.stack([rows_for(0)] + [along(rows_for(away), away) for away in range(1, chips)])
    return jnp.concatenate(
        [
            lax.dynamic_index_in_dim(received, (chip - g) % chips, 0, keepdims=False)
            for g in range(chips)
        ],
        axis=1,
    )


def solution(mesh):
    in_specs = (
        P(("dp", "ctx", "tp"), None),
        P(),
        P(None, "tp"),
        P(None, "tp"),
        P(),
        P(),
        P(("dp", "ctx", "tp")),
    )
    out_specs = P(("dp", "ctx", "tp"), None)
    return jax.shard_map(local, mesh=mesh, in_specs=in_specs, out_specs=out_specs, check_vma=False)
```

```python
import functools
import math

import jax
import jax.numpy as jnp
from jax import lax
from jax.experimental import pallas as pl
from jax.experimental.pallas import tpu as pltpu
from jax.sharding import PartitionSpec as P

HEAD_WIDTH = 128
DOCS = 8
LONGEST_DOC = 4096
CORES = 2
CHUNKS = (64, 64)
HIDDEN_SCORE = -1e30
LOWEST_MAX = -0.5e30
VMEM_BYTES = 24 * 1024 * 1024
COLUMN_TILE = 256
PER_DEVICE = sum(CHUNKS)
SMALL_COST = pl.CostEstimate(flops=1, bytes_accessed=1, transcendentals=0)


def rotary_tables(positions):
    half_width = HEAD_WIDTH // 2
    frequency = 500000.0 ** (-jnp.arange(half_width, dtype=jnp.float32) * 2.0 / HEAD_WIDTH)
    angles = positions[:, None] * frequency
    cosine = jnp.cos(angles)
    sine = jnp.sin(angles)
    return (
        jnp.concatenate([cosine, cosine], axis=-1),
        jnp.concatenate([-sine, sine], axis=-1),
    )


def ring_order(place_ref, chips):
    chip = place_ref[0]
    return [lax.rem(chip + away, chips) for away in (0, chips - 1, 1, 2)]


def project_kernel(
    place_ref, own_ref, right_ref, left_ref, far_ref, mine_ref, other_ref, o_ref, held_ref, sem
):
    chips, count, columns = o_ref.shape
    copy = pltpu.make_async_copy(other_ref, held_ref, sem)
    copy.start()
    rows = jnp.concatenate([own_ref[...], right_ref[...], left_ref[...], far_ref[...]], axis=0)
    order = ring_order(place_ref, chips)
    wide = columns // CORES
    for side, w_ref in enumerate((mine_ref, held_ref)):
        if side == 1:
            copy.wait()
        for n in range(0, wide, COLUMN_TILE):
            result = jnp.dot(
                rows, w_ref[:, n : n + COLUMN_TILE], preferred_element_type=jnp.float32
            ).astype(jnp.bfloat16)
            at = side * wide + n
            for slot, chip in enumerate(order):
                o_ref[chip, :, at : at + COLUMN_TILE] = result[slot * count : (slot + 1) * count, :]


def project(place, pieces, mine, other, chips):
    count, depth = pieces[0].shape
    wide = mine.shape[1]
    vmem = pl.BlockSpec(memory_space=pltpu.VMEM)
    return pl.pallas_call(
        project_kernel,
        in_specs=[pl.BlockSpec(memory_space=pltpu.SMEM)]
        + [vmem] * 5
        + [pl.BlockSpec(memory_space=pl.ANY)],
        out_specs=vmem,
        out_shape=jax.ShapeDtypeStruct((chips, count, CORES * wide), jnp.bfloat16),
        scratch_shapes=[pltpu.VMEM(other.shape, other.dtype), pltpu.SemaphoreType.DMA],
        compiler_params=pltpu.CompilerParams(vmem_limit_bytes=VMEM_BYTES),
        cost_estimate=SMALL_COST,
    )(place, *pieces, mine, other)


def pack_kernel(*refs):
    at = 0
    for ref in refs[:-1]:
        refs[-1][at : at + ref.shape[0], :] = ref[...]
        at += ref.shape[0]


def pack(blocks):
    vmem = pl.BlockSpec(memory_space=pltpu.VMEM)
    rows = sum(block.shape[0] for block in blocks)
    return pl.pallas_call(
        pack_kernel,
        in_specs=[vmem] * len(blocks),
        out_specs=vmem,
        out_shape=jax.ShapeDtypeStruct((rows, blocks[0].shape[1]), blocks[0].dtype),
        cost_estimate=SMALL_COST,
    )(*blocks)


def heads_kernel(
    place_ref,
    own_ref,
    right_ref,
    left_ref,
    far_ref,
    mine_ref,
    other_ref,
    kv_weights_ref,
    cos_ref,
    sin_ref,
    q_ref,
    kv_ref,
):
    parts, depth, wide = mine_ref.shape
    core = place_ref[1]
    order = ring_order(place_ref, parts // CORES)
    pieces = [own_ref[...], right_ref[...], left_ref[...], far_ref[...]]
    cosine, sine = cos_ref[...], sin_ref[...]

    def rotated(u):
        return (u * cosine + pltpu.roll(u, HEAD_WIDTH // 2, 1) * sine).astype(jnp.bfloat16)

    def product(w_ref, n):
        total = None
        for chip, piece in zip(order, pieces):
            for side, which in ((0, core), (1, 1 - core)):
                term = jnp.dot(
                    piece[:, side * depth : (side + 1) * depth],
                    w_ref[CORES * chip + which, :, n : n + 2 * HEAD_WIDTH],
                    preferred_element_type=jnp.float32,
                )
                total = term if total is None else total + term
        return total

    both = product(kv_weights_ref, 0)
    kv_ref[:, :HEAD_WIDTH] = rotated(both[:, :HEAD_WIDTH])
    kv_ref[:, HEAD_WIDTH:] = both[:, HEAD_WIDTH:].astype(jnp.bfloat16)
    for w_ref, at in ((mine_ref, core), (other_ref, 1 - core)):
        for n in range(0, wide, 2 * HEAD_WIDTH):
            both = product(w_ref, n)
            q_ref[at, :, n : n + HEAD_WIDTH] = rotated(both[:, :HEAD_WIDTH])
            q_ref[at, :, n + HEAD_WIDTH : n + 2 * HEAD_WIDTH] = rotated(both[:, HEAD_WIDTH:])


def project_heads(place, pieces, mine, other, kv_weights, cosine, sine):
    rows, wide_in = pieces[0].shape
    depth = wide_in // CORES
    wide = mine.shape[1]
    vmem = pl.BlockSpec(memory_space=pltpu.VMEM)
    by_part = [w.reshape(-1, depth, w.shape[1]) for w in (mine, other, kv_weights)]
    return pl.pallas_call(
        heads_kernel,
        in_specs=[pl.BlockSpec(memory_space=pltpu.SMEM)] + [vmem] * 9,
        out_specs=[vmem, vmem],
        out_shape=[
            jax.ShapeDtypeStruct((CORES, rows, wide), jnp.bfloat16),
            jax.ShapeDtypeStruct((rows, 2 * HEAD_WIDTH), jnp.bfloat16),
        ],
        compiler_params=pltpu.CompilerParams(vmem_limit_bytes=VMEM_BYTES),
        cost_estimate=SMALL_COST,
    )(place, *pieces, *by_part, cosine, sine)


def attention_kernel(settings, place_ref, order_ref, bounds_ref, *refs):
    key_begin, states, finish = settings
    refs = list(refs)
    take = lambda number: [refs.pop(0) for _ in range(number)]
    q_refs = take(len(CHUNKS))
    mine_ref, other_ref, first_ref = take(3)
    state_refs = take(2) if states else []
    out_refs = take(1 if finish else 2)
    q_all, max_ref, sum_ref, acc_ref = refs

    core = place_ref[1]
    groups, rows, _ = q_all.shape
    _, chips, key_size, wide = q_refs[0].shape
    together = rows // PER_DEVICE
    block_rows = chips * key_size
    block = CORES * chips * PER_DEVICE
    before = mine_ref.shape[0] // block_rows - 1
    pairs = before // 2
    scale = HEAD_WIDTH**-0.5 * math.log2(math.e)
    lane = lax.broadcasted_iota(jnp.int32, (1, HEAD_WIDTH), 1)

    def rows_of(start, number):
        at = pl.ds(start, number)
        keys = jnp.concatenate([mine_ref[at, :HEAD_WIDTH], other_ref[at, :HEAD_WIDTH]], axis=0)
        values = jnp.concatenate([mine_ref[at, HEAD_WIDTH:], other_ref[at, HEAD_WIDTH:]], axis=0)
        return keys, values

    def hidden_scores(chip, start, number, diagonal):
        column = lax.broadcasted_iota(jnp.int32, (1, CORES * number), 1)
        side = column >= number
        row = jnp.where(side, column - number, column)
        inside = lax.rem(row, key_size)
        stretch = CORES * PER_DEVICE // key_size
        key_pos = stretch * (start + row - inside) + inside + key_begin
        key_pos = key_pos + PER_DEVICE * jnp.where(side, 1 - core, core)
        at = pl.ds(pl.multiple_of(chip * PER_DEVICE, PER_DEVICE), PER_DEVICE)
        seen = key_pos >= first_ref[at, :]
        if diagonal:
            query_pos = before * block + CORES * PER_DEVICE * chip + PER_DEVICE * core
            query_pos = query_pos + lax.broadcasted_iota(jnp.int32, (PER_DEVICE, 1), 0)
            seen = seen & (key_pos <= query_pos)
        hide = jnp.where(seen, 0.0, HIDDEN_SCORE)
        return jnp.concatenate([hide] * together, axis=0)

    def run(keys, values, hide):
        def scores_of(group):
            scores = lax.dot_general(
                q_all[group], keys, (((1,), (1,)), ((), ())), preferred_element_type=jnp.float32
            )
            return scores if hide is None else scores + hide

        def weigh(group, scores):
            old_max = max_ref[group]
            new_max = jnp.maximum(old_max, jnp.max(scores, axis=1, keepdims=True))
            rescale = jnp.exp2((old_max - new_max) * scale)
            weights = jnp.exp2(scores * scale - new_max[:, :1] * scale)
            partial = weights[:, :HEAD_WIDTH]
            for g in range(1, weights.shape[1] // HEAD_WIDTH):
                partial = partial + weights[:, g * HEAD_WIDTH : (g + 1) * HEAD_WIDTH]
            max_ref[group] = new_max
            sum_ref[group] = sum_ref[group] * rescale + partial
            return weights.astype(jnp.bfloat16), rescale

        def collect(group, weights, rescale):
            acc_ref[group] = acc_ref[group] * rescale + jnp.dot(
                weights, values, preferred_element_type=jnp.float32
            )

        scores, last = scores_of(0), None
        for group in range(groups):
            following = scores_of(group + 1) if group + 1 < groups else None
            weighed = weigh(group, scores)
            if last is not None:
                collect(*last)
            last, scores = (group, *weighed), following
        collect(*last)

    def serve(step):
        chip = order_ref[step]
        for h in range(groups * together):
            at = (h % together) * PER_DEVICE
            side, start = divmod(h * HEAD_WIDTH, wide)
            for q_ref in q_refs:
                size = q_ref.shape[2]
                q_all[h // together, at : at + size, :] = q_ref[
                    side, chip, :, start : start + HEAD_WIDTH
                ]
                at += size
        if states:
            acc_ref[...] = state_refs[0][chip]
            packed = state_refs[1][chip]
            max_ref[...] = jnp.broadcast_to(packed[:, :, :1], packed.shape)
            sum_ref[...] = jnp.where(lane == HEAD_WIDTH - 1, packed, 0.0)
        else:
            max_ref[...] = jnp.full(max_ref.shape, LOWEST_MAX, jnp.float32)
            sum_ref[...] = jnp.zeros(sum_ref.shape, jnp.float32)
            acc_ref[...] = jnp.zeros(acc_ref.shape, jnp.float32)

        def visit(pair, masked):
            start = pl.multiple_of(pair * 2 * block_rows, 2 * block_rows)
            number = 2 * block_rows
            run(*rows_of(start, number), hidden_scores(chip, start, number, False) if masked else None)

        low, full = bounds_ref[0], bounds_ref[1]
        pl.loop(low, full)(lambda pair: visit(pair, True))
        pl.loop(full, pairs)(lambda pair: visit(pair, False))
        start, number = 2 * pairs * block_rows, (before + 1 - 2 * pairs) * block_rows
        run(*rows_of(start, number), hidden_scores(chip, start, number, True))

        for group in range(groups):
            total = jnp.sum(sum_ref[group], axis=1, keepdims=True)
            if finish:
                result = (acc_ref[group] / total).astype(jnp.bfloat16)
                for inside in range(together):
                    h = group * together + inside
                    out_refs[0][step, :, h * HEAD_WIDTH : (h + 1) * HEAD_WIDTH] = result[
                        inside * PER_DEVICE : (inside + 1) * PER_DEVICE, :
                    ]
            else:
                out_refs[0][chip, group] = acc_ref[group]
                out_refs[1][chip, group] = jnp.where(lane == HEAD_WIDTH - 1, total, max_ref[group])

    pl.loop(0, order_ref.shape[0])(serve)


def attend(place, order, queries, mine, other, first_key, key_begin, states, finish):
    _, chips, key_size, wide = queries[0].shape
    heads = CORES * wide // HEAD_WIDTH
    together = max(t for t in (1, 2, 4, 8) if t * PER_DEVICE <= 256 and heads % t == 0)
    block = CORES * chips * PER_DEVICE
    pairs = (mine.shape[0] // (chips * key_size) - 1) // 2
    low = jnp.minimum(first_key[0, 0] // (2 * block), pairs)
    full = jnp.clip((first_key[-1, -1] + 2 * block - 1) // (2 * block), low, pairs)
    bounds = jnp.stack([low, full]).astype(jnp.int32)
    state = (heads // together, together * PER_DEVICE, HEAD_WIDTH)
    vmem, smem = pl.BlockSpec(memory_space=pltpu.VMEM), pl.BlockSpec(memory_space=pltpu.SMEM)
    operands = [*queries, mine, other, first_key.reshape(-1, 1), *states]
    if finish:
        out_shape = [jax.ShapeDtypeStruct((order.shape[0], PER_DEVICE, CORES * wide), jnp.bfloat16)]
    else:
        out_shape = [jax.ShapeDtypeStruct((chips, *state), jnp.float32)] * 2
    return pl.pallas_call(
        functools.partial(attention_kernel, (key_begin, len(states) > 0, finish)),
        in_specs=[smem] * 3 + [vmem] * len(operands),
        out_specs=[vmem] * len(out_shape),
        scratch_shapes=[pltpu.VMEM(state, jnp.bfloat16)] + [pltpu.VMEM(state, jnp.float32)] * 3,
        out_shape=out_shape,
        compiler_params=pltpu.CompilerParams(vmem_limit_bytes=VMEM_BYTES),
        cost_estimate=pl.CostEstimate(
            flops=4 * order.shape[0] * PER_DEVICE * CORES * wide * mine.shape[0],
            bytes_accessed=4 * mine.size,
            transcendentals=0,
        ),
    )(place, order, bounds, *operands)


def local(hidden, gain, basis, w_query, key_matrix, value_matrix, doc_ids):
    ctx_count, tp_count = lax.axis_size("ctx"), lax.axis_size("tp")
    ctx_rank, tp_rank = lax.axis_index("ctx"), lax.axis_index("tp")
    chips = tp_count // CORES
    chip, core = tp_rank // CORES, tp_rank % CORES
    place = jnp.stack([chip, core]).astype(jnp.int32)
    count = hidden.shape[0]
    block_len = count * tp_count

    def along(value, step):
        moves = [(t, ((t // CORES + step) % chips) * CORES + t % CORES) for t in range(tp_count)]
        return lax.ppermute(value, "tp", moves)

    def swapped(value):
        return lax.ppermute(value, "tp", [(t, t ^ 1) for t in range(tp_count)])

    def after(value, *others):
        return lax.optimization_barrier((value, *others))[0]

    basis_other = swapped(basis)
    kv_weights = jnp.concatenate(
        [
            lax.dynamic_slice_in_dim(matrix, chip * HEAD_WIDTH, HEAD_WIDTH, 1)
            for matrix in (key_matrix, value_matrix)
        ],
        axis=1,
    )

    first_token = ctx_rank * block_len
    row_pos = (
        first_token
        + CORES * count * jnp.arange(chips, dtype=jnp.int32)[:, None]
        + count * core
        + jnp.arange(count, dtype=jnp.int32)[None, :]
    )
    cosine, sine = rotary_tables(row_pos.reshape(-1).astype(jnp.float32))
    cosine = cosine.reshape(chips, count, HEAD_WIDTH)
    sine = sine.reshape(chips, count, HEAD_WIDTH)
    blocks_before = min(-(-(LONGEST_DOC - 1) // block_len), ctx_count - 1)

    def normed_rows(start, size):
        values = hidden[start : start + size].astype(jnp.float32)
        meansq = jnp.mean(values * values, axis=-1, keepdims=True)
        return (values * lax.rsqrt(meansq + 1e-05) * gain.astype(jnp.float32)).astype(jnp.bfloat16)

    begins = [sum(CHUNKS[:k]) for k in range(len(CHUNKS))]
    normed = [normed_rows(begin, size) for begin, size in zip(begins, CHUNKS)]

    def gather(first, second, gate=None):
        first_right, second_left = along(first, 1), along(second, -1)
        second_right, first_left = along(second, 1), along(first, -1)
        onward = first_right if gate is None else after(first_right, gate)
        first_far, second_far = along(onward, 1), along(second_left, -1)
        return [
            (first, first_right, first_left, first_far),
            (second, second_right, second_left, second_far),
        ]

    gathered = gather(*normed)

    ids, cosine, sine, kv_weights = lax.optimization_barrier(
        (doc_ids, cosine, sine, kv_weights, gathered[0][1], gathered[1][2], basis_other)
    )[:4]
    smaller = (ids[None, :] < jnp.arange(DOCS, dtype=jnp.int32)[:, None]).astype(jnp.int32)
    doc_starts = jnp.sum(smaller, axis=1)
    for axis, length in (("ctx", ctx_count), ("tp", tp_count)):
        step = 1
        while step < length:
            doc_starts += lax.ppermute(doc_starts, axis, [(i, i ^ step) for i in range(length)])
            step *= 2
    gathered[0] = (after(gathered[0][0], doc_starts, *gathered[1]),) + gathered[0][1:]
    columns = [project(place, group, basis, basis_other, chips) for group in gathered]
    pieces = gather(*[c.reshape(-1, c.shape[2]) for c in columns], columns[1])

    doc_first = jnp.max(
        jnp.where(doc_starts[:, None, None] <= row_pos[None], doc_starts[:, None, None], 0), axis=0
    )
    first_key = doc_first - first_token + blocks_before * block_len

    query_other = swapped(after(w_query, columns[0]))
    queries, windows, states = [], [], []
    for k, size in enumerate(CHUNKS):
        begin = begins[k]
        chunk = pieces[k]
        if k + 1 < len(CHUNKS):
            chunk = (after(chunk[0], *pieces[k + 1]),) + chunk[1:]
        chunk_q, chunk_kv = project_heads(
            place,
            chunk,
            w_query,
            query_other,
            kv_weights,
            cosine[:, begin : begin + size].reshape(chips * size, HEAD_WIDTH),
            sine[:, begin : begin + size].reshape(chips * size, HEAD_WIDTH),
        )
        queries.append(chunk_q.reshape(CORES, chips, size, -1))
        blocks = [
            lax.ppermute(chunk_kv, "ctx", [(i, i + s) for i in range(ctx_count - s)])
            for s in range(blocks_before, 0, -1)
        ] + [chunk_kv]
        if k > 0:
            everyone = jnp.arange(chips, dtype=jnp.int32)
            states = attend(place, everyone, queries, *windows[0], first_key, begins[0], [], False)
            blocks = [after(received, *states) for received in blocks[:-1]] + blocks[-1:]
        mine = pack(blocks)
        windows.append((mine, swapped(mine)))

    def finished(aways):
        order = (chip + jnp.array(aways, jnp.int32)) % chips
        return attend(place, order, queries, *windows[1], first_key, begins[1], states, True)[0]

    first_two, last_two = finished((2, 1)), finished((3, 0))
    received = jnp.stack(
        [last_two[1], along(first_two[1], 1), along(first_two[0], 2), along(last_two[0], 3)]
    )
    return jnp.concatenate(
        [
            lax.dynamic_index_in_dim(received, (chip - g) % chips, 0, keepdims=False)
            for g in range(chips)
        ],
        axis=1,
    )


def solution(mesh):
    in_specs = (
        P(("dp", "ctx", "tp"), None),
        P(),
        P(None, "tp"),
        P(None, "tp"),
        P(),
        P(),
        P(("dp", "ctx", "tp")),
    )
    out_specs = P(("dp", "ctx", "tp"), None)
    return jax.shard_map(local, mesh=mesh, in_specs=in_specs, out_specs=out_specs, check_vma=False)
```

```python
import functools
import math

import jax
import jax.numpy as jnp
from jax import lax
from jax.experimental import pallas as pl
from jax.experimental.pallas import tpu as pltpu
from jax.sharding import PartitionSpec as P

HEAD_WIDTH = 128
DOCS = 8
LONGEST_DOC = 4096
CORES = 2
CHUNKS = (64, 64)
HIDDEN_SCORE = -1e30
LOWEST_MAX = -0.5e30
VMEM_BYTES = 16 * 1024 * 1024
PROJECT_VMEM_BYTES = 24 * 1024 * 1024
COLUMN_TILE = 256
PER_DEVICE = sum(CHUNKS)
SMALL_COST = pl.CostEstimate(flops=1, bytes_accessed=1, transcendentals=0)


def rotary_tables(positions):
    half_width = HEAD_WIDTH // 2
    frequency = 500000.0 ** (-jnp.arange(half_width, dtype=jnp.float32) * 2.0 / HEAD_WIDTH)
    angles = positions[:, None] * frequency
    cosine = jnp.cos(angles)
    sine = jnp.sin(angles)
    return (
        jnp.concatenate([cosine, cosine], axis=-1),
        jnp.concatenate([-sine, sine], axis=-1),
    )


def ring_order(place_ref, chips):
    chip = place_ref[0]
    return [lax.rem(chip + away, chips) for away in (0, chips - 1, 1, 2)]


def project_kernel(place_ref, *refs):
    piece_refs, (mine_ref, other_ref), o_refs, (held_ref, sem) = (
        refs[:8],
        refs[8:10],
        refs[10:12],
        refs[12:],
    )
    chips, count, columns = o_refs[0].shape
    copy = pltpu.make_async_copy(other_ref, held_ref, sem)
    copy.start()
    order = ring_order(place_ref, chips)
    wide = columns // CORES
    for side, w_ref in enumerate((mine_ref, held_ref)):
        if side == 1:
            copy.wait()
        for k, o_ref in enumerate(o_refs):
            rows = jnp.concatenate([ref[...] for ref in piece_refs[4 * k : 4 * k + 4]], axis=0)
            for n in range(0, wide, COLUMN_TILE):
                result = jnp.dot(
                    rows, w_ref[:, n : n + COLUMN_TILE], preferred_element_type=jnp.float32
                ).astype(jnp.bfloat16)
                at = side * wide + n
                for slot, chip in enumerate(order):
                    o_ref[chip, :, at : at + COLUMN_TILE] = result[
                        slot * count : (slot + 1) * count, :
                    ]


def project(place, pieces, mine, other, chips):
    count, depth = pieces[0].shape
    wide = mine.shape[1]
    vmem = pl.BlockSpec(memory_space=pltpu.VMEM)
    return pl.pallas_call(
        project_kernel,
        in_specs=[pl.BlockSpec(memory_space=pltpu.SMEM)]
        + [vmem] * 9
        + [pl.BlockSpec(memory_space=pl.ANY)],
        out_specs=[vmem] * 2,
        out_shape=[jax.ShapeDtypeStruct((chips, count, CORES * wide), jnp.bfloat16)] * 2,
        scratch_shapes=[pltpu.VMEM(other.shape, other.dtype), pltpu.SemaphoreType.DMA],
        compiler_params=pltpu.CompilerParams(vmem_limit_bytes=PROJECT_VMEM_BYTES),
        cost_estimate=SMALL_COST,
    )(place, *pieces, mine, other)


def pack_kernel(*refs):
    at = 0
    for ref in refs[:-1]:
        refs[-1][at : at + ref.shape[0], :] = ref[...]
        at += ref.shape[0]


def pack(blocks):
    vmem = pl.BlockSpec(memory_space=pltpu.VMEM)
    rows = sum(block.shape[0] for block in blocks)
    return pl.pallas_call(
        pack_kernel,
        in_specs=[vmem] * len(blocks),
        out_specs=vmem,
        out_shape=jax.ShapeDtypeStruct((rows, blocks[0].shape[1]), blocks[0].dtype),
        cost_estimate=SMALL_COST,
    )(*blocks)


def heads_kernel(rotations, place_ref, *refs):
    piece_refs, (cos_ref, sin_ref), refs = refs[:8], refs[8:10], refs[10:]
    w_refs, o_ref = refs[:-1], refs[-1]
    parts, depth, wide = w_refs[0].shape
    core = place_ref[1]
    chips = parts // CORES
    order = ring_order(place_ref, chips)
    count = piece_refs[0].shape[0] // chips

    for k in range(2):
        pieces = [ref[...] for ref in piece_refs[4 * k : 4 * k + 4]]
        own_rows = slice(k * count, (k + 1) * count)
        cosine = cos_ref[:, own_rows, :].reshape(chips * count, HEAD_WIDTH)
        sine = sin_ref[:, own_rows, :].reshape(chips * count, HEAD_WIDTH)
        for which, w_ref in enumerate(w_refs):
            for n in range(0, wide, 2 * HEAD_WIDTH):
                total = None
                for chip, piece in zip(order, pieces):
                    for side, of_core in ((0, core), (1, 1 - core)):
                        term = jnp.dot(
                            piece[:, side * depth : (side + 1) * depth],
                            w_ref[CORES * chip + of_core, :, n : n + 2 * HEAD_WIDTH],
                            preferred_element_type=jnp.float32,
                        )
                        total = term if total is None else total + term
                for i, rotate in enumerate(rotations):
                    u = total[:, i * HEAD_WIDTH : (i + 1) * HEAD_WIDTH]
                    if rotate:
                        u = u * cosine + pltpu.roll(u, HEAD_WIDTH // 2, 1) * sine
                    u = u.astype(jnp.bfloat16).reshape(chips, count, HEAD_WIDTH)
                    at = slice(n + i * HEAD_WIDTH, n + (i + 1) * HEAD_WIDTH)
                    if len(w_refs) == 1:
                        o_ref[:, own_rows, at] = u
                    else:
                        o_ref[core if which == 0 else 1 - core, :, own_rows, at] = u


def project_heads(place, pieces, cosine, sine, weights, rotations):
    depth = pieces[0].shape[1] // CORES
    wide = weights[0].shape[1]
    vmem = pl.BlockSpec(memory_space=pltpu.VMEM)
    by_part = [w.reshape(-1, depth, wide) for w in weights]
    shape = (*cosine.shape[:2], wide)
    return pl.pallas_call(
        functools.partial(heads_kernel, rotations),
        in_specs=[pl.BlockSpec(memory_space=pltpu.SMEM)] + [vmem] * (10 + len(weights)),
        out_specs=vmem,
        out_shape=jax.ShapeDtypeStruct(
            shape if len(weights) == 1 else (CORES, *shape), jnp.bfloat16
        ),
        compiler_params=pltpu.CompilerParams(vmem_limit_bytes=VMEM_BYTES),
        cost_estimate=SMALL_COST,
    )(place, *pieces, cosine, sine, *by_part)


def attention_kernel(
    place_ref, order_ref, bounds_ref, q_ref, mine_ref, other_ref, first_ref, o_ref, q_all, max_ref, sum_ref, acc_ref
):
    core = place_ref[1]
    groups, rows, _ = q_all.shape
    _, chips, count, wide = q_ref.shape
    served = order_ref.shape[0]
    per_chip = groups // served
    together = rows // count
    half = chips * count
    block = CORES * half
    last_block = mine_ref.shape[0] // half - 1
    scale = HEAD_WIDTH**-0.5 * math.log2(math.e)

    for step in range(served):
        for h in range(per_chip * together):
            at = (h % together) * count
            side, start = divmod(h * HEAD_WIDTH, wide)
            q_all[step * per_chip + h // together, at : at + count, :] = q_ref[
                side, order_ref[step], :, start : start + HEAD_WIDTH
            ]
    max_ref[...] = jnp.full(max_ref.shape, LOWEST_MAX, jnp.float32)
    sum_ref[...] = jnp.zeros(sum_ref.shape, jnp.float32)
    acc_ref[...] = jnp.zeros(acc_ref.shape, jnp.float32)

    def hidden_scores(chip, key_block):
        column = lax.broadcasted_iota(jnp.int32, (1, block), 1)
        side = column >= half
        row = jnp.where(side, column - half, column)
        key_pos = key_block * block + CORES * row - lax.rem(row, count)
        key_pos = key_pos + count * jnp.where(side, 1 - core, core)
        query_pos = last_block * block + CORES * count * chip + count * core
        query_pos = query_pos + lax.broadcasted_iota(jnp.int32, (count, 1), 0)
        at = pl.ds(pl.multiple_of(chip * count, count), count)
        seen = (key_pos >= first_ref[at, :]) & (key_pos <= query_pos)
        hide = jnp.where(seen, 0.0, HIDDEN_SCORE)
        return jnp.concatenate([hide] * together, axis=0)

    def visit(key_block, masked):
        at = pl.ds(pl.multiple_of(key_block * half, half), half)
        keys = jnp.concatenate([mine_ref[at, :HEAD_WIDTH], other_ref[at, :HEAD_WIDTH]], axis=0)
        values = jnp.concatenate([mine_ref[at, HEAD_WIDTH:], other_ref[at, HEAD_WIDTH:]], axis=0)
        hides = [hidden_scores(order_ref[step], key_block) for step in range(served) if masked]

        def scores_of(group):
            scores = lax.dot_general(
                q_all[group], keys, (((1,), (1,)), ((), ())), preferred_element_type=jnp.float32
            )
            return scores + hides[group // per_chip] if masked else scores

        def weigh(group, scores):
            old_max = max_ref[group]
            new_max = jnp.maximum(old_max, jnp.max(scores, axis=1, keepdims=True))
            rescale = jnp.exp2((old_max - new_max) * scale)
            weights = jnp.exp2(scores * scale - new_max[:, :1] * scale)
            partial = weights[:, :HEAD_WIDTH]
            for g in range(1, block // HEAD_WIDTH):
                partial = partial + weights[:, g * HEAD_WIDTH : (g + 1) * HEAD_WIDTH]
            max_ref[group] = new_max
            sum_ref[group] = sum_ref[group] * rescale + partial
            return weights.astype(jnp.bfloat16), rescale

        def collect(group, weights, rescale):
            acc_ref[group] = acc_ref[group] * rescale + jnp.dot(
                weights, values, preferred_element_type=jnp.float32
            )

        scores, last = scores_of(0), None
        for group in range(groups):
            following = scores_of(group + 1) if group + 1 < groups else None
            weighed = weigh(group, scores)
            if last is not None:
                collect(*last)
            last, scores = (group, *weighed), following
        collect(*last)

    low, full = bounds_ref[0], bounds_ref[1]
    pl.loop(low, full + 1)(lambda k: visit(jnp.where(k == full, last_block, k), True))
    pl.loop(full, last_block)(lambda k: visit(k, False))

    for group in range(groups):
        result = (acc_ref[group] / jnp.sum(sum_ref[group], axis=1, keepdims=True)).astype(jnp.bfloat16)
        for inside in range(together):
            h = group % per_chip * together + inside
            o_ref[group // per_chip, :, h * HEAD_WIDTH : (h + 1) * HEAD_WIDTH] = result[
                inside * count : (inside + 1) * count, :
            ]


def attend(place, order, queries, mine, other, first_key):
    _, chips, count, wide = queries.shape
    served = order.shape[0]
    heads = CORES * wide // HEAD_WIDTH
    together = max(t for t in (1, 2, 4, 8) if t * count <= 256 and heads % t == 0)
    block = CORES * chips * count
    last_block = mine.shape[0] // (chips * count) - 1
    low = jnp.minimum(first_key[0, 0] // block, last_block)
    full = jnp.clip((first_key[-1, -1] + block - 1) // block, low, last_block)
    bounds = jnp.stack([low, full]).astype(jnp.int32)
    state = (served * heads // together, together * count, HEAD_WIDTH)
    vmem, smem = pl.BlockSpec(memory_space=pltpu.VMEM), pl.BlockSpec(memory_space=pltpu.SMEM)
    return pl.pallas_call(
        attention_kernel,
        in_specs=[smem] * 3 + [vmem] * 4,
        out_specs=vmem,
        scratch_shapes=[pltpu.VMEM(state, jnp.bfloat16)] + [pltpu.VMEM(state, jnp.float32)] * 3,
        out_shape=jax.ShapeDtypeStruct((served, count, CORES * wide), jnp.bfloat16),
        compiler_params=pltpu.CompilerParams(vmem_limit_bytes=VMEM_BYTES),
        cost_estimate=pl.CostEstimate(
            flops=4 * served * count * CORES * wide * mine.shape[0],
            bytes_accessed=4 * mine.size,
            transcendentals=0,
        ),
    )(place, order, bounds, queries, mine, other, first_key.reshape(-1, 1))


def local(hidden, gain, basis, w_query, key_matrix, value_matrix, doc_ids):
    ctx_count, tp_count = lax.axis_size("ctx"), lax.axis_size("tp")
    ctx_rank, tp_rank = lax.axis_index("ctx"), lax.axis_index("tp")
    chips = tp_count // CORES
    chip, core = tp_rank // CORES, tp_rank % CORES
    place = jnp.stack([chip, core]).astype(jnp.int32)
    count = hidden.shape[0]
    block_len = count * tp_count

    def along(value, step):
        moves = [(t, ((t // CORES + step) % chips) * CORES + t % CORES) for t in range(tp_count)]
        return lax.ppermute(value, "tp", moves)

    def swapped(value):
        return lax.ppermute(value, "tp", [(t, t ^ 1) for t in range(tp_count)])

    def after(value, *others):
        return lax.optimization_barrier((value, *others))[0]

    basis_other = swapped(basis)
    kv_weights = jnp.concatenate(
        [
            lax.dynamic_slice_in_dim(matrix, chip * HEAD_WIDTH, HEAD_WIDTH, 1)
            for matrix in (key_matrix, value_matrix)
        ],
        axis=1,
    )

    first_token = ctx_rank * block_len
    row_pos = (
        first_token
        + CORES * count * jnp.arange(chips, dtype=jnp.int32)[:, None]
        + count * core
        + jnp.arange(count, dtype=jnp.int32)[None, :]
    )
    cosine, sine = rotary_tables(row_pos.reshape(-1).astype(jnp.float32))
    cosine = cosine.reshape(chips, count, HEAD_WIDTH)
    sine = sine.reshape(chips, count, HEAD_WIDTH)
    blocks_before = min(-(-(LONGEST_DOC - 1) // block_len), ctx_count - 1)

    def normed_rows(start, size):
        values = hidden[start : start + size].astype(jnp.float32)
        meansq = jnp.mean(values * values, axis=-1, keepdims=True)
        return (values * lax.rsqrt(meansq + 1e-05) * gain.astype(jnp.float32)).astype(jnp.bfloat16)

    begins = [sum(CHUNKS[:k]) for k in range(len(CHUNKS))]
    normed = [normed_rows(begin, size) for begin, size in zip(begins, CHUNKS)]

    def gather(first, second):
        first_right, second_left = along(first, 1), along(second, -1)
        second_right, first_left = along(second, 1), along(first, -1)
        first_far, second_far = along(first_right, 1), along(second_left, -1)
        return [
            (first, first_right, first_left, first_far),
            (second, second_right, second_left, second_far),
        ]

    gathered = gather(*normed)

    ids, cosine, sine, kv_weights = lax.optimization_barrier(
        (doc_ids, cosine, sine, kv_weights, gathered[0][1], gathered[1][2], basis_other)
    )[:4]
    smaller = (ids[None, :] < jnp.arange(DOCS, dtype=jnp.int32)[:, None]).astype(jnp.int32)
    doc_starts = jnp.sum(smaller, axis=1)
    for axis, length in (("ctx", ctx_count), ("tp", tp_count)):
        step = 1
        while step < length:
            doc_starts += lax.ppermute(doc_starts, axis, [(i, i ^ step) for i in range(length)])
            step *= 2
    first = (after(gathered[0][0], doc_starts),) + gathered[0][1:]
    columns = project(place, first + gathered[1], basis, basis_other, chips)
    first, second = gather(*[c.reshape(-1, c.shape[2]) for c in columns])
    pieces = first + second

    doc_first = jnp.max(
        jnp.where(doc_starts[:, None, None] <= row_pos[None], doc_starts[:, None, None], 0), axis=0
    )
    first_key = doc_first - first_token + blocks_before * block_len

    query_other = swapped(after(w_query, columns[0]))
    own = project_heads(place, pieces, cosine, sine, [kv_weights], (True, False))
    own = own.reshape(chips * count, -1)
    blocks = [
        lax.ppermute(own, "ctx", [(i, i + s) for i in range(ctx_count - s)])
        for s in range(blocks_before, 0, -1)
    ]
    queries = project_heads(place, pieces, cosine, sine, [w_query, query_other], (True, True))
    mine = pack([after(received, queries) for received in blocks] + [own])
    other = swapped(mine)

    def finished(aways):
        order = (chip + jnp.array(aways, jnp.int32)) % chips
        return attend(place, order, queries, mine, other, first_key)

    first_two, last_two = finished((2, 1)), finished((3, 0))
    received = jnp.stack(
        [last_two[1], along(first_two[1], 1), along(first_two[0], 2), along(last_two[0], 3)]
    )
    return jnp.concatenate(
        [
            lax.dynamic_index_in_dim(received, (chip - g) % chips, 0, keepdims=False)
            for g in range(chips)
        ],
        axis=1,
    )


def solution(mesh):
    in_specs = (
        P(("dp", "ctx", "tp"), None),
        P(),
        P(None, "tp"),
        P(None, "tp"),
        P(),
        P(),
        P(("dp", "ctx", "tp")),
    )
    out_specs = P(("dp", "ctx", "tp"), None)
    return jax.shard_map(local, mesh=mesh, in_specs=in_specs, out_specs=out_specs, check_vma=False)
```

```python
import functools
import math

import jax
import jax.numpy as jnp
from jax import lax
from jax.experimental import pallas as pl
from jax.experimental.pallas import tpu as pltpu
from jax.sharding import PartitionSpec as P

HEAD_WIDTH = 128
DOCS = 8
LONGEST_DOC = 4096
CORES = 2
CHUNKS = (64, 64)
HIDDEN_SCORE = -1e30
LOWEST_MAX = -0.5e30
VMEM_BYTES = 16 * 1024 * 1024
PROJECT_VMEM_BYTES = 24 * 1024 * 1024
COLUMN_TILE = 256
PER_DEVICE = sum(CHUNKS)
SMALL_COST = pl.CostEstimate(flops=1, bytes_accessed=1, transcendentals=0)


def rotary_tables(positions):
    half_width = HEAD_WIDTH // 2
    frequency = 500000.0 ** (-jnp.arange(half_width, dtype=jnp.float32) * 2.0 / HEAD_WIDTH)
    angles = positions[:, None] * frequency
    cosine = jnp.cos(angles)
    sine = jnp.sin(angles)
    return (
        jnp.concatenate([cosine, cosine], axis=-1),
        jnp.concatenate([-sine, sine], axis=-1),
    )


def ring_order(place_ref, chips):
    chip = place_ref[0]
    return [lax.rem(chip + away, chips) for away in (0, chips - 1, 1, 2)]


def project_kernel(place_ref, *refs):
    piece_refs, mine_ref, other_ref, o_refs = refs[:8], refs[8], refs[9], refs[10:12]
    rows_ref, held_ref, sems = refs[12:]
    chips, count, columns = o_refs[0].shape
    copies = [
        pltpu.make_async_copy(ref, rows_ref.at[pl.ds(i * count, count)], sems.at[i])
        for i, ref in enumerate(piece_refs)
    ]
    copies.append(pltpu.make_async_copy(other_ref, held_ref, sems.at[len(piece_refs)]))
    for copy in copies:
        copy.start()
    order = ring_order(place_ref, chips)
    wide = columns // CORES
    many = chips * count
    for side, w_ref in enumerate((mine_ref, held_ref)):
        if side == 1:
            copies[-1].wait()
        for k, o_ref in enumerate(o_refs):
            if side == 0:
                for copy in copies[k * chips : (k + 1) * chips]:
                    copy.wait()
            for n in range(0, wide, COLUMN_TILE):
                result = jnp.dot(
                    rows_ref[k * many : (k + 1) * many, :],
                    w_ref[:, n : n + COLUMN_TILE],
                    preferred_element_type=jnp.float32,
                ).astype(jnp.bfloat16)
                at = side * wide + n
                for slot, chip in enumerate(order):
                    o_ref[chip, :, at : at + COLUMN_TILE] = result[
                        slot * count : (slot + 1) * count, :
                    ]


def project(place, pieces, mine, other, chips):
    count, depth = pieces[0].shape
    wide = mine.shape[1]
    vmem, anywhere = pl.BlockSpec(memory_space=pltpu.VMEM), pl.BlockSpec(memory_space=pl.ANY)
    return pl.pallas_call(
        project_kernel,
        in_specs=[pl.BlockSpec(memory_space=pltpu.SMEM)] + [anywhere] * 8 + [vmem, anywhere],
        out_specs=[vmem] * 2,
        out_shape=[jax.ShapeDtypeStruct((chips, count, CORES * wide), jnp.bfloat16)] * 2,
        scratch_shapes=[
            pltpu.VMEM((len(pieces) * count, depth), jnp.bfloat16),
            pltpu.VMEM(other.shape, other.dtype),
            pltpu.SemaphoreType.DMA((len(pieces) + 1,)),
        ],
        compiler_params=pltpu.CompilerParams(vmem_limit_bytes=PROJECT_VMEM_BYTES),
        cost_estimate=SMALL_COST,
    )(place, *pieces, mine, other)


def pack_kernel(*refs):
    at = 0
    for ref in refs[:-1]:
        refs[-1][at : at + ref.shape[0], :] = ref[...]
        at += ref.shape[0]


def pack(blocks):
    vmem = pl.BlockSpec(memory_space=pltpu.VMEM)
    rows = sum(block.shape[0] for block in blocks)
    return pl.pallas_call(
        pack_kernel,
        in_specs=[vmem] * len(blocks),
        out_specs=vmem,
        out_shape=jax.ShapeDtypeStruct((rows, blocks[0].shape[1]), blocks[0].dtype),
        cost_estimate=SMALL_COST,
    )(*blocks)


def heads_kernel(rotations, place_ref, *refs):
    piece_refs, (cos_ref, sin_ref), refs = refs[:8], refs[8:10], refs[10:]
    w_refs, o_ref = refs[:-1], refs[-1]
    parts, depth, wide = w_refs[0].shape
    core = place_ref[1]
    chips = parts // CORES
    order = ring_order(place_ref, chips)
    count = piece_refs[0].shape[0] // chips

    for k in range(2):
        pieces = [ref[...] for ref in piece_refs[4 * k : 4 * k + 4]]
        own_rows = slice(k * count, (k + 1) * count)
        cosine = cos_ref[:, own_rows, :].reshape(chips * count, HEAD_WIDTH)
        sine = sin_ref[:, own_rows, :].reshape(chips * count, HEAD_WIDTH)
        for which, w_ref in enumerate(w_refs):
            for n in range(0, wide, 2 * HEAD_WIDTH):
                total = None
                for chip, piece in zip(order, pieces):
                    for side, of_core in ((0, core), (1, 1 - core)):
                        term = jnp.dot(
                            piece[:, side * depth : (side + 1) * depth],
                            w_ref[CORES * chip + of_core, :, n : n + 2 * HEAD_WIDTH],
                            preferred_element_type=jnp.float32,
                        )
                        total = term if total is None else total + term
                for i, rotate in enumerate(rotations):
                    u = total[:, i * HEAD_WIDTH : (i + 1) * HEAD_WIDTH]
                    if rotate:
                        u = u * cosine + pltpu.roll(u, HEAD_WIDTH // 2, 1) * sine
                    u = u.astype(jnp.bfloat16).reshape(chips, count, HEAD_WIDTH)
                    at = slice(n + i * HEAD_WIDTH, n + (i + 1) * HEAD_WIDTH)
                    if len(w_refs) == 1:
                        o_ref[:, own_rows, at] = u
                    else:
                        o_ref[core if which == 0 else 1 - core, :, own_rows, at] = u


def project_heads(place, pieces, cosine, sine, weights, rotations):
    depth = pieces[0].shape[1] // CORES
    wide = weights[0].shape[1]
    vmem = pl.BlockSpec(memory_space=pltpu.VMEM)
    by_part = [w.reshape(-1, depth, wide) for w in weights]
    shape = (*cosine.shape[:2], wide)
    return pl.pallas_call(
        functools.partial(heads_kernel, rotations),
        in_specs=[pl.BlockSpec(memory_space=pltpu.SMEM)] + [vmem] * (10 + len(weights)),
        out_specs=vmem,
        out_shape=jax.ShapeDtypeStruct(
            shape if len(weights) == 1 else (CORES, *shape), jnp.bfloat16
        ),
        compiler_params=pltpu.CompilerParams(vmem_limit_bytes=VMEM_BYTES),
        cost_estimate=SMALL_COST,
    )(place, *pieces, cosine, sine, *by_part)


def attention_kernel(own, place_ref, order_ref, bounds_ref, *refs):
    q_ref, mine_ref, other_ref, first_ref = refs[:4]
    if own:
        acc_out, packed_out, q_all, max_ref, sum_ref, acc_ref = refs[4:]
    else:
        acc_in, packed_in, o_ref, q_all, max_ref, sum_ref, acc_ref = refs[4:]
    core = place_ref[1]
    groups, rows, _ = q_all.shape
    _, chips, count, wide = q_ref.shape
    served = order_ref.shape[0]
    per_chip = groups // served
    together = rows // count
    half = chips * count
    block = CORES * half
    scale = HEAD_WIDTH**-0.5 * math.log2(math.e)
    lane = lax.broadcasted_iota(jnp.int32, (1, HEAD_WIDTH), 1)
    chip_at = [step if own else order_ref[step] for step in range(served)]

    for step, chip in enumerate(chip_at):
        for h in range(per_chip * together):
            at = (h % together) * count
            side, start = divmod(h * HEAD_WIDTH, wide)
            q_all[step * per_chip + h // together, at : at + count, :] = q_ref[
                side, chip, :, start : start + HEAD_WIDTH
            ]
        if not own:
            for g in range(per_chip):
                packed = packed_in[chip, g]
                acc_ref[step * per_chip + g] = acc_in[chip, g]
                max_ref[step * per_chip + g] = jnp.broadcast_to(packed[:, :1], packed.shape)
                sum_ref[step * per_chip + g] = jnp.where(lane == HEAD_WIDTH - 1, packed, 0.0)
    if own:
        max_ref[...] = jnp.full(max_ref.shape, LOWEST_MAX, jnp.float32)
        sum_ref[...] = jnp.zeros(sum_ref.shape, jnp.float32)
        acc_ref[...] = jnp.zeros(acc_ref.shape, jnp.float32)

    def hidden_scores(chip, key_start, number, query_start):
        column = lax.broadcasted_iota(jnp.int32, (1, CORES * number), 1)
        side = column >= number
        row = jnp.where(side, column - number, column)
        key_pos = key_start + CORES * row - lax.rem(row, count)
        key_pos = key_pos + count * jnp.where(side, 1 - core, core)
        seen = key_pos >= first_ref[pl.ds(pl.multiple_of(chip * count, count), count), :]
        if own:
            query_pos = query_start + CORES * count * chip + count * core
            seen = seen & (key_pos <= query_pos + lax.broadcasted_iota(jnp.int32, (count, 1), 0))
        hide = jnp.where(seen, 0.0, HIDDEN_SCORE)
        return jnp.concatenate([hide] * together, axis=0)

    def rows_of(start, number):
        at = pl.ds(start, number)
        keys = jnp.concatenate([mine_ref[at, :HEAD_WIDTH], other_ref[at, :HEAD_WIDTH]], axis=0)
        values = jnp.concatenate([mine_ref[at, HEAD_WIDTH:], other_ref[at, HEAD_WIDTH:]], axis=0)
        return keys, values

    def scores_of(job):
        group, keys, _, hide = job
        scores = lax.dot_general(
            q_all[group], keys, (((1,), (1,)), ((), ())), preferred_element_type=jnp.float32
        )
        return scores if hide is None else scores + hide

    def weigh(job, scores):
        group = job[0]
        old_max = max_ref[group]
        new_max = jnp.maximum(old_max, jnp.max(scores, axis=1, keepdims=True))
        rescale = jnp.exp2((old_max - new_max) * scale)
        weights = jnp.exp2(scores * scale - new_max[:, :1] * scale)
        partial = weights[:, :HEAD_WIDTH]
        for g in range(1, weights.shape[1] // HEAD_WIDTH):
            partial = partial + weights[:, g * HEAD_WIDTH : (g + 1) * HEAD_WIDTH]
        max_ref[group] = new_max
        sum_ref[group] = sum_ref[group] * rescale + partial
        return weights.astype(jnp.bfloat16), rescale

    def collect(job, weights, rescale):
        group, _, values, _ = job
        acc_ref[group] = acc_ref[group] * rescale + jnp.dot(
            weights, values, preferred_element_type=jnp.float32
        )

    def run(jobs):
        scores, last = scores_of(jobs[0]), None
        for i, job in enumerate(jobs):
            following = scores_of(jobs[i + 1]) if i + 1 < len(jobs) else None
            weighed = weigh(job, scores)
            if last is not None:
                collect(*last)
            last, scores = (job, *weighed), following
        collect(*last)

    def visit(key_block, masked):
        keys, values = rows_of(pl.multiple_of(key_block * half, half), half)
        jobs = []
        for step, chip in enumerate(chip_at):
            hide = hidden_scores(chip, key_block * block, half, None) if masked else None
            jobs += [(step * per_chip + g, keys, values, hide) for g in range(per_chip)]
        run(jobs)

    if own:
        jobs, start = [], bounds_ref[2]
        for step, chip in enumerate(chip_at):
            number = (chip + 1) * count
            keys, values = rows_of(0, number)
            hide = hidden_scores(chip, start, number, start)
            jobs += [(step * per_chip + g, keys, values, hide) for g in range(per_chip)]
        run(jobs)
    else:
        low, full = bounds_ref[0], bounds_ref[1]
        pl.loop(low, full)(lambda k: visit(k, True))
        pl.loop(full, mine_ref.shape[0] // half)(lambda k: visit(k, False))

    for group in range(groups):
        step, g = divmod(group, per_chip)
        total = jnp.sum(sum_ref[group], axis=1, keepdims=True)
        if own:
            acc_out[step, g] = acc_ref[group]
            packed_out[step, g] = jnp.where(lane == HEAD_WIDTH - 1, total, max_ref[group])
        else:
            result = (acc_ref[group] / total).astype(jnp.bfloat16)
            for inside in range(together):
                h = g * together + inside
                o_ref[step, :, h * HEAD_WIDTH : (h + 1) * HEAD_WIDTH] = result[
                    inside * count : (inside + 1) * count, :
                ]


def attend(place, order, queries, mine, other, first_key, before, states):
    _, chips, count, wide = queries.shape
    served = order.shape[0]
    own = len(states) == 0
    heads = CORES * wide // HEAD_WIDTH
    together = max(t for t in (1, 2, 4, 8) if t * count <= 256 and heads % t == 0)
    block = CORES * chips * count
    low = jnp.minimum(first_key[0, 0] // block, before)
    full = jnp.clip((first_key[-1, -1] + block - 1) // block, low, before)
    bounds = jnp.stack([low, full, jnp.full_like(low, before * block)]).astype(jnp.int32)
    rows = (together * count, HEAD_WIDTH)
    state = (served * heads // together, *rows)
    vmem, smem = pl.BlockSpec(memory_space=pltpu.VMEM), pl.BlockSpec(memory_space=pltpu.SMEM)
    if own:
        out_shape = [jax.ShapeDtypeStruct((chips, heads // together, *rows), jnp.float32)] * 2
    else:
        out_shape = [jax.ShapeDtypeStruct((served, count, CORES * wide), jnp.bfloat16)]
    return pl.pallas_call(
        functools.partial(attention_kernel, own),
        in_specs=[smem] * 3 + [vmem] * (4 + len(states)),
        out_specs=[vmem] * len(out_shape),
        scratch_shapes=[pltpu.VMEM(state, jnp.bfloat16)] + [pltpu.VMEM(state, jnp.float32)] * 3,
        out_shape=out_shape,
        compiler_params=pltpu.CompilerParams(vmem_limit_bytes=VMEM_BYTES),
        cost_estimate=pl.CostEstimate(
            flops=4 * served * count * CORES * wide * mine.shape[0],
            bytes_accessed=4 * mine.size,
            transcendentals=0,
        ),
    )(place, order, bounds, queries, mine, other, first_key.reshape(-1, 1), *states)


def local(hidden, gain, basis, w_query, key_matrix, value_matrix, doc_ids):
    ctx_count, tp_count = lax.axis_size("ctx"), lax.axis_size("tp")
    ctx_rank, tp_rank = lax.axis_index("ctx"), lax.axis_index("tp")
    chips = tp_count // CORES
    chip, core = tp_rank // CORES, tp_rank % CORES
    place = jnp.stack([chip, core]).astype(jnp.int32)
    count = hidden.shape[0]
    block_len = count * tp_count

    def along(value, step):
        moves = [(t, ((t // CORES + step) % chips) * CORES + t % CORES) for t in range(tp_count)]
        return lax.ppermute(value, "tp", moves)

    def swapped(value):
        return lax.ppermute(value, "tp", [(t, t ^ 1) for t in range(tp_count)])

    def after(value, *others):
        return lax.optimization_barrier((value, *others))[0]

    def summed(counts, axis, steps):
        for step in steps:
            moves = [(i, i ^ step) for i in range(lax.axis_size(axis))]
            counts += lax.ppermute(counts, axis, moves)
        return counts

    basis_other = swapped(basis)
    kv_weights = jnp.concatenate(
        [
            lax.dynamic_slice_in_dim(matrix, chip * HEAD_WIDTH, HEAD_WIDTH, 1)
            for matrix in (key_matrix, value_matrix)
        ],
        axis=1,
    )

    first_token = ctx_rank * block_len
    row_pos = (
        first_token
        + CORES * count * jnp.arange(chips, dtype=jnp.int32)[:, None]
        + count * core
        + jnp.arange(count, dtype=jnp.int32)[None, :]
    )
    cosine, sine = rotary_tables(row_pos.reshape(-1).astype(jnp.float32))
    cosine = cosine.reshape(chips, count, HEAD_WIDTH)
    sine = sine.reshape(chips, count, HEAD_WIDTH)
    blocks_before = min(-(-(LONGEST_DOC - 1) // block_len), ctx_count - 1)

    def normed_rows(start, size):
        values = hidden[start : start + size].astype(jnp.float32)
        meansq = jnp.mean(values * values, axis=-1, keepdims=True)
        return (values * lax.rsqrt(meansq + 1e-05) * gain.astype(jnp.float32)).astype(jnp.bfloat16)

    begins = [sum(CHUNKS[:k]) for k in range(len(CHUNKS))]
    normed = [normed_rows(begin, size) for begin, size in zip(begins, CHUNKS)]

    def gather(first, second):
        first_right, second_left = along(first, 1), along(second, -1)
        second_right, first_left = along(second, 1), along(first, -1)
        first_far, second_far = along(first_right, 1), along(second_left, -1)
        return [
            (first, first_right, first_left, first_far),
            (second, second_right, second_left, second_far),
        ]

    gathered = gather(*normed)

    ids, cosine, sine, kv_weights = lax.optimization_barrier(
        (doc_ids, cosine, sine, kv_weights, gathered[0][1], gathered[1][2], basis_other)
    )[:4]
    smaller = (ids[None, :] < jnp.arange(DOCS, dtype=jnp.int32)[:, None]).astype(jnp.int32)
    doc_starts = jnp.sum(smaller, axis=1)
    doc_starts = summed(doc_starts, "ctx", [1 << i for i in range((ctx_count - 1).bit_length())])
    doc_starts = summed(doc_starts, "tp", [1])
    first = (after(gathered[0][0], doc_starts),) + gathered[0][1:]
    columns = project(place, first + gathered[1], basis, basis_other, chips)
    first, second = gather(*[c.reshape(-1, c.shape[2]) for c in columns])
    pieces = first + second

    query_other = swapped(after(w_query, columns[0]))
    pieces = (after(pieces[0], query_other),) + pieces[1:]
    own = project_heads(place, pieces, cosine, sine, [kv_weights], (True, False))
    own = own.reshape(chips * count, -1)
    own_other = swapped(own)
    blocks = [
        lax.ppermute(own, "ctx", [(i, i + s) for i in range(ctx_count - s)])
        for s in range(blocks_before, 0, -1)
    ]
    doc_starts = summed(
        after(doc_starts, own_other), "tp", [CORES << i for i in range((chips - 1).bit_length())]
    )
    doc_first = jnp.max(
        jnp.where(doc_starts[:, None, None] <= row_pos[None], doc_starts[:, None, None], 0), axis=0
    )
    first_key = doc_first - first_token + blocks_before * block_len

    queries = project_heads(place, pieces, cosine, sine, [w_query, query_other], (True, True))
    everyone = jnp.arange(chips, dtype=jnp.int32)
    states = attend(place, everyone, queries, own, own_other, first_key, blocks_before, [])
    mine = pack([after(received, *states) for received in blocks])
    other = swapped(mine)

    def finished(aways):
        order = (chip + jnp.array(aways, jnp.int32)) % chips
        return attend(place, order, queries, mine, other, first_key, blocks_before, states)[0]

    first_two, last_two = finished((2, 1)), finished((3, 0))
    received = jnp.stack(
        [last_two[1], along(first_two[1], 1), along(first_two[0], 2), along(last_two[0], 3)]
    )
    return jnp.concatenate(
        [
            lax.dynamic_index_in_dim(received, (chip - g) % chips, 0, keepdims=False)
            for g in range(chips)
        ],
        axis=1,
    )


def solution(mesh):
    in_specs = (
        P(("dp", "ctx", "tp"), None),
        P(),
        P(None, "tp"),
        P(None, "tp"),
        P(),
        P(),
        P(("dp", "ctx", "tp")),
    )
    out_specs = P(("dp", "ctx", "tp"), None)
    return jax.shard_map(local, mesh=mesh, in_specs=in_specs, out_specs=out_specs, check_vma=False)
```

```python
import functools
import math

import jax
import jax.numpy as jnp
from jax import lax
from jax.experimental import pallas as pl
from jax.experimental.pallas import tpu as pltpu
from jax.sharding import PartitionSpec as P

HEAD_WIDTH = 128
DOCS = 8
LONGEST_DOC = 4096
CORES = 2
CHUNKS = (64, 64)
HIDDEN_SCORE = -1e30
LOWEST_MAX = -0.5e30
VMEM_BYTES = 16 * 1024 * 1024
PROJECT_VMEM_BYTES = 24 * 1024 * 1024
COLUMN_TILE = 256
PER_DEVICE = sum(CHUNKS)
SMALL_COST = pl.CostEstimate(flops=1, bytes_accessed=1, transcendentals=0)


def rotary_tables(positions):
    half_width = HEAD_WIDTH // 2
    frequency = 500000.0 ** (-jnp.arange(half_width, dtype=jnp.float32) * 2.0 / HEAD_WIDTH)
    angles = positions[:, None] * frequency
    cosine = jnp.cos(angles)
    sine = jnp.sin(angles)
    return (
        jnp.concatenate([cosine, cosine], axis=-1),
        jnp.concatenate([-sine, sine], axis=-1),
    )


def ring_order(place_ref, chips):
    chip = place_ref[0]
    return [lax.rem(chip + away, chips) for away in (0, chips - 1, 1, 2)]


def project_kernel(place_ref, *refs):
    piece_refs, mine_ref, other_ref, o_refs = refs[:8], refs[8], refs[9], refs[10:12]
    rows_ref, held_ref, sems = refs[12:]
    chips, count, columns = o_refs[0].shape
    copies = [
        pltpu.make_async_copy(ref, rows_ref.at[pl.ds(i * count, count)], sems.at[i])
        for i, ref in enumerate(piece_refs)
    ]
    copies.append(pltpu.make_async_copy(other_ref, held_ref, sems.at[len(piece_refs)]))
    for copy in copies:
        copy.start()
    order = ring_order(place_ref, chips)
    wide = columns // CORES
    many = chips * count
    for side, w_ref in enumerate((mine_ref, held_ref)):
        if side == 1:
            copies[-1].wait()
        for k, o_ref in enumerate(o_refs):
            if side == 0:
                for copy in copies[k * chips : (k + 1) * chips]:
                    copy.wait()
            for n in range(0, wide, COLUMN_TILE):
                result = jnp.dot(
                    rows_ref[k * many : (k + 1) * many, :],
                    w_ref[:, n : n + COLUMN_TILE],
                    preferred_element_type=jnp.float32,
                ).astype(jnp.bfloat16)
                at = side * wide + n
                for slot, chip in enumerate(order):
                    o_ref[chip, :, at : at + COLUMN_TILE] = result[
                        slot * count : (slot + 1) * count, :
                    ]


def project(place, pieces, mine, other, chips):
    count, depth = pieces[0].shape
    wide = mine.shape[1]
    vmem, anywhere = pl.BlockSpec(memory_space=pltpu.VMEM), pl.BlockSpec(memory_space=pl.ANY)
    return pl.pallas_call(
        project_kernel,
        in_specs=[pl.BlockSpec(memory_space=pltpu.SMEM)] + [anywhere] * 8 + [vmem, anywhere],
        out_specs=[vmem] * 2,
        out_shape=[jax.ShapeDtypeStruct((chips, count, CORES * wide), jnp.bfloat16)] * 2,
        scratch_shapes=[
            pltpu.VMEM((len(pieces) * count, depth), jnp.bfloat16),
            pltpu.VMEM(other.shape, other.dtype),
            pltpu.SemaphoreType.DMA((len(pieces) + 1,)),
        ],
        compiler_params=pltpu.CompilerParams(vmem_limit_bytes=PROJECT_VMEM_BYTES),
        cost_estimate=SMALL_COST,
    )(place, *pieces, mine, other)


def pack_kernel(*refs):
    o_ref, sources = refs[-1], refs[:-1]
    blocks = len(sources) // 2
    chips, count, _ = sources[0].shape
    for block in range(blocks):
        for chip in range(chips):
            for k in range(2):
                at = ((block * chips + chip) * 2 + k) * count
                o_ref[at : at + count, :] = sources[k * blocks + block][chip]


def pack(first, second):
    vmem = pl.BlockSpec(memory_space=pltpu.VMEM)
    chips, count, wide = first[0].shape
    return pl.pallas_call(
        pack_kernel,
        in_specs=[vmem] * (2 * len(first)),
        out_specs=vmem,
        out_shape=jax.ShapeDtypeStruct((2 * len(first) * chips * count, wide), first[0].dtype),
        compiler_params=pltpu.CompilerParams(vmem_limit_bytes=VMEM_BYTES),
        cost_estimate=SMALL_COST,
    )(*first, *second)


def heads_kernel(rotations, place_ref, *refs):
    rotations, chunks = rotations
    piece_refs, refs = refs[: 4 * chunks], refs[4 * chunks :]
    (cos_ref, sin_ref), w_refs, o_ref = refs[:2], refs[2:-1], refs[-1]
    parts, depth, wide = w_refs[0].shape
    core = place_ref[1]
    chips = parts // CORES
    order = ring_order(place_ref, chips)
    count = piece_refs[0].shape[0] // chips

    for k in range(chunks):
        pieces = [ref[...] for ref in piece_refs[4 * k : 4 * k + 4]]
        own_rows = slice(k * count, (k + 1) * count)
        cosine = cos_ref[:, own_rows, :].reshape(chips * count, HEAD_WIDTH)
        sine = sin_ref[:, own_rows, :].reshape(chips * count, HEAD_WIDTH)
        for which, w_ref in enumerate(w_refs):
            for n in range(0, wide, 2 * HEAD_WIDTH):
                total = None
                for chip, piece in zip(order, pieces):
                    for side, of_core in ((0, core), (1, 1 - core)):
                        term = jnp.dot(
                            piece[:, side * depth : (side + 1) * depth],
                            w_ref[CORES * chip + of_core, :, n : n + 2 * HEAD_WIDTH],
                            preferred_element_type=jnp.float32,
                        )
                        total = term if total is None else total + term
                for i, rotate in enumerate(rotations):
                    u = total[:, i * HEAD_WIDTH : (i + 1) * HEAD_WIDTH]
                    if rotate:
                        u = u * cosine + pltpu.roll(u, HEAD_WIDTH // 2, 1) * sine
                    u = u.astype(jnp.bfloat16).reshape(chips, count, HEAD_WIDTH)
                    at = slice(n + i * HEAD_WIDTH, n + (i + 1) * HEAD_WIDTH)
                    if len(w_refs) == 1:
                        o_ref[:, own_rows, at] = u
                    else:
                        o_ref[core if which == 0 else 1 - core, :, own_rows, at] = u


def project_heads(place, pieces, cosine, sine, weights, rotations):
    depth = pieces[0].shape[1] // CORES
    wide = weights[0].shape[1]
    vmem = pl.BlockSpec(memory_space=pltpu.VMEM)
    by_part = [w.reshape(-1, depth, wide) for w in weights]
    shape = (*cosine.shape[:2], wide)
    return pl.pallas_call(
        functools.partial(heads_kernel, (rotations, len(pieces) // 4)),
        in_specs=[pl.BlockSpec(memory_space=pltpu.SMEM)] + [vmem] * (len(pieces) + 2 + len(weights)),
        out_specs=vmem,
        out_shape=jax.ShapeDtypeStruct(
            shape if len(weights) == 1 else (CORES, *shape), jnp.bfloat16
        ),
        compiler_params=pltpu.CompilerParams(vmem_limit_bytes=VMEM_BYTES),
        cost_estimate=SMALL_COST,
    )(place, *pieces, cosine, sine, *by_part)


def attention_kernel(own, place_ref, order_ref, bounds_ref, *refs):
    q_ref, mine_ref, other_ref, first_ref = refs[:4]
    if own:
        acc_out, packed_out, q_all, max_ref, sum_ref, acc_ref = refs[4:]
    else:
        acc_in, packed_in, o_ref, q_all, max_ref, sum_ref, acc_ref = refs[4:]
    core = place_ref[1]
    groups, rows, _ = q_all.shape
    _, chips, count, wide = q_ref.shape
    served = order_ref.shape[0]
    per_chip = groups // served
    together = rows // count
    half = chips * count
    block = CORES * half
    scale = HEAD_WIDTH**-0.5 * math.log2(math.e)
    lane = lax.broadcasted_iota(jnp.int32, (1, HEAD_WIDTH), 1)
    chip_at = [step if own else order_ref[step] for step in range(served)]

    for step, chip in enumerate(chip_at):
        for h in range(per_chip * together):
            at = (h % together) * count
            side, start = divmod(h * HEAD_WIDTH, wide)
            q_all[step * per_chip + h // together, at : at + count, :] = q_ref[
                side, chip, :, start : start + HEAD_WIDTH
            ]
        if not own:
            for g in range(per_chip):
                packed = packed_in[chip, g]
                acc_ref[step * per_chip + g] = acc_in[chip, g]
                max_ref[step * per_chip + g] = jnp.broadcast_to(packed[:, :1], packed.shape)
                sum_ref[step * per_chip + g] = jnp.where(lane == HEAD_WIDTH - 1, packed, 0.0)
    if own:
        max_ref[...] = jnp.full(max_ref.shape, LOWEST_MAX, jnp.float32)
        sum_ref[...] = jnp.zeros(sum_ref.shape, jnp.float32)
        acc_ref[...] = jnp.zeros(acc_ref.shape, jnp.float32)

    def hidden_scores(chip, key_start, number, query_start):
        column = lax.broadcasted_iota(jnp.int32, (1, CORES * number), 1)
        side = column >= number
        row = jnp.where(side, column - number, column)
        key_pos = key_start + CORES * row - lax.rem(row, count)
        key_pos = key_pos + count * jnp.where(side, 1 - core, core)
        seen = key_pos >= first_ref[pl.ds(pl.multiple_of(chip * count, count), count), :]
        if own:
            query_pos = query_start + CORES * count * chip + count * core
            seen = seen & (key_pos <= query_pos + lax.broadcasted_iota(jnp.int32, (count, 1), 0))
        hide = jnp.where(seen, 0.0, HIDDEN_SCORE)
        return jnp.concatenate([hide] * together, axis=0)

    def rows_of(start, number):
        at = pl.ds(start, number)
        keys = jnp.concatenate([mine_ref[at, :HEAD_WIDTH], other_ref[at, :HEAD_WIDTH]], axis=0)
        values = jnp.concatenate([mine_ref[at, HEAD_WIDTH:], other_ref[at, HEAD_WIDTH:]], axis=0)
        return keys, values

    def scores_of(job):
        group, keys, _, hide = job
        scores = lax.dot_general(
            q_all[group], keys, (((1,), (1,)), ((), ())), preferred_element_type=jnp.float32
        )
        return scores if hide is None else scores + hide

    def weigh(job, scores):
        group = job[0]
        old_max = max_ref[group]
        new_max = jnp.maximum(old_max, jnp.max(scores, axis=1, keepdims=True))
        rescale = jnp.exp2((old_max - new_max) * scale)
        weights = jnp.exp2(scores * scale - new_max[:, :1] * scale)
        partial = weights[:, :HEAD_WIDTH]
        for g in range(1, weights.shape[1] // HEAD_WIDTH):
            partial = partial + weights[:, g * HEAD_WIDTH : (g + 1) * HEAD_WIDTH]
        max_ref[group] = new_max
        sum_ref[group] = sum_ref[group] * rescale + partial
        return weights.astype(jnp.bfloat16), rescale

    def collect(job, weights, rescale):
        group, _, values, _ = job
        acc_ref[group] = acc_ref[group] * rescale + jnp.dot(
            weights, values, preferred_element_type=jnp.float32
        )

    def run(jobs):
        scores, last = scores_of(jobs[0]), None
        for i, job in enumerate(jobs):
            following = scores_of(jobs[i + 1]) if i + 1 < len(jobs) else None
            weighed = weigh(job, scores)
            if last is not None:
                collect(*last)
            last, scores = (job, *weighed), following
        collect(*last)

    def visit(key_block, masked):
        keys, values = rows_of(pl.multiple_of(key_block * half, half), half)
        jobs = []
        for step, chip in enumerate(chip_at):
            hide = hidden_scores(chip, key_block * block, half, None) if masked else None
            jobs += [(step * per_chip + g, keys, values, hide) for g in range(per_chip)]
        run(jobs)

    if own:
        jobs, start = [], bounds_ref[2]
        for step, chip in enumerate(chip_at):
            number = (chip + 1) * count
            keys, values = rows_of(0, number)
            hide = hidden_scores(chip, start, number, start)
            jobs += [(step * per_chip + g, keys, values, hide) for g in range(per_chip)]
        run(jobs)
    else:
        low, full = bounds_ref[0], bounds_ref[1]
        pl.loop(low, full)(lambda k: visit(k, True))
        pl.loop(full, mine_ref.shape[0] // half)(lambda k: visit(k, False))

    for group in range(groups):
        step, g = divmod(group, per_chip)
        total = jnp.sum(sum_ref[group], axis=1, keepdims=True)
        if own:
            acc_out[step, g] = acc_ref[group]
            packed_out[step, g] = jnp.where(lane == HEAD_WIDTH - 1, total, max_ref[group])
        else:
            result = (acc_ref[group] / total).astype(jnp.bfloat16)
            for inside in range(together):
                h = g * together + inside
                o_ref[step, :, h * HEAD_WIDTH : (h + 1) * HEAD_WIDTH] = result[
                    inside * count : (inside + 1) * count, :
                ]


def attend(place, order, queries, mine, other, first_key, before, states):
    _, chips, count, wide = queries.shape
    served = order.shape[0]
    own = len(states) == 0
    heads = CORES * wide // HEAD_WIDTH
    together = max(t for t in (1, 2, 4, 8) if t * count <= 256 and heads % t == 0)
    block = CORES * chips * count
    low = jnp.minimum(first_key[0, 0] // block, before)
    full = jnp.clip((first_key[-1, -1] + block - 1) // block, low, before)
    bounds = jnp.stack([low, full, jnp.full_like(low, before * block)]).astype(jnp.int32)
    rows = (together * count, HEAD_WIDTH)
    state = (served * heads // together, *rows)
    vmem, smem = pl.BlockSpec(memory_space=pltpu.VMEM), pl.BlockSpec(memory_space=pltpu.SMEM)
    if own:
        out_shape = [jax.ShapeDtypeStruct((chips, heads // together, *rows), jnp.float32)] * 2
    else:
        out_shape = [jax.ShapeDtypeStruct((served, count, CORES * wide), jnp.bfloat16)]
    return pl.pallas_call(
        functools.partial(attention_kernel, own),
        in_specs=[smem] * 3 + [vmem] * (4 + len(states)),
        out_specs=[vmem] * len(out_shape),
        scratch_shapes=[pltpu.VMEM(state, jnp.bfloat16)] + [pltpu.VMEM(state, jnp.float32)] * 3,
        out_shape=out_shape,
        compiler_params=pltpu.CompilerParams(vmem_limit_bytes=VMEM_BYTES),
        cost_estimate=pl.CostEstimate(
            flops=4 * served * count * CORES * wide * mine.shape[0],
            bytes_accessed=4 * mine.size,
            transcendentals=0,
        ),
    )(place, order, bounds, queries, mine, other, first_key.reshape(-1, 1), *states)


def local(hidden, gain, basis, w_query, key_matrix, value_matrix, doc_ids):
    ctx_count, tp_count = lax.axis_size("ctx"), lax.axis_size("tp")
    ctx_rank, tp_rank = lax.axis_index("ctx"), lax.axis_index("tp")
    chips = tp_count // CORES
    chip, core = tp_rank // CORES, tp_rank % CORES
    place = jnp.stack([chip, core]).astype(jnp.int32)
    count = hidden.shape[0]
    block_len = count * tp_count

    def along(value, step):
        moves = [(t, ((t // CORES + step) % chips) * CORES + t % CORES) for t in range(tp_count)]
        return lax.ppermute(value, "tp", moves)

    def swapped(value):
        return lax.ppermute(value, "tp", [(t, t ^ 1) for t in range(tp_count)])

    def after(value, *others):
        return lax.optimization_barrier((value, *others))[0]

    def summed(counts, axis, steps):
        for step in steps:
            moves = [(i, i ^ step) for i in range(lax.axis_size(axis))]
            counts += lax.ppermute(counts, axis, moves)
        return counts

    basis_other = swapped(basis)
    kv_weights = jnp.concatenate(
        [
            lax.dynamic_slice_in_dim(matrix, chip * HEAD_WIDTH, HEAD_WIDTH, 1)
            for matrix in (key_matrix, value_matrix)
        ],
        axis=1,
    )

    first_token = ctx_rank * block_len
    row_pos = (
        first_token
        + CORES * count * jnp.arange(chips, dtype=jnp.int32)[:, None]
        + count * core
        + jnp.arange(count, dtype=jnp.int32)[None, :]
    )
    cosine, sine = rotary_tables(row_pos.reshape(-1).astype(jnp.float32))
    cosine = cosine.reshape(chips, count, HEAD_WIDTH)
    sine = sine.reshape(chips, count, HEAD_WIDTH)
    blocks_before = min(-(-(LONGEST_DOC - 1) // block_len), ctx_count - 1)

    def normed_rows(start, size):
        values = hidden[start : start + size].astype(jnp.float32)
        meansq = jnp.mean(values * values, axis=-1, keepdims=True)
        return (values * lax.rsqrt(meansq + 1e-05) * gain.astype(jnp.float32)).astype(jnp.bfloat16)

    begins = [sum(CHUNKS[:k]) for k in range(len(CHUNKS))]
    normed = [normed_rows(begin, size) for begin, size in zip(begins, CHUNKS)]

    def gather(first, second):
        first_right, second_left = along(first, 1), along(second, -1)
        second_right, first_left = along(second, 1), along(first, -1)
        first_far, second_far = along(first_right, 1), along(second_left, -1)
        return [
            (first, first_right, first_left, first_far),
            (second, second_right, second_left, second_far),
        ]

    smaller = (doc_ids[None, :] < jnp.arange(DOCS, dtype=jnp.int32)[:, None]).astype(jnp.int32)
    doc_starts = jnp.sum(smaller, axis=1)
    doc_starts = sum([along(doc_starts, step) for step in range(1, chips)], doc_starts)
    normed = [after(rows, doc_starts) for rows in normed]
    gathered = gather(*normed)
    doc_starts, cosine, sine, kv_weights = lax.optimization_barrier(
        (doc_starts, cosine, sine, kv_weights, gathered[0][1], gathered[1][2], basis_other)
    )[:4]
    doc_starts = summed(doc_starts, "ctx", [1 << i for i in range((ctx_count - 1).bit_length())])
    doc_starts = summed(doc_starts, "tp", [1])
    first = (after(gathered[0][0], doc_starts),) + gathered[0][1:]
    columns = project(place, first + gathered[1], basis, basis_other, chips)
    query_other = swapped(after(w_query, columns[0]))
    first, second = [c.reshape(-1, c.shape[2]) for c in columns]
    first_right, first_left = along(first, 1), along(first, -1)
    first_far = along(first_right, 1)
    second_left = along(after(second, first_left), -1)
    second_right = along(after(second, first_far, query_other), 1)
    second_far = along(second_left, -1)
    pieces = (first, first_right, first_left, first_far)
    pieces += (second, second_right, second_left, second_far)

    def shifts(key_values, steps):
        return [
            lax.ppermute(key_values, "ctx", [(i, i + s) for i in range(ctx_count - s)]) for s in steps
        ]

    steps = list(range(blocks_before, 0, -1))
    early = len(steps) - 1
    own, blocks = [], []
    for k in range(2):
        rows = slice(k * CHUNKS[0], (k + 1) * CHUNKS[0])
        chunk = pieces[4 * k : 4 * k + 4]
        if k == 1:
            chunk = (after(chunk[0], *blocks[0][:early]),) + chunk[1:]
        own.append(
            project_heads(
                place,
                chunk,
                cosine[:, rows],
                sine[:, rows],
                [kv_weights],
                (True, False),
            )
        )
        here = shifts(own[k], steps[:early])
        later = after(own[k], *here) if k == 0 else own[k]
        blocks.append(here + shifts(later, steps[early:]))

    doc_first = jnp.max(
        jnp.where(doc_starts[:, None, None] <= row_pos[None], doc_starts[:, None, None], 0), axis=0
    )
    first_key = doc_first - first_token + blocks_before * block_len

    queries = project_heads(place, pieces, cosine, sine, [w_query, query_other], (True, True))
    everyone = jnp.arange(chips, dtype=jnp.int32)
    own = pack(own[:1], own[1:])
    states = attend(place, everyone, queries, own, swapped(own), first_key, blocks_before, [])
    mine = pack(blocks[0], [after(received, *states) for received in blocks[1]])
    other = swapped(mine)

    def finished(aways):
        order = (chip + jnp.array(aways, jnp.int32)) % chips
        return attend(place, order, queries, mine, other, first_key, blocks_before, states)[0]

    first_two, last_two = finished((2, 1)), finished((3, 0))
    received = jnp.stack(
        [last_two[1], along(first_two[1], 1), along(first_two[0], 2), along(last_two[0], 3)]
    )
    return jnp.concatenate(
        [
            lax.dynamic_index_in_dim(received, (chip - g) % chips, 0, keepdims=False)
            for g in range(chips)
        ],
        axis=1,
    )


def solution(mesh):
    in_specs = (
        P(("dp", "ctx", "tp"), None),
        P(),
        P(None, "tp"),
        P(None, "tp"),
        P(),
        P(),
        P(("dp", "ctx", "tp")),
    )
    out_specs = P(("dp", "ctx", "tp"), None)
    return jax.shard_map(local, mesh=mesh, in_specs=in_specs, out_specs=out_specs, check_vma=False)
```

```python
import functools
import math

import jax
import jax.numpy as jnp
from jax import lax
from jax.experimental import pallas as pl
from jax.experimental.pallas import tpu as pltpu
from jax.sharding import PartitionSpec as P

HEAD_WIDTH = 128
DOCS = 8
LONGEST_DOC = 4096
CORES = 2
CHUNKS = (64, 64)
HIDDEN_SCORE = -1e30
LOWEST_MAX = -0.5e30
VMEM_BYTES = 16 * 1024 * 1024
PROJECT_VMEM_BYTES = 24 * 1024 * 1024
COLUMN_TILE = 256
PER_DEVICE = sum(CHUNKS)
SMALL_COST = pl.CostEstimate(flops=1, bytes_accessed=1, transcendentals=0)


def rotary_tables(positions):
    half_width = HEAD_WIDTH // 2
    frequency = 500000.0 ** (-jnp.arange(half_width, dtype=jnp.float32) * 2.0 / HEAD_WIDTH)
    angles = positions[:, None] * frequency
    cosine = jnp.cos(angles)
    sine = jnp.sin(angles)
    return (
        jnp.concatenate([cosine, cosine], axis=-1),
        jnp.concatenate([-sine, sine], axis=-1),
    )


def ring_order(place_ref, chips):
    chip = place_ref[0]
    return [lax.rem(chip + away, chips) for away in (0, chips - 1, 1, 2)]


def project_kernel(place_ref, *refs):
    piece_refs, mine_ref, other_ref, o_refs = refs[:8], refs[8], refs[9], refs[10:12]
    rows_ref, held_ref, sems = refs[12:]
    chips, count, columns = o_refs[0].shape
    copies = [
        pltpu.make_async_copy(ref, rows_ref.at[pl.ds(i * count, count)], sems.at[i])
        for i, ref in enumerate(piece_refs)
    ]
    copies.append(pltpu.make_async_copy(other_ref, held_ref, sems.at[len(piece_refs)]))
    for copy in copies:
        copy.start()
    order = ring_order(place_ref, chips)
    wide = columns // CORES
    many = chips * count
    for side, w_ref in enumerate((mine_ref, held_ref)):
        if side == 1:
            copies[-1].wait()
        for k, o_ref in enumerate(o_refs):
            if side == 0:
                for copy in copies[k * chips : (k + 1) * chips]:
                    copy.wait()
            for n in range(0, wide, COLUMN_TILE):
                result = jnp.dot(
                    rows_ref[k * many : (k + 1) * many, :],
                    w_ref[:, n : n + COLUMN_TILE],
                    preferred_element_type=jnp.float32,
                ).astype(jnp.bfloat16)
                at = side * wide + n
                for slot, chip in enumerate(order):
                    o_ref[chip, :, at : at + COLUMN_TILE] = result[
                        slot * count : (slot + 1) * count, :
                    ]


def project(place, pieces, mine, other, chips):
    count, depth = pieces[0].shape
    wide = mine.shape[1]
    vmem, anywhere = pl.BlockSpec(memory_space=pltpu.VMEM), pl.BlockSpec(memory_space=pl.ANY)
    return pl.pallas_call(
        project_kernel,
        in_specs=[pl.BlockSpec(memory_space=pltpu.SMEM)] + [anywhere] * 8 + [vmem, anywhere],
        out_specs=[vmem] * 2,
        out_shape=[jax.ShapeDtypeStruct((chips, count, CORES * wide), jnp.bfloat16)] * 2,
        scratch_shapes=[
            pltpu.VMEM((len(pieces) * count, depth), jnp.bfloat16),
            pltpu.VMEM(other.shape, other.dtype),
            pltpu.SemaphoreType.DMA((len(pieces) + 1,)),
        ],
        compiler_params=pltpu.CompilerParams(vmem_limit_bytes=PROJECT_VMEM_BYTES),
        cost_estimate=SMALL_COST,
    )(place, *pieces, mine, other)


def pack_kernel(*refs):
    at = 0
    for ref in refs[:-1]:
        refs[-1][at : at + ref.shape[0], :] = ref[...]
        at += ref.shape[0]


def pack(blocks):
    vmem = pl.BlockSpec(memory_space=pltpu.VMEM)
    rows = sum(block.shape[0] for block in blocks)
    return pl.pallas_call(
        pack_kernel,
        in_specs=[vmem] * len(blocks),
        out_specs=vmem,
        out_shape=jax.ShapeDtypeStruct((rows, blocks[0].shape[1]), blocks[0].dtype),
        cost_estimate=SMALL_COST,
    )(*blocks)


def heads_kernel(rotations, place_ref, *refs):
    piece_refs, (cos_ref, sin_ref), refs = refs[:8], refs[8:10], refs[10:]
    w_refs, o_ref = refs[:-1], refs[-1]
    parts, depth, wide = w_refs[0].shape
    core = place_ref[1]
    chips = parts // CORES
    order = ring_order(place_ref, chips)
    count = piece_refs[0].shape[0] // chips

    for k in range(2):
        pieces = [ref[...] for ref in piece_refs[4 * k : 4 * k + 4]]
        own_rows = slice(k * count, (k + 1) * count)
        cosine = cos_ref[:, own_rows, :].reshape(chips * count, HEAD_WIDTH)
        sine = sin_ref[:, own_rows, :].reshape(chips * count, HEAD_WIDTH)
        for which, w_ref in enumerate(w_refs):
            for n in range(0, wide, 2 * HEAD_WIDTH):
                total = None
                for chip, piece in zip(order, pieces):
                    for side, of_core in ((0, core), (1, 1 - core)):
                        term = jnp.dot(
                            piece[:, side * depth : (side + 1) * depth],
                            w_ref[CORES * chip + of_core, :, n : n + 2 * HEAD_WIDTH],
                            preferred_element_type=jnp.float32,
                        )
                        total = term if total is None else total + term
                for i, rotate in enumerate(rotations):
                    u = total[:, i * HEAD_WIDTH : (i + 1) * HEAD_WIDTH]
                    if rotate:
                        u = u * cosine + pltpu.roll(u, HEAD_WIDTH // 2, 1) * sine
                    u = u.astype(jnp.bfloat16).reshape(chips, count, HEAD_WIDTH)
                    at = slice(n + i * HEAD_WIDTH, n + (i + 1) * HEAD_WIDTH)
                    if len(w_refs) == 1:
                        o_ref[:, own_rows, at] = u
                    else:
                        o_ref[core if which == 0 else 1 - core, :, own_rows, at] = u


def project_heads(place, pieces, cosine, sine, weights, rotations):
    depth = pieces[0].shape[1] // CORES
    wide = weights[0].shape[1]
    vmem = pl.BlockSpec(memory_space=pltpu.VMEM)
    by_part = [w.reshape(-1, depth, wide) for w in weights]
    shape = (*cosine.shape[:2], wide)
    return pl.pallas_call(
        functools.partial(heads_kernel, rotations),
        in_specs=[pl.BlockSpec(memory_space=pltpu.SMEM)] + [vmem] * (10 + len(weights)),
        out_specs=vmem,
        out_shape=jax.ShapeDtypeStruct(
            shape if len(weights) == 1 else (CORES, *shape), jnp.bfloat16
        ),
        compiler_params=pltpu.CompilerParams(vmem_limit_bytes=VMEM_BYTES),
        cost_estimate=SMALL_COST,
    )(place, *pieces, cosine, sine, *by_part)


def attention_kernel(own, place_ref, order_ref, bounds_ref, *refs):
    q_ref, mine_ref, other_ref, first_ref = refs[:4]
    if own:
        acc_out, packed_out, q_all, max_ref, sum_ref, acc_ref = refs[4:]
    else:
        acc_in, packed_in, o_ref, q_all, max_ref, sum_ref, acc_ref = refs[4:]
    core = place_ref[1]
    groups, rows, _ = q_all.shape
    _, chips, count, wide = q_ref.shape
    served = order_ref.shape[0]
    per_chip = groups // served
    together = rows // count
    half = chips * count
    block = CORES * half
    scale = HEAD_WIDTH**-0.5 * math.log2(math.e)
    lane = lax.broadcasted_iota(jnp.int32, (1, HEAD_WIDTH), 1)
    chip_at = [step if own else order_ref[step] for step in range(served)]

    for step, chip in enumerate(chip_at):
        for h in range(per_chip * together):
            at = (h % together) * count
            side, start = divmod(h * HEAD_WIDTH, wide)
            q_all[step * per_chip + h // together, at : at + count, :] = q_ref[
                side, chip, :, start : start + HEAD_WIDTH
            ]
        if not own:
            for g in range(per_chip):
                packed = packed_in[chip, g]
                acc_ref[step * per_chip + g] = acc_in[chip, g]
                max_ref[step * per_chip + g] = jnp.broadcast_to(packed[:, :1], packed.shape)
                sum_ref[step * per_chip + g] = jnp.where(lane == HEAD_WIDTH - 1, packed, 0.0)
    if own:
        max_ref[...] = jnp.full(max_ref.shape, LOWEST_MAX, jnp.float32)
        sum_ref[...] = jnp.zeros(sum_ref.shape, jnp.float32)
        acc_ref[...] = jnp.zeros(acc_ref.shape, jnp.float32)

    def hidden_scores(chip, key_start, number, query_start):
        column = lax.broadcasted_iota(jnp.int32, (1, CORES * number), 1)
        side = column >= number
        row = jnp.where(side, column - number, column)
        key_pos = key_start + CORES * row - lax.rem(row, count)
        key_pos = key_pos + count * jnp.where(side, 1 - core, core)
        seen = key_pos >= first_ref[pl.ds(pl.multiple_of(chip * count, count), count), :]
        if own:
            query_pos = query_start + CORES * count * chip + count * core
            seen = seen & (key_pos <= query_pos + lax.broadcasted_iota(jnp.int32, (count, 1), 0))
        hide = jnp.where(seen, 0.0, HIDDEN_SCORE)
        return jnp.concatenate([hide] * together, axis=0)

    def rows_of(start, number):
        at = pl.ds(start, number)
        keys = jnp.concatenate([mine_ref[at, :HEAD_WIDTH], other_ref[at, :HEAD_WIDTH]], axis=0)
        values = jnp.concatenate([mine_ref[at, HEAD_WIDTH:], other_ref[at, HEAD_WIDTH:]], axis=0)
        return keys, values

    def scores_of(job):
        group, keys, _, hide = job
        scores = lax.dot_general(
            q_all[group], keys, (((1,), (1,)), ((), ())), preferred_element_type=jnp.float32
        )
        return scores if hide is None else scores + hide

    def weigh(job, scores):
        group = job[0]
        old_max = max_ref[group]
        new_max = jnp.maximum(old_max, jnp.max(scores, axis=1, keepdims=True))
        rescale = jnp.exp2((old_max - new_max) * scale)
        weights = jnp.exp2(scores * scale - new_max[:, :1] * scale)
        partial = weights[:, :HEAD_WIDTH]
        for g in range(1, weights.shape[1] // HEAD_WIDTH):
            partial = partial + weights[:, g * HEAD_WIDTH : (g + 1) * HEAD_WIDTH]
        max_ref[group] = new_max
        sum_ref[group] = sum_ref[group] * rescale + partial
        return weights.astype(jnp.bfloat16), rescale

    def collect(job, weights, rescale):
        group, _, values, _ = job
        acc_ref[group] = acc_ref[group] * rescale + jnp.dot(
            weights, values, preferred_element_type=jnp.float32
        )

    def run(jobs):
        scores, last = scores_of(jobs[0]), None
        for i, job in enumerate(jobs):
            following = scores_of(jobs[i + 1]) if i + 1 < len(jobs) else None
            weighed = weigh(job, scores)
            if last is not None:
                collect(*last)
            last, scores = (job, *weighed), following
        collect(*last)

    def visit(key_block, masked):
        keys, values = rows_of(pl.multiple_of(key_block * half, half), half)
        jobs = []
        for step, chip in enumerate(chip_at):
            hide = hidden_scores(chip, key_block * block, half, None) if masked else None
            jobs += [(step * per_chip + g, keys, values, hide) for g in range(per_chip)]
        run(jobs)

    if own:
        jobs, start = [], bounds_ref[2]
        for step, chip in enumerate(chip_at):
            number = (chip + 1) * count
            keys, values = rows_of(0, number)
            hide = hidden_scores(chip, start, number, start)
            jobs += [(step * per_chip + g, keys, values, hide) for g in range(per_chip)]
        run(jobs)
    else:
        low, full = bounds_ref[0], bounds_ref[1]
        pl.loop(low, full)(lambda k: visit(k, True))
        pl.loop(full, mine_ref.shape[0] // half)(lambda k: visit(k, False))

    for group in range(groups):
        step, g = divmod(group, per_chip)
        total = jnp.sum(sum_ref[group], axis=1, keepdims=True)
        if own:
            acc_out[step, g] = acc_ref[group]
            packed_out[step, g] = jnp.where(lane == HEAD_WIDTH - 1, total, max_ref[group])
        else:
            result = (acc_ref[group] / total).astype(jnp.bfloat16)
            for inside in range(together):
                h = g * together + inside
                o_ref[step, :, h * HEAD_WIDTH : (h + 1) * HEAD_WIDTH] = result[
                    inside * count : (inside + 1) * count, :
                ]


def attend(place, order, queries, mine, other, first_key, before, states):
    _, chips, count, wide = queries.shape
    served = order.shape[0]
    own = len(states) == 0
    heads = CORES * wide // HEAD_WIDTH
    together = max(t for t in (1, 2, 4, 8) if t * count <= 256 and heads % t == 0)
    block = CORES * chips * count
    low = jnp.minimum(first_key[0, 0] // block, before)
    full = jnp.clip((first_key[-1, -1] + block - 1) // block, low, before)
    bounds = jnp.stack([low, full, jnp.full_like(low, before * block)]).astype(jnp.int32)
    rows = (together * count, HEAD_WIDTH)
    state = (served * heads // together, *rows)
    vmem, smem = pl.BlockSpec(memory_space=pltpu.VMEM), pl.BlockSpec(memory_space=pltpu.SMEM)
    if own:
        out_shape = [jax.ShapeDtypeStruct((chips, heads // together, *rows), jnp.float32)] * 2
    else:
        out_shape = [jax.ShapeDtypeStruct((served, count, CORES * wide), jnp.bfloat16)]
    return pl.pallas_call(
        functools.partial(attention_kernel, own),
        in_specs=[smem] * 3 + [vmem] * (4 + len(states)),
        out_specs=[vmem] * len(out_shape),
        scratch_shapes=[pltpu.VMEM(state, jnp.bfloat16)] + [pltpu.VMEM(state, jnp.float32)] * 3,
        out_shape=out_shape,
        compiler_params=pltpu.CompilerParams(vmem_limit_bytes=VMEM_BYTES),
        cost_estimate=pl.CostEstimate(
            flops=4 * served * count * CORES * wide * mine.shape[0],
            bytes_accessed=4 * mine.size,
            transcendentals=0,
        ),
    )(place, order, bounds, queries, mine, other, first_key.reshape(-1, 1), *states)


def local(hidden, gain, basis, w_query, key_matrix, value_matrix, doc_ids):
    ctx_count, tp_count = lax.axis_size("ctx"), lax.axis_size("tp")
    ctx_rank, tp_rank = lax.axis_index("ctx"), lax.axis_index("tp")
    chips = tp_count // CORES
    chip, core = tp_rank // CORES, tp_rank % CORES
    place = jnp.stack([chip, core]).astype(jnp.int32)
    count = hidden.shape[0]
    block_len = count * tp_count

    def along(value, step):
        moves = [(t, ((t // CORES + step) % chips) * CORES + t % CORES) for t in range(tp_count)]
        return lax.ppermute(value, "tp", moves)

    def swapped(value):
        return lax.ppermute(value, "tp", [(t, t ^ 1) for t in range(tp_count)])

    def after(value, *others):
        return lax.optimization_barrier((value, *others))[0]

    def summed(counts, axis, steps):
        for step in steps:
            moves = [(i, i ^ step) for i in range(lax.axis_size(axis))]
            counts += lax.ppermute(counts, axis, moves)
        return counts

    basis_other = swapped(basis)
    kv_weights = jnp.concatenate(
        [
            lax.dynamic_slice_in_dim(matrix, chip * HEAD_WIDTH, HEAD_WIDTH, 1)
            for matrix in (key_matrix, value_matrix)
        ],
        axis=1,
    )

    first_token = ctx_rank * block_len
    row_pos = (
        first_token
        + CORES * count * jnp.arange(chips, dtype=jnp.int32)[:, None]
        + count * core
        + jnp.arange(count, dtype=jnp.int32)[None, :]
    )
    cosine, sine = rotary_tables(row_pos.reshape(-1).astype(jnp.float32))
    cosine = cosine.reshape(chips, count, HEAD_WIDTH)
    sine = sine.reshape(chips, count, HEAD_WIDTH)
    blocks_before = min(-(-(LONGEST_DOC - 1) // block_len), ctx_count - 1)

    def normed_rows(start, size):
        values = hidden[start : start + size].astype(jnp.float32)
        meansq = jnp.mean(values * values, axis=-1, keepdims=True)
        return (values * lax.rsqrt(meansq + 1e-05) * gain.astype(jnp.float32)).astype(jnp.bfloat16)

    begins = [sum(CHUNKS[:k]) for k in range(len(CHUNKS))]
    normed = [normed_rows(begin, size) for begin, size in zip(begins, CHUNKS)]

    def gather(first, second):
        first_right, second_left = along(first, 1), along(second, -1)
        second_right, first_left = along(second, 1), along(first, -1)
        first_far, second_far = along(first_right, 1), along(second_left, -1)
        return [
            (first, first_right, first_left, first_far),
            (second, second_right, second_left, second_far),
        ]

    gathered = gather(*normed)

    ids, cosine, sine, kv_weights = lax.optimization_barrier(
        (doc_ids, cosine, sine, kv_weights, gathered[0][1], gathered[1][2], basis_other)
    )[:4]
    smaller = (ids[None, :] < jnp.arange(DOCS, dtype=jnp.int32)[:, None]).astype(jnp.int32)
    doc_starts = jnp.sum(smaller, axis=1)
    doc_starts = summed(doc_starts, "ctx", [1 << i for i in range((ctx_count - 1).bit_length())])
    doc_starts = summed(doc_starts, "tp", [1])
    doc_starts = after(doc_starts, gathered[0][2], gathered[1][1])
    doc_starts = sum([along(doc_starts, step) for step in range(1, chips)], doc_starts)
    first = (after(gathered[0][0], doc_starts),) + gathered[0][1:]
    columns = project(place, first + gathered[1], basis, basis_other, chips)
    first, second = gather(*[c.reshape(-1, c.shape[2]) for c in columns])
    pieces = first + second

    query_other = swapped(after(w_query, columns[0]))
    pieces = (after(pieces[0], query_other),) + pieces[1:]
    own = project_heads(place, pieces, cosine, sine, [kv_weights], (True, False))
    own = own.reshape(chips * count, -1)
    own_other = swapped(own)
    blocks = [
        lax.ppermute(own, "ctx", [(i, i + s) for i in range(ctx_count - s)])
        for s in range(blocks_before, 0, -1)
    ]
    doc_first = jnp.max(
        jnp.where(doc_starts[:, None, None] <= row_pos[None], doc_starts[:, None, None], 0), axis=0
    )
    first_key = doc_first - first_token + blocks_before * block_len

    queries = project_heads(place, pieces, cosine, sine, [w_query, query_other], (True, True))
    everyone = jnp.arange(chips, dtype=jnp.int32)
    states = attend(place, everyone, queries, own, own_other, first_key, blocks_before, [])
    mine = pack([after(received, *states) for received in blocks])
    other = swapped(mine)

    def finished(aways):
        order = (chip + jnp.array(aways, jnp.int32)) % chips
        return attend(place, order, queries, mine, other, first_key, blocks_before, states)[0]

    both, before_last, last = finished((2, 1)), finished((3,)), finished((0,))
    received = jnp.stack(
        [last[0], along(both[1], 1), along(both[0], 2), along(before_last[0], 3)]
    )
    return jnp.concatenate(
        [
            lax.dynamic_index_in_dim(received, (chip - g) % chips, 0, keepdims=False)
            for g in range(chips)
        ],
        axis=1,
    )


def solution(mesh):
    in_specs = (
        P(("dp", "ctx", "tp"), None),
        P(),
        P(None, "tp"),
        P(None, "tp"),
        P(),
        P(),
        P(("dp", "ctx", "tp")),
    )
    out_specs = P(("dp", "ctx", "tp"), None)
    return jax.shard_map(local, mesh=mesh, in_specs=in_specs, out_specs=out_specs, check_vma=False)
```

```python
import functools
import math

import jax
import jax.numpy as jnp
from jax import lax
from jax.experimental import pallas as pl
from jax.experimental.pallas import tpu as pltpu
from jax.sharding import PartitionSpec as P

HEAD_WIDTH = 128
DOCS = 8
LONGEST_DOC = 4096
CORES = 2
CHUNKS = (64, 64)
HIDDEN_SCORE = -1e30
LOWEST_MAX = -0.5e30
VMEM_BYTES = 16 * 1024 * 1024
PROJECT_VMEM_BYTES = 24 * 1024 * 1024
COLUMN_TILE = 256
PER_DEVICE = sum(CHUNKS)
SMALL_COST = pl.CostEstimate(flops=1, bytes_accessed=1, transcendentals=0)


def rotary_tables(positions):
    half_width = HEAD_WIDTH // 2
    frequency = 500000.0 ** (-jnp.arange(half_width, dtype=jnp.float32) * 2.0 / HEAD_WIDTH)
    angles = positions[:, None] * frequency
    cosine = jnp.cos(angles)
    sine = jnp.sin(angles)
    return (
        jnp.concatenate([cosine, cosine], axis=-1),
        jnp.concatenate([-sine, sine], axis=-1),
    )


def ring_order(place_ref, chips):
    chip = place_ref[0]
    return [lax.rem(chip + away, chips) for away in (0, chips - 1, 1, 2)]


def project_kernel(place_ref, *refs):
    piece_refs, mine_ref, other_ref, o_refs = refs[:8], refs[8], refs[9], refs[10:12]
    rows_ref, held_ref, sems = refs[12:]
    chips, count, columns = o_refs[0].shape
    copies = [
        pltpu.make_async_copy(ref, rows_ref.at[pl.ds(i * count, count)], sems.at[i])
        for i, ref in enumerate(piece_refs)
    ]
    copies.append(pltpu.make_async_copy(other_ref, held_ref, sems.at[len(piece_refs)]))
    for copy in copies:
        copy.start()
    order = ring_order(place_ref, chips)
    wide = columns // CORES
    many = chips * count
    for side, w_ref in enumerate((mine_ref, held_ref)):
        if side == 1:
            copies[-1].wait()
        for k, o_ref in enumerate(o_refs):
            if side == 0:
                for copy in copies[k * chips : (k + 1) * chips]:
                    copy.wait()
            for n in range(0, wide, COLUMN_TILE):
                result = jnp.dot(
                    rows_ref[k * many : (k + 1) * many, :],
                    w_ref[:, n : n + COLUMN_TILE],
                    preferred_element_type=jnp.float32,
                ).astype(jnp.bfloat16)
                at = side * wide + n
                for slot, chip in enumerate(order):
                    o_ref[chip, :, at : at + COLUMN_TILE] = result[
                        slot * count : (slot + 1) * count, :
                    ]


def project(place, pieces, mine, other, chips):
    count, depth = pieces[0].shape
    wide = mine.shape[1]
    vmem, anywhere = pl.BlockSpec(memory_space=pltpu.VMEM), pl.BlockSpec(memory_space=pl.ANY)
    return pl.pallas_call(
        project_kernel,
        in_specs=[pl.BlockSpec(memory_space=pltpu.SMEM)] + [anywhere] * 8 + [vmem, anywhere],
        out_specs=[vmem] * 2,
        out_shape=[jax.ShapeDtypeStruct((chips, count, CORES * wide), jnp.bfloat16)] * 2,
        scratch_shapes=[
            pltpu.VMEM((len(pieces) * count, depth), jnp.bfloat16),
            pltpu.VMEM(other.shape, other.dtype),
            pltpu.SemaphoreType.DMA((len(pieces) + 1,)),
        ],
        compiler_params=pltpu.CompilerParams(vmem_limit_bytes=PROJECT_VMEM_BYTES),
        cost_estimate=SMALL_COST,
    )(place, *pieces, mine, other)


def pack_kernel(*refs):
    at = 0
    for ref in refs[:-1]:
        refs[-1][at : at + ref.shape[0], :] = ref[...]
        at += ref.shape[0]


def pack(blocks):
    vmem = pl.BlockSpec(memory_space=pltpu.VMEM)
    rows = sum(block.shape[0] for block in blocks)
    return pl.pallas_call(
        pack_kernel,
        in_specs=[vmem] * len(blocks),
        out_specs=vmem,
        out_shape=jax.ShapeDtypeStruct((rows, blocks[0].shape[1]), blocks[0].dtype),
        compiler_params=pltpu.CompilerParams(vmem_limit_bytes=VMEM_BYTES),
        cost_estimate=SMALL_COST,
    )(*blocks)


def heads_kernel(rotations, place_ref, *refs):
    piece_refs, (cos_ref, sin_ref), refs = refs[:8], refs[8:10], refs[10:]
    w_refs, o_ref = refs[:-1], refs[-1]
    parts, depth, wide = w_refs[0].shape
    core = place_ref[1]
    chips = parts // CORES
    order = ring_order(place_ref, chips)
    count = piece_refs[0].shape[0] // chips

    for k in range(2):
        pieces = [ref[...] for ref in piece_refs[4 * k : 4 * k + 4]]
        own_rows = slice(k * count, (k + 1) * count)
        cosine = cos_ref[:, own_rows, :].reshape(chips * count, HEAD_WIDTH)
        sine = sin_ref[:, own_rows, :].reshape(chips * count, HEAD_WIDTH)
        for which, w_ref in enumerate(w_refs):
            for n in range(0, wide, 2 * HEAD_WIDTH):
                total = None
                for chip, piece in zip(order, pieces):
                    for side, of_core in ((0, core), (1, 1 - core)):
                        term = jnp.dot(
                            piece[:, side * depth : (side + 1) * depth],
                            w_ref[CORES * chip + of_core, :, n : n + 2 * HEAD_WIDTH],
                            preferred_element_type=jnp.float32,
                        )
                        total = term if total is None else total + term
                for i, rotate in enumerate(rotations):
                    u = total[:, i * HEAD_WIDTH : (i + 1) * HEAD_WIDTH]
                    if rotate:
                        u = u * cosine + pltpu.roll(u, HEAD_WIDTH // 2, 1) * sine
                    u = u.astype(jnp.bfloat16).reshape(chips, count, HEAD_WIDTH)
                    at = slice(n + i * HEAD_WIDTH, n + (i + 1) * HEAD_WIDTH)
                    if len(w_refs) == 1:
                        o_ref[:, own_rows, at] = u
                    else:
                        o_ref[core if which == 0 else 1 - core, :, own_rows, at] = u


def project_heads(place, pieces, cosine, sine, weights, rotations):
    depth = pieces[0].shape[1] // CORES
    wide = weights[0].shape[1]
    vmem = pl.BlockSpec(memory_space=pltpu.VMEM)
    by_part = [w.reshape(-1, depth, wide) for w in weights]
    shape = (*cosine.shape[:2], wide)
    return pl.pallas_call(
        functools.partial(heads_kernel, rotations),
        in_specs=[pl.BlockSpec(memory_space=pltpu.SMEM)] + [vmem] * (10 + len(weights)),
        out_specs=vmem,
        out_shape=jax.ShapeDtypeStruct(
            shape if len(weights) == 1 else (CORES, *shape), jnp.bfloat16
        ),
        compiler_params=pltpu.CompilerParams(vmem_limit_bytes=VMEM_BYTES),
        cost_estimate=SMALL_COST,
    )(place, *pieces, cosine, sine, *by_part)


def attention_kernel(own, place_ref, order_ref, bounds_ref, *refs):
    q_ref, mine_ref, other_ref, first_ref = refs[:4]
    if own:
        acc_out, packed_out, q_all, max_ref, sum_ref, acc_ref = refs[4:]
    else:
        acc_in, packed_in, o_ref, q_all, max_ref, sum_ref, acc_ref = refs[4:]
    core = place_ref[1]
    groups, rows, _ = q_all.shape
    _, chips, count, wide = q_ref.shape
    served = order_ref.shape[0]
    per_chip = groups // served
    together = rows // count
    half = chips * count
    block = CORES * half
    scale = HEAD_WIDTH**-0.5 * math.log2(math.e)
    lane = lax.broadcasted_iota(jnp.int32, (1, HEAD_WIDTH), 1)
    chip_at = [step if own else order_ref[step] for step in range(served)]

    for step, chip in enumerate(chip_at):
        for h in range(per_chip * together):
            at = (h % together) * count
            side, start = divmod(h * HEAD_WIDTH, wide)
            q_all[step * per_chip + h // together, at : at + count, :] = q_ref[
                side, chip, :, start : start + HEAD_WIDTH
            ]
        if not own:
            for g in range(per_chip):
                packed = packed_in[chip, g]
                acc_ref[step * per_chip + g] = acc_in[chip, g]
                max_ref[step * per_chip + g] = jnp.broadcast_to(packed[:, :1], packed.shape)
                sum_ref[step * per_chip + g] = jnp.where(lane == HEAD_WIDTH - 1, packed, 0.0)
    if own:
        max_ref[...] = jnp.full(max_ref.shape, LOWEST_MAX, jnp.float32)
        sum_ref[...] = jnp.zeros(sum_ref.shape, jnp.float32)
        acc_ref[...] = jnp.zeros(acc_ref.shape, jnp.float32)

    def hidden_scores(chip, key_start, number, query_start):
        column = lax.broadcasted_iota(jnp.int32, (1, CORES * number), 1)
        side = column >= number
        row = jnp.where(side, column - number, column)
        key_pos = key_start + CORES * row - lax.rem(row, count)
        key_pos = key_pos + count * jnp.where(side, 1 - core, core)
        seen = key_pos >= first_ref[pl.ds(pl.multiple_of(chip * count, count), count), :]
        if own:
            query_pos = query_start + CORES * count * chip + count * core
            seen = seen & (key_pos <= query_pos + lax.broadcasted_iota(jnp.int32, (count, 1), 0))
        hide = jnp.where(seen, 0.0, HIDDEN_SCORE)
        return jnp.concatenate([hide] * together, axis=0)

    def rows_of(start, number):
        at = pl.ds(start, number)
        keys = jnp.concatenate([mine_ref[at, :HEAD_WIDTH], other_ref[at, :HEAD_WIDTH]], axis=0)
        values = jnp.concatenate([mine_ref[at, HEAD_WIDTH:], other_ref[at, HEAD_WIDTH:]], axis=0)
        return keys, values

    def scores_of(job):
        group, keys, _, hide = job
        scores = lax.dot_general(
            q_all[group], keys, (((1,), (1,)), ((), ())), preferred_element_type=jnp.float32
        )
        return scores if hide is None else scores + hide

    def weigh(job, scores):
        group = job[0]
        old_max = max_ref[group]
        new_max = jnp.maximum(old_max, jnp.max(scores, axis=1, keepdims=True))
        rescale = jnp.exp2((old_max - new_max) * scale)
        weights = jnp.exp2(scores * scale - new_max[:, :1] * scale)
        partial = weights[:, :HEAD_WIDTH]
        for g in range(1, weights.shape[1] // HEAD_WIDTH):
            partial = partial + weights[:, g * HEAD_WIDTH : (g + 1) * HEAD_WIDTH]
        max_ref[group] = new_max
        sum_ref[group] = sum_ref[group] * rescale + partial
        return weights.astype(jnp.bfloat16), rescale

    def collect(job, weights, rescale):
        group, _, values, _ = job
        acc_ref[group] = acc_ref[group] * rescale + jnp.dot(
            weights, values, preferred_element_type=jnp.float32
        )

    def run(jobs):
        scores, last = scores_of(jobs[0]), None
        for i, job in enumerate(jobs):
            following = scores_of(jobs[i + 1]) if i + 1 < len(jobs) else None
            weighed = weigh(job, scores)
            if last is not None:
                collect(*last)
            last, scores = (job, *weighed), following
        collect(*last)

    def visit(key_block, masked):
        keys, values = rows_of(pl.multiple_of(key_block * half, half), half)
        jobs = []
        for step, chip in enumerate(chip_at):
            hide = hidden_scores(chip, key_block * block, half, None) if masked else None
            jobs += [(step * per_chip + g, keys, values, hide) for g in range(per_chip)]
        run(jobs)

    if own:
        jobs, start = [], bounds_ref[2]
        for step, chip in enumerate(chip_at):
            number = (chip + 1) * count
            keys, values = rows_of(0, number)
            hide = hidden_scores(chip, start, number, start)
            jobs += [(step * per_chip + g, keys, values, hide) for g in range(per_chip)]
        run(jobs)
    else:
        low, full = bounds_ref[0], bounds_ref[1]
        pl.loop(low, full)(lambda k: visit(k, True))
        pl.loop(full, mine_ref.shape[0] // half)(lambda k: visit(k, False))

    for group in range(groups):
        step, g = divmod(group, per_chip)
        total = jnp.sum(sum_ref[group], axis=1, keepdims=True)
        if own:
            acc_out[step, g] = acc_ref[group]
            packed_out[step, g] = jnp.where(lane == HEAD_WIDTH - 1, total, max_ref[group])
        else:
            result = (acc_ref[group] / total).astype(jnp.bfloat16)
            for inside in range(together):
                h = g * together + inside
                o_ref[step, :, h * HEAD_WIDTH : (h + 1) * HEAD_WIDTH] = result[
                    inside * count : (inside + 1) * count, :
                ]


def attend(place, order, bounds, queries, mine, other, first_key, states):
    _, chips, count, wide = queries.shape
    served = order.shape[0]
    own = len(states) == 0
    heads = CORES * wide // HEAD_WIDTH
    together = max(t for t in (1, 2, 4, 8) if t * count <= 256 and heads % t == 0)
    rows = (together * count, HEAD_WIDTH)
    state = (served * heads // together, *rows)
    vmem, smem = pl.BlockSpec(memory_space=pltpu.VMEM), pl.BlockSpec(memory_space=pltpu.SMEM)
    if own:
        out_shape = [jax.ShapeDtypeStruct((chips, heads // together, *rows), jnp.float32)] * 2
    else:
        out_shape = [jax.ShapeDtypeStruct((served, count, CORES * wide), jnp.bfloat16)]
    return pl.pallas_call(
        functools.partial(attention_kernel, own),
        in_specs=[smem] * 3 + [vmem] * (4 + len(states)),
        out_specs=[vmem] * len(out_shape),
        scratch_shapes=[pltpu.VMEM(state, jnp.bfloat16)] + [pltpu.VMEM(state, jnp.float32)] * 3,
        out_shape=out_shape,
        compiler_params=pltpu.CompilerParams(vmem_limit_bytes=VMEM_BYTES),
        cost_estimate=pl.CostEstimate(
            flops=4 * served * count * CORES * wide * mine.shape[0],
            bytes_accessed=4 * mine.size,
            transcendentals=0,
        ),
    )(place, order, bounds, queries, mine, other, first_key, *states)


def local(hidden, gain, basis, w_query, key_matrix, value_matrix, doc_ids):
    ctx_count, tp_count = lax.axis_size("ctx"), lax.axis_size("tp")
    ctx_rank, tp_rank = lax.axis_index("ctx"), lax.axis_index("tp")
    chips = tp_count // CORES
    chip, core = tp_rank // CORES, tp_rank % CORES
    place = jnp.stack([chip, core]).astype(jnp.int32)
    count = hidden.shape[0]
    block_len = count * tp_count

    def along(value, step):
        moves = [(t, ((t // CORES + step) % chips) * CORES + t % CORES) for t in range(tp_count)]
        return lax.ppermute(value, "tp", moves)

    def swapped(value):
        return lax.ppermute(value, "tp", [(t, t ^ 1) for t in range(tp_count)])

    def after(value, *others):
        return lax.optimization_barrier((value, *others))[0]

    def summed(counts, axis, steps):
        for step in steps:
            moves = [(i, i ^ step) for i in range(lax.axis_size(axis))]
            counts += lax.ppermute(counts, axis, moves)
        return counts

    basis_other = swapped(basis)
    kv_weights = jnp.concatenate(
        [
            lax.dynamic_slice_in_dim(matrix, chip * HEAD_WIDTH, HEAD_WIDTH, 1)
            for matrix in (key_matrix, value_matrix)
        ],
        axis=1,
    )

    first_token = ctx_rank * block_len
    row_pos = (
        first_token
        + CORES * count * jnp.arange(chips, dtype=jnp.int32)[:, None]
        + count * core
        + jnp.arange(count, dtype=jnp.int32)[None, :]
    )
    cosine, sine = rotary_tables(row_pos.reshape(-1).astype(jnp.float32))
    cosine = cosine.reshape(chips, count, HEAD_WIDTH)
    sine = sine.reshape(chips, count, HEAD_WIDTH)
    blocks_before = min(-(-(LONGEST_DOC - 1) // block_len), ctx_count - 1)

    def normed_rows(start, size):
        values = hidden[start : start + size].astype(jnp.float32)
        meansq = jnp.mean(values * values, axis=-1, keepdims=True)
        return (values * lax.rsqrt(meansq + 1e-05) * gain.astype(jnp.float32)).astype(jnp.bfloat16)

    begins = [sum(CHUNKS[:k]) for k in range(len(CHUNKS))]
    normed = [normed_rows(begin, size) for begin, size in zip(begins, CHUNKS)]

    def gather(first, second):
        first_right, second_left = along(first, 1), along(second, -1)
        second_right, first_left = along(second, 1), along(first, -1)
        first_far, second_far = along(first_right, 1), along(second_left, -1)
        return [
            (first, first_right, first_left, first_far),
            (second, second_right, second_left, second_far),
        ]

    gathered = gather(*normed)

    ids, cosine, sine, kv_weights = lax.optimization_barrier(
        (doc_ids, cosine, sine, kv_weights, gathered[0][1], gathered[1][2], basis_other)
    )[:4]
    smaller = (ids[None, :] < jnp.arange(DOCS, dtype=jnp.int32)[:, None]).astype(jnp.int32)
    doc_starts = jnp.sum(smaller, axis=1)
    doc_starts = summed(doc_starts, "ctx", [1 << i for i in range((ctx_count - 1).bit_length())])
    doc_starts = summed(doc_starts, "tp", [1])
    doc_starts = after(doc_starts, gathered[0][2], gathered[1][1])
    doc_starts = sum([along(doc_starts, step) for step in range(1, chips)], doc_starts)
    doc_first = jnp.max(
        jnp.where(doc_starts[:, None, None] <= row_pos[None], doc_starts[:, None, None], 0), axis=0
    )
    first_key = doc_first - first_token + blocks_before * block_len
    low = jnp.minimum(first_key[0, 0] // block_len, blocks_before)
    full = jnp.clip((first_key[-1, -1] + block_len - 1) // block_len, low, blocks_before)
    bounds = jnp.stack([low, full, jnp.full_like(low, blocks_before * block_len)]).astype(jnp.int32)
    orders = [
        (chip + jnp.array(aways, jnp.int32)) % chips for aways in ((2, 1), (3, 0))
    ] + [jnp.arange(chips, dtype=jnp.int32)]
    first, first_key, bounds, orders, place = lax.optimization_barrier(
        (gathered[0][0], first_key.reshape(-1, 1), bounds, orders, place)
    )
    first = (first,) + gathered[0][1:]
    columns = project(place, first + gathered[1], basis, basis_other, chips)
    first, second = gather(*[c.reshape(-1, c.shape[2]) for c in columns])
    pieces = first + second

    query_other = swapped(after(w_query, columns[0]))
    pieces = (after(pieces[0], query_other),) + pieces[1:]
    own = project_heads(place, pieces, cosine, sine, [kv_weights], (True, False))
    own = own.reshape(chips * count, -1)
    own_other = swapped(own)
    blocks = [
        lax.ppermute(own, "ctx", [(i, i + s) for i in range(ctx_count - s)])
        for s in range(blocks_before, 0, -1)
    ]
    queries = project_heads(place, pieces, cosine, sine, [w_query, query_other], (True, True))
    states = attend(place, orders[2], bounds, queries, own, own_other, first_key, [])
    mine = pack([after(received, *states) for received in blocks])
    other = swapped(mine)
    first_two, last_two = [
        attend(place, order, bounds, queries, mine, other, first_key, states)[0]
        for order in orders[:2]
    ]
    received = jnp.stack(
        [last_two[1], along(first_two[1], 1), along(first_two[0], 2), along(last_two[0], 3)]
    )
    return jnp.concatenate(
        [
            lax.dynamic_index_in_dim(received, (chip - g) % chips, 0, keepdims=False)
            for g in range(chips)
        ],
        axis=1,
    )


def solution(mesh):
    in_specs = (
        P(("dp", "ctx", "tp"), None),
        P(),
        P(None, "tp"),
        P(None, "tp"),
        P(),
        P(),
        P(("dp", "ctx", "tp")),
    )
    out_specs = P(("dp", "ctx", "tp"), None)
    return jax.shard_map(local, mesh=mesh, in_specs=in_specs, out_specs=out_specs, check_vma=False)
```

```python
import functools
import math

import jax
import jax.numpy as jnp
from jax import lax
from jax.experimental import pallas as pl
from jax.experimental.pallas import tpu as pltpu
from jax.sharding import PartitionSpec as P

HEAD_WIDTH = 128
DOCS = 8
LONGEST_DOC = 4096
CORES = 2
CHUNKS = (64, 64)
HIDDEN_SCORE = -1e30
LOWEST_MAX = -0.5e30
VMEM_BYTES = 16 * 1024 * 1024
PROJECT_VMEM_BYTES = 24 * 1024 * 1024
COLUMN_TILE = 256
PER_DEVICE = sum(CHUNKS)
SMALL_COST = pl.CostEstimate(flops=1, bytes_accessed=1, transcendentals=0)


def rotary_tables(positions):
    half_width = HEAD_WIDTH // 2
    frequency = 500000.0 ** (-jnp.arange(half_width, dtype=jnp.float32) * 2.0 / HEAD_WIDTH)
    angles = positions[:, None] * frequency
    cosine = jnp.cos(angles)
    sine = jnp.sin(angles)
    return (
        jnp.concatenate([cosine, cosine], axis=-1),
        jnp.concatenate([-sine, sine], axis=-1),
    )


def ring_order(place_ref, chips):
    chip = place_ref[0]
    return [lax.rem(chip + away, chips) for away in (0, chips - 1, 1, 2)]


def project_kernel(place_ref, *refs):
    piece_refs, mine_ref, other_ref, o_refs = refs[:8], refs[8], refs[9], refs[10:12]
    rows_ref, held_ref, sems = refs[12:]
    chips, count, columns = o_refs[0].shape
    copies = [
        pltpu.make_async_copy(ref, rows_ref.at[pl.ds(i * count, count)], sems.at[i])
        for i, ref in enumerate(piece_refs)
    ]
    copies.append(pltpu.make_async_copy(other_ref, held_ref, sems.at[len(piece_refs)]))
    for copy in copies:
        copy.start()
    order = ring_order(place_ref, chips)
    wide = columns // CORES
    many = chips * count
    for side, w_ref in enumerate((mine_ref, held_ref)):
        if side == 1:
            copies[-1].wait()
        for k, o_ref in enumerate(o_refs):
            if side == 0:
                for copy in copies[k * chips : (k + 1) * chips]:
                    copy.wait()
            for n in range(0, wide, COLUMN_TILE):
                result = jnp.dot(
                    rows_ref[k * many : (k + 1) * many, :],
                    w_ref[:, n : n + COLUMN_TILE],
                    preferred_element_type=jnp.float32,
                ).astype(jnp.bfloat16)
                at = side * wide + n
                for slot, chip in enumerate(order):
                    o_ref[chip, :, at : at + COLUMN_TILE] = result[
                        slot * count : (slot + 1) * count, :
                    ]


def project(place, pieces, mine, other, chips):
    count, depth = pieces[0].shape
    wide = mine.shape[1]
    vmem, anywhere = pl.BlockSpec(memory_space=pltpu.VMEM), pl.BlockSpec(memory_space=pl.ANY)
    return pl.pallas_call(
        project_kernel,
        in_specs=[pl.BlockSpec(memory_space=pltpu.SMEM)] + [anywhere] * 8 + [vmem, anywhere],
        out_specs=[vmem] * 2,
        out_shape=[jax.ShapeDtypeStruct((chips, count, CORES * wide), jnp.bfloat16)] * 2,
        scratch_shapes=[
            pltpu.VMEM((len(pieces) * count, depth), jnp.bfloat16),
            pltpu.VMEM(other.shape, other.dtype),
            pltpu.SemaphoreType.DMA((len(pieces) + 1,)),
        ],
        compiler_params=pltpu.CompilerParams(vmem_limit_bytes=PROJECT_VMEM_BYTES),
        cost_estimate=SMALL_COST,
    )(place, *pieces, mine, other)


def pack_kernel(*refs):
    at = 0
    for ref in refs[:-1]:
        refs[-1][at : at + ref.shape[0], :] = ref[...]
        at += ref.shape[0]


def pack(blocks):
    vmem = pl.BlockSpec(memory_space=pltpu.VMEM)
    rows = sum(block.shape[0] for block in blocks)
    return pl.pallas_call(
        pack_kernel,
        in_specs=[vmem] * len(blocks),
        out_specs=vmem,
        out_shape=jax.ShapeDtypeStruct((rows, blocks[0].shape[1]), blocks[0].dtype),
        compiler_params=pltpu.CompilerParams(vmem_limit_bytes=VMEM_BYTES),
        cost_estimate=SMALL_COST,
    )(*blocks)


def heads_kernel(place_ref, *refs):
    piece_refs, (cos_ref, sin_ref), w_refs, (kv_ref, q_ref) = refs[:8], refs[8:10], refs[10:13], refs[13:]
    parts, depth, _ = w_refs[0].shape
    core = place_ref[1]
    chips = parts // CORES
    order = ring_order(place_ref, chips)
    count = piece_refs[0].shape[0] // chips

    for k in range(2):
        pieces = [ref[...] for ref in piece_refs[4 * k : 4 * k + 4]]
        own_rows = slice(k * count, (k + 1) * count)
        cosine = cos_ref[:, own_rows, :].reshape(chips * count, HEAD_WIDTH)
        sine = sin_ref[:, own_rows, :].reshape(chips * count, HEAD_WIDTH)
        for which, w_ref in enumerate(w_refs):
            for n in range(0, w_ref.shape[2], 2 * HEAD_WIDTH):
                total = None
                for chip, piece in zip(order, pieces):
                    for side, of_core in ((0, core), (1, 1 - core)):
                        term = jnp.dot(
                            piece[:, side * depth : (side + 1) * depth],
                            w_ref[CORES * chip + of_core, :, n : n + 2 * HEAD_WIDTH],
                            preferred_element_type=jnp.float32,
                        )
                        total = term if total is None else total + term
                for i in range(2):
                    u = total[:, i * HEAD_WIDTH : (i + 1) * HEAD_WIDTH]
                    if which > 0 or i == 0:
                        u = u * cosine + pltpu.roll(u, HEAD_WIDTH // 2, 1) * sine
                    u = u.astype(jnp.bfloat16).reshape(chips, count, HEAD_WIDTH)
                    at = slice(n + i * HEAD_WIDTH, n + (i + 1) * HEAD_WIDTH)
                    if which == 0:
                        kv_ref[:, own_rows, at] = u
                    else:
                        q_ref[core if which == 1 else 1 - core, :, own_rows, at] = u


def project_heads(place, pieces, cosine, sine, weights):
    depth = pieces[0].shape[1] // CORES
    vmem = pl.BlockSpec(memory_space=pltpu.VMEM)
    by_part = [w.reshape(-1, depth, w.shape[1]) for w in weights]
    rows = cosine.shape[:2]
    return pl.pallas_call(
        heads_kernel,
        in_specs=[pl.BlockSpec(memory_space=pltpu.SMEM)] + [vmem] * 13,
        out_specs=[vmem] * 2,
        out_shape=[
            jax.ShapeDtypeStruct((*rows, weights[0].shape[1]), jnp.bfloat16),
            jax.ShapeDtypeStruct((CORES, *rows, weights[1].shape[1]), jnp.bfloat16),
        ],
        compiler_params=pltpu.CompilerParams(vmem_limit_bytes=VMEM_BYTES),
        cost_estimate=SMALL_COST,
    )(place, *pieces, cosine, sine, *by_part)


def attention_kernel(own, place_ref, order_ref, bounds_ref, *refs):
    q_ref, mine_ref, other_ref, first_ref = refs[:4]
    if own:
        acc_out, packed_out, q_all, max_ref, sum_ref, acc_ref = refs[4:]
    else:
        acc_in, packed_in, o_ref, q_all, max_ref, sum_ref, acc_ref = refs[4:]
    core = place_ref[1]
    groups, rows, _ = q_all.shape
    _, chips, count, wide = q_ref.shape
    served = order_ref.shape[0]
    per_chip = groups // served
    together = rows // count
    half = chips * count
    block = CORES * half
    scale = HEAD_WIDTH**-0.5 * math.log2(math.e)
    lane = lax.broadcasted_iota(jnp.int32, (1, HEAD_WIDTH), 1)
    chip_at = [step if own else order_ref[step] for step in range(served)]

    for step, chip in enumerate(chip_at):
        for h in range(per_chip * together):
            at = (h % together) * count
            side, start = divmod(h * HEAD_WIDTH, wide)
            q_all[step * per_chip + h // together, at : at + count, :] = q_ref[
                side, chip, :, start : start + HEAD_WIDTH
            ]
        if not own:
            for g in range(per_chip):
                packed = packed_in[chip, g]
                acc_ref[step * per_chip + g] = acc_in[chip, g]
                max_ref[step * per_chip + g] = jnp.broadcast_to(packed[:, :1], packed.shape)
                sum_ref[step * per_chip + g] = jnp.where(lane == HEAD_WIDTH - 1, packed, 0.0)
    if own:
        max_ref[...] = jnp.full(max_ref.shape, LOWEST_MAX, jnp.float32)
        sum_ref[...] = jnp.zeros(sum_ref.shape, jnp.float32)
        acc_ref[...] = jnp.zeros(acc_ref.shape, jnp.float32)

    def hidden_scores(chip, key_start, number, query_start):
        column = lax.broadcasted_iota(jnp.int32, (1, CORES * number), 1)
        side = column >= number
        row = jnp.where(side, column - number, column)
        key_pos = key_start + CORES * row - lax.rem(row, count)
        key_pos = key_pos + count * jnp.where(side, 1 - core, core)
        seen = key_pos >= first_ref[pl.ds(pl.multiple_of(chip * count, count), count), :]
        if own:
            query_pos = query_start + CORES * count * chip + count * core
            seen = seen & (key_pos <= query_pos + lax.broadcasted_iota(jnp.int32, (count, 1), 0))
        hide = jnp.where(seen, 0.0, HIDDEN_SCORE)
        return jnp.concatenate([hide] * together, axis=0)

    def rows_of(start, number):
        at = pl.ds(start, number)
        keys = jnp.concatenate([mine_ref[at, :HEAD_WIDTH], other_ref[at, :HEAD_WIDTH]], axis=0)
        values = jnp.concatenate([mine_ref[at, HEAD_WIDTH:], other_ref[at, HEAD_WIDTH:]], axis=0)
        return keys, values

    def scores_of(job):
        group, keys, _, hide = job
        scores = lax.dot_general(
            q_all[group], keys, (((1,), (1,)), ((), ())), preferred_element_type=jnp.float32
        )
        return scores if hide is None else scores + hide

    def weigh(job, scores):
        group = job[0]
        old_max = max_ref[group]
        new_max = jnp.maximum(old_max, jnp.max(scores, axis=1, keepdims=True))
        rescale = jnp.exp2((old_max - new_max) * scale)
        weights = jnp.exp2(scores * scale - new_max[:, :1] * scale)
        partial = weights[:, :HEAD_WIDTH]
        for g in range(1, weights.shape[1] // HEAD_WIDTH):
            partial = partial + weights[:, g * HEAD_WIDTH : (g + 1) * HEAD_WIDTH]
        max_ref[group] = new_max
        sum_ref[group] = sum_ref[group] * rescale + partial
        return weights.astype(jnp.bfloat16), rescale

    def collect(job, weights, rescale):
        group, _, values, _ = job
        acc_ref[group] = acc_ref[group] * rescale + jnp.dot(
            weights, values, preferred_element_type=jnp.float32
        )

    def run(jobs):
        scores, last = scores_of(jobs[0]), None
        for i, job in enumerate(jobs):
            following = scores_of(jobs[i + 1]) if i + 1 < len(jobs) else None
            weighed = weigh(job, scores)
            if last is not None:
                collect(*last)
            last, scores = (job, *weighed), following
        collect(*last)

    def visit(key_block, masked):
        keys, values = rows_of(pl.multiple_of(key_block * half, half), half)
        jobs = []
        for step, chip in enumerate(chip_at):
            hide = hidden_scores(chip, key_block * block, half, None) if masked else None
            jobs += [(step * per_chip + g, keys, values, hide) for g in range(per_chip)]
        run(jobs)

    if own:
        jobs, start = [], bounds_ref[2]
        for step, chip in enumerate(chip_at):
            number = (chip + 1) * count
            keys, values = rows_of(0, number)
            hide = hidden_scores(chip, start, number, start)
            jobs += [(step * per_chip + g, keys, values, hide) for g in range(per_chip)]
        run(jobs)
    else:
        low, full = bounds_ref[0], bounds_ref[1]
        pl.loop(low, full)(lambda k: visit(k, True))
        pl.loop(full, mine_ref.shape[0] // half)(lambda k: visit(k, False))

    for group in range(groups):
        step, g = divmod(group, per_chip)
        total = jnp.sum(sum_ref[group], axis=1, keepdims=True)
        if own:
            acc_out[step, g] = acc_ref[group]
            packed_out[step, g] = jnp.where(lane == HEAD_WIDTH - 1, total, max_ref[group])
        else:
            result = (acc_ref[group] / total).astype(jnp.bfloat16)
            for inside in range(together):
                h = g * together + inside
                o_ref[step, :, h * HEAD_WIDTH : (h + 1) * HEAD_WIDTH] = result[
                    inside * count : (inside + 1) * count, :
                ]


def attend(place, order, queries, mine, other, first_key, before, states):
    _, chips, count, wide = queries.shape
    served = order.shape[0]
    own = len(states) == 0
    heads = CORES * wide // HEAD_WIDTH
    together = max(t for t in (1, 2, 4, 8) if t * count <= 256 and heads % t == 0)
    block = CORES * chips * count
    low = jnp.minimum(first_key[0, 0] // block, before)
    full = jnp.clip((first_key[-1, -1] + block - 1) // block, low, before)
    bounds = jnp.stack([low, full, jnp.full_like(low, before * block)]).astype(jnp.int32)
    rows = (together * count, HEAD_WIDTH)
    state = (served * heads // together, *rows)
    vmem, smem = pl.BlockSpec(memory_space=pltpu.VMEM), pl.BlockSpec(memory_space=pltpu.SMEM)
    if own:
        out_shape = [jax.ShapeDtypeStruct((chips, heads // together, *rows), jnp.float32)] * 2
    else:
        out_shape = [jax.ShapeDtypeStruct((served, count, CORES * wide), jnp.bfloat16)]
    return pl.pallas_call(
        functools.partial(attention_kernel, own),
        in_specs=[smem] * 3 + [vmem] * (4 + len(states)),
        out_specs=[vmem] * len(out_shape),
        scratch_shapes=[pltpu.VMEM(state, jnp.bfloat16)] + [pltpu.VMEM(state, jnp.float32)] * 3,
        out_shape=out_shape,
        compiler_params=pltpu.CompilerParams(vmem_limit_bytes=VMEM_BYTES),
        cost_estimate=pl.CostEstimate(
            flops=4 * served * count * CORES * wide * mine.shape[0],
            bytes_accessed=4 * mine.size,
            transcendentals=0,
        ),
    )(place, order, bounds, queries, mine, other, first_key.reshape(-1, 1), *states)


def local(hidden, gain, basis, w_query, key_matrix, value_matrix, doc_ids):
    ctx_count, tp_count = lax.axis_size("ctx"), lax.axis_size("tp")
    ctx_rank, tp_rank = lax.axis_index("ctx"), lax.axis_index("tp")
    chips = tp_count // CORES
    chip, core = tp_rank // CORES, tp_rank % CORES
    place = jnp.stack([chip, core]).astype(jnp.int32)
    count = hidden.shape[0]
    block_len = count * tp_count

    def along(value, step):
        moves = [(t, ((t // CORES + step) % chips) * CORES + t % CORES) for t in range(tp_count)]
        return lax.ppermute(value, "tp", moves)

    def swapped(value):
        return lax.ppermute(value, "tp", [(t, t ^ 1) for t in range(tp_count)])

    def after(value, *others):
        return lax.optimization_barrier((value, *others))[0]

    def summed(counts, axis, steps):
        for step in steps:
            moves = [(i, i ^ step) for i in range(lax.axis_size(axis))]
            counts += lax.ppermute(counts, axis, moves)
        return counts

    basis_other = swapped(basis)
    kv_weights = jnp.concatenate(
        [
            lax.dynamic_slice_in_dim(matrix, chip * HEAD_WIDTH, HEAD_WIDTH, 1)
            for matrix in (key_matrix, value_matrix)
        ],
        axis=1,
    )

    first_token = ctx_rank * block_len
    row_pos = (
        first_token
        + CORES * count * jnp.arange(chips, dtype=jnp.int32)[:, None]
        + count * core
        + jnp.arange(count, dtype=jnp.int32)[None, :]
    )
    cosine, sine = rotary_tables(row_pos.reshape(-1).astype(jnp.float32))
    cosine = cosine.reshape(chips, count, HEAD_WIDTH)
    sine = sine.reshape(chips, count, HEAD_WIDTH)
    blocks_before = min(-(-(LONGEST_DOC - 1) // block_len), ctx_count - 1)

    def normed_rows(start, size):
        values = hidden[start : start + size].astype(jnp.float32)
        meansq = jnp.mean(values * values, axis=-1, keepdims=True)
        return (values * lax.rsqrt(meansq + 1e-05) * gain.astype(jnp.float32)).astype(jnp.bfloat16)

    begins = [sum(CHUNKS[:k]) for k in range(len(CHUNKS))]
    normed = [normed_rows(begin, size) for begin, size in zip(begins, CHUNKS)]

    def gather(first, second):
        first_right, second_left = along(first, 1), along(second, -1)
        second_right, first_left = along(second, 1), along(first, -1)
        first_far, second_far = along(first_right, 1), along(second_left, -1)
        return [
            (first, first_right, first_left, first_far),
            (second, second_right, second_left, second_far),
        ]

    gathered = gather(*normed)

    ids, cosine, sine, kv_weights = lax.optimization_barrier(
        (doc_ids, cosine, sine, kv_weights, gathered[0][1], gathered[1][2], basis_other)
    )[:4]
    smaller = (ids[None, :] < jnp.arange(DOCS, dtype=jnp.int32)[:, None]).astype(jnp.int32)
    doc_starts = jnp.sum(smaller, axis=1)
    doc_starts = summed(doc_starts, "ctx", [1 << i for i in range((ctx_count - 1).bit_length())])
    doc_starts = summed(doc_starts, "tp", [1])
    doc_starts = after(doc_starts, gathered[0][2], gathered[1][1])
    doc_starts = sum([along(doc_starts, step) for step in range(1, chips)], doc_starts)
    first = (after(gathered[0][0], doc_starts),) + gathered[0][1:]
    columns = project(place, first + gathered[1], basis, basis_other, chips)
    first, second = gather(*[c.reshape(-1, c.shape[2]) for c in columns])
    pieces = first + second

    query_other = swapped(after(w_query, columns[0]))
    own, queries = project_heads(place, pieces, cosine, sine, [kv_weights, w_query, query_other])
    own = own.reshape(chips * count, -1)
    own_other = swapped(own)
    blocks = [
        lax.ppermute(own, "ctx", [(i, i + s) for i in range(ctx_count - s)])
        for s in range(blocks_before, 0, -1)
    ]
    doc_first = jnp.max(
        jnp.where(doc_starts[:, None, None] <= row_pos[None], doc_starts[:, None, None], 0), axis=0
    )
    first_key = doc_first - first_token + blocks_before * block_len

    everyone = jnp.arange(chips, dtype=jnp.int32)
    states = attend(place, everyone, queries, own, own_other, first_key, blocks_before, [])
    mine = pack([after(received, *states) for received in blocks])
    other = swapped(mine)

    def finished(aways):
        order = (chip + jnp.array(aways, jnp.int32)) % chips
        return attend(place, order, queries, mine, other, first_key, blocks_before, states)[0]

    first_two, last_two = finished((2, 1)), finished((3, 0))
    received = jnp.stack(
        [last_two[1], along(first_two[1], 1), along(first_two[0], 2), along(last_two[0], 3)]
    )
    return jnp.concatenate(
        [
            lax.dynamic_index_in_dim(received, (chip - g) % chips, 0, keepdims=False)
            for g in range(chips)
        ],
        axis=1,
    )


def solution(mesh):
    in_specs = (
        P(("dp", "ctx", "tp"), None),
        P(),
        P(None, "tp"),
        P(None, "tp"),
        P(),
        P(),
        P(("dp", "ctx", "tp")),
    )
    out_specs = P(("dp", "ctx", "tp"), None)
    return jax.shard_map(local, mesh=mesh, in_specs=in_specs, out_specs=out_specs, check_vma=False)
```

```python
import functools
import math

import jax
import jax.numpy as jnp
from jax import lax
from jax.experimental import pallas as pl
from jax.experimental.pallas import tpu as pltpu
from jax.sharding import PartitionSpec as P

HEAD_WIDTH = 128
DOCS = 8
LONGEST_DOC = 4096
CORES = 2
CHUNKS = (64, 64)
HIDDEN_SCORE = -1e30
LOWEST_MAX = -0.5e30
VMEM_BYTES = 16 * 1024 * 1024
PROJECT_VMEM_BYTES = 24 * 1024 * 1024
COLUMN_TILE = 256
PER_DEVICE = sum(CHUNKS)
SMALL_COST = pl.CostEstimate(flops=1, bytes_accessed=1, transcendentals=0)


def rotary_tables(positions):
    half_width = HEAD_WIDTH // 2
    frequency = 500000.0 ** (-jnp.arange(half_width, dtype=jnp.float32) * 2.0 / HEAD_WIDTH)
    angles = positions[:, None] * frequency
    cosine = jnp.cos(angles)
    sine = jnp.sin(angles)
    return (
        jnp.concatenate([cosine, cosine], axis=-1),
        jnp.concatenate([-sine, sine], axis=-1),
    )


def ring_order(place_ref, chips):
    chip = place_ref[0]
    return [lax.rem(chip + away, chips) for away in (0, chips - 1, 1, 2)]


def project_kernel(place_ref, *refs):
    piece_refs, mine_ref, other_ref, o_refs = refs[:8], refs[8], refs[9], refs[10:12]
    rows_ref, held_ref, sems = refs[12:]
    chips, count, columns = o_refs[0].shape
    copies = [
        pltpu.make_async_copy(ref, rows_ref.at[pl.ds(i * count, count)], sems.at[i])
        for i, ref in enumerate(piece_refs)
    ]
    copies.append(pltpu.make_async_copy(other_ref, held_ref, sems.at[len(piece_refs)]))
    for copy in copies:
        copy.start()
    order = ring_order(place_ref, chips)
    wide = columns // CORES
    many = chips * count
    for side, w_ref in enumerate((mine_ref, held_ref)):
        if side == 1:
            copies[-1].wait()
        for k, o_ref in enumerate(o_refs):
            if side == 0:
                for copy in copies[k * chips : (k + 1) * chips]:
                    copy.wait()
            for n in range(0, wide, COLUMN_TILE):
                result = jnp.dot(
                    rows_ref[k * many : (k + 1) * many, :],
                    w_ref[:, n : n + COLUMN_TILE],
                    preferred_element_type=jnp.float32,
                ).astype(jnp.bfloat16)
                at = side * wide + n
                for slot, chip in enumerate(order):
                    o_ref[chip, :, at : at + COLUMN_TILE] = result[
                        slot * count : (slot + 1) * count, :
                    ]


def project(place, pieces, mine, other, chips):
    count, depth = pieces[0].shape
    wide = mine.shape[1]
    vmem, anywhere = pl.BlockSpec(memory_space=pltpu.VMEM), pl.BlockSpec(memory_space=pl.ANY)
    return pl.pallas_call(
        project_kernel,
        in_specs=[pl.BlockSpec(memory_space=pltpu.SMEM)] + [anywhere] * 8 + [vmem, anywhere],
        out_specs=[vmem] * 2,
        out_shape=[jax.ShapeDtypeStruct((chips, count, CORES * wide), jnp.bfloat16)] * 2,
        scratch_shapes=[
            pltpu.VMEM((len(pieces) * count, depth), jnp.bfloat16),
            pltpu.VMEM(other.shape, other.dtype),
            pltpu.SemaphoreType.DMA((len(pieces) + 1,)),
        ],
        compiler_params=pltpu.CompilerParams(vmem_limit_bytes=PROJECT_VMEM_BYTES),
        cost_estimate=SMALL_COST,
    )(place, *pieces, mine, other)


def pack_kernel(*refs):
    at = 0
    for ref in refs[:-1]:
        refs[-1][at : at + ref.shape[0], :] = ref[...]
        at += ref.shape[0]


def pack(blocks):
    vmem = pl.BlockSpec(memory_space=pltpu.VMEM)
    rows = sum(block.shape[0] for block in blocks)
    return pl.pallas_call(
        pack_kernel,
        in_specs=[vmem] * len(blocks),
        out_specs=vmem,
        out_shape=jax.ShapeDtypeStruct((rows, blocks[0].shape[1]), blocks[0].dtype),
        compiler_params=pltpu.CompilerParams(vmem_limit_bytes=VMEM_BYTES),
        cost_estimate=SMALL_COST,
    )(*blocks)


def heads_kernel(place_ref, *refs):
    piece_refs, (cos_ref, sin_ref), w_refs, (kv_ref, q_ref) = refs[:8], refs[8:10], refs[10:13], refs[13:]
    parts, depth, _ = w_refs[0].shape
    core = place_ref[1]
    chips = parts // CORES
    order = ring_order(place_ref, chips)
    count = piece_refs[0].shape[0] // chips

    for k in range(2):
        pieces = [ref[...] for ref in piece_refs[4 * k : 4 * k + 4]]
        own_rows = slice(k * count, (k + 1) * count)
        cosine = cos_ref[:, own_rows, :].reshape(chips * count, HEAD_WIDTH)
        sine = sin_ref[:, own_rows, :].reshape(chips * count, HEAD_WIDTH)
        for which, w_ref in enumerate(w_refs):
            for n in range(0, w_ref.shape[2], 2 * HEAD_WIDTH):
                total = None
                for chip, piece in zip(order, pieces):
                    for side, of_core in ((0, core), (1, 1 - core)):
                        term = jnp.dot(
                            piece[:, side * depth : (side + 1) * depth],
                            w_ref[CORES * chip + of_core, :, n : n + 2 * HEAD_WIDTH],
                            preferred_element_type=jnp.float32,
                        )
                        total = term if total is None else total + term
                for i in range(2):
                    u = total[:, i * HEAD_WIDTH : (i + 1) * HEAD_WIDTH]
                    if which > 0 or i == 0:
                        u = u * cosine + pltpu.roll(u, HEAD_WIDTH // 2, 1) * sine
                    u = u.astype(jnp.bfloat16).reshape(chips, count, HEAD_WIDTH)
                    at = slice(n + i * HEAD_WIDTH, n + (i + 1) * HEAD_WIDTH)
                    if which == 0:
                        kv_ref[:, own_rows, at] = u
                    else:
                        q_ref[core if which == 1 else 1 - core, :, own_rows, at] = u


def project_heads(place, pieces, cosine, sine, weights):
    depth = pieces[0].shape[1] // CORES
    vmem = pl.BlockSpec(memory_space=pltpu.VMEM)
    by_part = [w.reshape(-1, depth, w.shape[1]) for w in weights]
    rows = cosine.shape[:2]
    return pl.pallas_call(
        heads_kernel,
        in_specs=[pl.BlockSpec(memory_space=pltpu.SMEM)] + [vmem] * 13,
        out_specs=[vmem] * 2,
        out_shape=[
            jax.ShapeDtypeStruct((*rows, weights[0].shape[1]), jnp.bfloat16),
            jax.ShapeDtypeStruct((CORES, *rows, weights[1].shape[1]), jnp.bfloat16),
        ],
        compiler_params=pltpu.CompilerParams(vmem_limit_bytes=VMEM_BYTES),
        cost_estimate=SMALL_COST,
    )(place, *pieces, cosine, sine, *by_part)


def attention_kernel(own, place_ref, order_ref, bounds_ref, *refs):
    q_ref, mine_ref, other_ref, first_ref = refs[:4]
    if own:
        acc_out, packed_out, q_all, max_ref, sum_ref, acc_ref = refs[4:]
    else:
        acc_in, packed_in, o_ref, q_all, max_ref, sum_ref, acc_ref = refs[4:]
    core = place_ref[1]
    groups, rows, _ = q_all.shape
    _, chips, count, wide = q_ref.shape
    served = order_ref.shape[0]
    per_chip = groups // served
    together = rows // count
    half = chips * count
    block = CORES * half
    scale = HEAD_WIDTH**-0.5 * math.log2(math.e)
    lane = lax.broadcasted_iota(jnp.int32, (1, HEAD_WIDTH), 1)
    chip_at = [step if own else order_ref[step] for step in range(served)]

    for step, chip in enumerate(chip_at):
        for h in range(per_chip * together):
            at = (h % together) * count
            side, start = divmod(h * HEAD_WIDTH, wide)
            q_all[step * per_chip + h // together, at : at + count, :] = q_ref[
                side, chip, :, start : start + HEAD_WIDTH
            ]
        if not own:
            for g in range(per_chip):
                packed = packed_in[chip, g]
                acc_ref[step * per_chip + g] = acc_in[chip, g]
                max_ref[step * per_chip + g] = jnp.broadcast_to(packed[:, :1], packed.shape)
                sum_ref[step * per_chip + g] = jnp.where(lane == HEAD_WIDTH - 1, packed, 0.0)
    if own:
        max_ref[...] = jnp.full(max_ref.shape, LOWEST_MAX, jnp.float32)
        sum_ref[...] = jnp.zeros(sum_ref.shape, jnp.float32)
        acc_ref[...] = jnp.zeros(acc_ref.shape, jnp.float32)

    def hidden_scores(chip, key_start, number, query_start):
        column = lax.broadcasted_iota(jnp.int32, (1, CORES * number), 1)
        side = column >= number
        row = jnp.where(side, column - number, column)
        key_pos = key_start + CORES * row - lax.rem(row, count)
        key_pos = key_pos + count * jnp.where(side, 1 - core, core)
        seen = key_pos >= first_ref[pl.ds(pl.multiple_of(chip * count, count), count), :]
        if own:
            query_pos = query_start + CORES * count * chip + count * core
            seen = seen & (key_pos <= query_pos + lax.broadcasted_iota(jnp.int32, (count, 1), 0))
        hide = jnp.where(seen, 0.0, HIDDEN_SCORE)
        return jnp.concatenate([hide] * together, axis=0)

    def rows_of(start, number):
        at = pl.ds(start, number)
        keys = jnp.concatenate([mine_ref[at, :HEAD_WIDTH], other_ref[at, :HEAD_WIDTH]], axis=0)
        values = jnp.concatenate([mine_ref[at, HEAD_WIDTH:], other_ref[at, HEAD_WIDTH:]], axis=0)
        return keys, values

    def scores_of(job):
        group, keys, _, hide = job
        scores = lax.dot_general(
            q_all[group], keys, (((1,), (1,)), ((), ())), preferred_element_type=jnp.float32
        )
        return scores if hide is None else scores + hide

    def weigh(job, scores):
        group = job[0]
        old_max = max_ref[group]
        new_max = jnp.maximum(old_max, jnp.max(scores, axis=1, keepdims=True))
        rescale = jnp.exp2((old_max - new_max) * scale)
        weights = jnp.exp2(scores * scale - new_max[:, :1] * scale)
        partial = weights[:, :HEAD_WIDTH]
        for g in range(1, weights.shape[1] // HEAD_WIDTH):
            partial = partial + weights[:, g * HEAD_WIDTH : (g + 1) * HEAD_WIDTH]
        max_ref[group] = new_max
        sum_ref[group] = sum_ref[group] * rescale + partial
        return weights.astype(jnp.bfloat16), rescale

    def collect(job, weights, rescale):
        group, _, values, _ = job
        acc_ref[group] = acc_ref[group] * rescale + jnp.dot(
            weights, values, preferred_element_type=jnp.float32
        )

    def run(jobs):
        scores, last = scores_of(jobs[0]), None
        for i, job in enumerate(jobs):
            following = scores_of(jobs[i + 1]) if i + 1 < len(jobs) else None
            weighed = weigh(job, scores)
            if last is not None:
                collect(*last)
            last, scores = (job, *weighed), following
        collect(*last)

    def visit(key_block, masked):
        keys, values = rows_of(pl.multiple_of(key_block * half, half), half)
        jobs = []
        for step, chip in enumerate(chip_at):
            hide = hidden_scores(chip, key_block * block, half, None) if masked else None
            jobs += [(step * per_chip + g, keys, values, hide) for g in range(per_chip)]
        run(jobs)

    if own:
        jobs, start = [], bounds_ref[2]
        for step, chip in enumerate(chip_at):
            number = (chip + 1) * count
            keys, values = rows_of(0, number)
            hide = hidden_scores(chip, start, number, start)
            jobs += [(step * per_chip + g, keys, values, hide) for g in range(per_chip)]
        run(jobs)
    else:
        low, full = bounds_ref[0], bounds_ref[1]
        pl.loop(low, full)(lambda k: visit(k, True))
        pl.loop(full, mine_ref.shape[0] // half)(lambda k: visit(k, False))

    for group in range(groups):
        step, g = divmod(group, per_chip)
        total = jnp.sum(sum_ref[group], axis=1, keepdims=True)
        if own:
            acc_out[step, g] = acc_ref[group]
            packed_out[step, g] = jnp.where(lane == HEAD_WIDTH - 1, total, max_ref[group])
        else:
            result = (acc_ref[group] / total).astype(jnp.bfloat16)
            for inside in range(together):
                h = g * together + inside
                o_ref[step, :, h * HEAD_WIDTH : (h + 1) * HEAD_WIDTH] = result[
                    inside * count : (inside + 1) * count, :
                ]


def attend(place, order, queries, mine, other, first_key, before, states):
    _, chips, count, wide = queries.shape
    served = order.shape[0]
    own = len(states) == 0
    heads = CORES * wide // HEAD_WIDTH
    together = max(t for t in (1, 2, 4, 8) if t * count <= 256 and heads % t == 0)
    block = CORES * chips * count
    low = jnp.minimum(first_key[0, 0] // block, before)
    full = jnp.clip((first_key[-1, -1] + block - 1) // block, low, before)
    bounds = jnp.stack([low, full, jnp.full_like(low, before * block)]).astype(jnp.int32)
    rows = (together * count, HEAD_WIDTH)
    state = (served * heads // together, *rows)
    vmem, smem = pl.BlockSpec(memory_space=pltpu.VMEM), pl.BlockSpec(memory_space=pltpu.SMEM)
    if own:
        out_shape = [jax.ShapeDtypeStruct((chips, heads // together, *rows), jnp.float32)] * 2
    else:
        out_shape = [jax.ShapeDtypeStruct((served, count, CORES * wide), jnp.bfloat16)]
    return pl.pallas_call(
        functools.partial(attention_kernel, own),
        in_specs=[smem] * 3 + [vmem] * (4 + len(states)),
        out_specs=[vmem] * len(out_shape),
        scratch_shapes=[pltpu.VMEM(state, jnp.bfloat16)] + [pltpu.VMEM(state, jnp.float32)] * 3,
        out_shape=out_shape,
        compiler_params=pltpu.CompilerParams(vmem_limit_bytes=VMEM_BYTES),
        cost_estimate=pl.CostEstimate(
            flops=4 * served * count * CORES * wide * mine.shape[0],
            bytes_accessed=4 * mine.size,
            transcendentals=0,
        ),
    )(place, order, bounds, queries, mine, other, first_key.reshape(-1, 1), *states)


def local(hidden, gain, basis, w_query, key_matrix, value_matrix, doc_ids):
    ctx_count, tp_count = lax.axis_size("ctx"), lax.axis_size("tp")
    ctx_rank, tp_rank = lax.axis_index("ctx"), lax.axis_index("tp")
    chips = tp_count // CORES
    chip, core = tp_rank // CORES, tp_rank % CORES
    place = jnp.stack([chip, core]).astype(jnp.int32)
    count = hidden.shape[0]
    block_len = count * tp_count

    def along(value, step):
        moves = [(t, ((t // CORES + step) % chips) * CORES + t % CORES) for t in range(tp_count)]
        return lax.ppermute(value, "tp", moves)

    def swapped(value):
        return lax.ppermute(value, "tp", [(t, t ^ 1) for t in range(tp_count)])

    def after(value, *others):
        return lax.optimization_barrier((value, *others))[0]

    def summed(counts, axis, steps):
        for step in steps:
            moves = [(i, i ^ step) for i in range(lax.axis_size(axis))]
            counts += lax.ppermute(counts, axis, moves)
        return counts

    basis_other = swapped(basis)
    kv_weights = jnp.concatenate(
        [
            lax.dynamic_slice_in_dim(matrix, chip * HEAD_WIDTH, HEAD_WIDTH, 1)
            for matrix in (key_matrix, value_matrix)
        ],
        axis=1,
    )

    first_token = ctx_rank * block_len
    row_pos = (
        first_token
        + CORES * count * jnp.arange(chips, dtype=jnp.int32)[:, None]
        + count * core
        + jnp.arange(count, dtype=jnp.int32)[None, :]
    )
    cosine, sine = rotary_tables(row_pos.reshape(-1).astype(jnp.float32))
    cosine = cosine.reshape(chips, count, HEAD_WIDTH)
    sine = sine.reshape(chips, count, HEAD_WIDTH)
    blocks_before = min(-(-(LONGEST_DOC - 1) // block_len), ctx_count - 1)

    def normed_rows(start, size):
        values = hidden[start : start + size].astype(jnp.float32)
        meansq = jnp.mean(values * values, axis=-1, keepdims=True)
        return (values * lax.rsqrt(meansq + 1e-05) * gain.astype(jnp.float32)).astype(jnp.bfloat16)

    begins = [sum(CHUNKS[:k]) for k in range(len(CHUNKS))]
    normed = [normed_rows(begin, size) for begin, size in zip(begins, CHUNKS)]

    def gather(first, second):
        first_right, second_left = along(first, 1), along(second, -1)
        second_right, first_left = along(second, 1), along(first, -1)
        first_far, second_far = along(first_right, 1), along(second_left, -1)
        return [
            (first, first_right, first_left, first_far),
            (second, second_right, second_left, second_far),
        ]

    gathered = gather(*normed)

    ids, cosine, sine, kv_weights = lax.optimization_barrier(
        (doc_ids, cosine, sine, kv_weights, gathered[0][1], gathered[1][2], basis_other)
    )[:4]
    smaller = (ids[None, :] < jnp.arange(DOCS, dtype=jnp.int32)[:, None]).astype(jnp.int32)
    doc_starts = jnp.sum(smaller, axis=1)
    doc_starts = summed(doc_starts, "ctx", [1 << i for i in range((ctx_count - 1).bit_length())])
    doc_starts = summed(doc_starts, "tp", [1])
    doc_starts = after(doc_starts, gathered[0][2], gathered[1][1])
    doc_starts = sum([along(doc_starts, step) for step in range(1, chips)], doc_starts)
    first = (after(gathered[0][0], doc_starts),) + gathered[0][1:]
    columns = project(place, first + gathered[1], basis, basis_other, chips)
    first, second = gather(*[c.reshape(-1, c.shape[2]) for c in columns])
    pieces = first + second

    query_other = swapped(after(w_query, columns[0]))
    own, queries = project_heads(place, pieces, cosine, sine, [kv_weights, w_query, query_other])
    own = own.reshape(chips * count, -1)
    own_other = swapped(own)
    blocks = [
        lax.ppermute(own, "ctx", [(i, i + s) for i in range(ctx_count - s)])
        for s in range(blocks_before, 0, -1)
    ]
    doc_first = jnp.max(
        jnp.where(doc_starts[:, None, None] <= row_pos[None], doc_starts[:, None, None], 0), axis=0
    )
    first_key = doc_first - first_token + blocks_before * block_len

    everyone = jnp.arange(chips, dtype=jnp.int32)
    states = attend(place, everyone, queries, own, own_other, first_key, blocks_before, [])
    mine = pack([after(received, *states) for received in blocks])
    other = swapped(mine)

    def finished(aways):
        order = (chip + jnp.array(aways, jnp.int32)) % chips
        return attend(place, order, queries, mine, other, first_key, blocks_before, states)[0]

    others, last = finished((2, 1, 3)), finished((0,))
    received = jnp.stack(
        [last[0], along(others[1], 1), along(others[0], 2), along(others[2], 3)]
    )
    return jnp.concatenate(
        [
            lax.dynamic_index_in_dim(received, (chip - g) % chips, 0, keepdims=False)
            for g in range(chips)
        ],
        axis=1,
    )


def solution(mesh):
    in_specs = (
        P(("dp", "ctx", "tp"), None),
        P(),
        P(None, "tp"),
        P(None, "tp"),
        P(),
        P(),
        P(("dp", "ctx", "tp")),
    )
    out_specs = P(("dp", "ctx", "tp"), None)
    return jax.shard_map(local, mesh=mesh, in_specs=in_specs, out_specs=out_specs, check_vma=False)
```
